32 devices in a mesh: rep: 8 (over z, y), grp: 4 (over x, core).
Axes of the slice: x: 2, y: 2, z: 4, core: 2. Of those that a mesh axis runs over, the one named last changes fastest.
Arguments:
- tokens: bfloat16 [16, 580, 1024], P('rep', 'grp'), may hold values from -6 to 6
- cotangent: bfloat16 [16, 580, 1024], P('rep', 'grp'), may hold values from -6 to 6
- image_valid: int32 [16], P('rep'), may hold values 0 or 1
- token_valid: int32 [16, 580], P('rep'), may hold values from 0 to 1, as said below
- norm1_gain: bfloat16 [2, 1024], P(None, 'grp'), may hold values from 0.5 to 1.5
- norm1_bias: bfloat16 [2, 1024], P(None, 'grp'), may hold values from -2 to 2
- w_qkv: bfloat16 [2, 1024, 3072], P(None, 'grp'), may hold values from -0.1875 to 0.1875
- b_qv: bfloat16 [2, 2048], P(None, 'grp'), may hold values from -2 to 2
- w_out: bfloat16 [2, 1024, 1024], P(None, 'grp'), may hold values from -0.5 to 0.5
- b_out: bfloat16 [2, 1024], P(None, 'grp'), may hold values from -2 to 2
- norm2_gain: bfloat16 [2, 1024], P(None, 'grp'), may hold values from 0.5 to 1.5
- norm2_bias: bfloat16 [2, 1024], P(None, 'grp'), may hold values from -2 to 2
- w_up: bfloat16 [2, 1024, 4096], P(None, 'grp'), may hold values from -0.1875 to 0.1875
- b_up: bfloat16 [2, 4096], P(None, 'grp'), may hold values from -2 to 2
- w_down: bfloat16 [2, 4096, 1024], P(None, 'grp'), may hold values from -0.09375 to 0.09375
- b_down: bfloat16 [2, 1024], P(None, 'grp'), may hold values from -2 to 2
Outputs:
- activations: bfloat16 [16, 580, 1024], P('rep', 'grp')
- grad_tokens: bfloat16 [16, 580, 1024], P('rep', 'grp')
- grad_norm1_gain: float32 [2, 1024], P(None, 'grp')
- grad_norm1_bias: float32 [2, 1024], P(None, 'grp')
- grad_w_qkv: float32 [2, 1024, 3072], P(None, 'grp')
- grad_b_qv: float32 [2, 2048], P(None, 'grp')
- grad_w_out: float32 [2, 1024, 1024], P(None, 'grp')
- grad_b_out: float32 [2, 1024], P(None, 'grp')
- grad_norm2_gain: float32 [2, 1024], P(None, 'grp')
- grad_norm2_bias: float32 [2, 1024], P(None, 'grp')
- grad_w_up: float32 [2, 1024, 4096], P(None, 'grp')
- grad_b_up: float32 [2, 4096], P(None, 'grp')
- grad_w_down: float32 [2, 4096, 1024], P(None, 'grp')
- grad_b_down: float32 [2, 1024], P(None, 'grp')
The draws below stay inside these ranges and needn't reach their ends.
Inputs may be any that keep to these rules, and one draw needn't show every extreme that they name: `token_valid`: each row is 1 on a prefix of 508 slots or more and 0 after it.
All inputs are finite; a program needn't handle non-finite values. No bound on the sum of `image_valid` on one device may be relied on, other than what follows from the above.
Results may differ from the reference program's by a relative error of at most 0.017.
Values may be sent and summed in bfloat16 or wider, within the bound.
A program may use at most 320 MiB of HBM per device.

```python
import jax
import jax.numpy as jnp
from jax import lax

D = 1024
HEAD = 64
FF = 4096
SEQ = 580
LAYERS = 2
IMAGES = 16


def draw_token_valid(key, part):
    key = jax.random.fold_in(key, 7)
    shortest = SEQ - SEQ // 8
    lengths = jax.random.randint(key, (IMAGES,), shortest, SEQ + 1)
    lengths = lengths.at[0].set(shortest)
    positions = jnp.arange(SEQ)
    return (positions[None, :] < lengths[:, None]).astype(jnp.int32)


def plant(values, stream_key, least, high):
    shape = values.shape
    place = [jax.random.randint(jax.random.fold_in(stream_key, axis), (), 0, shape[axis]) for axis in range(len(shape))]
    values = values.at[tuple(place)].set(least)
    longest = shape.index(max(shape))
    place[longest] = (place[longest] + 1) % shape[longest]
    return values.at[tuple(place)].set(high)


def shard_levels(key, extent, shards, low, high):
    loudness = 1.0
    for position, shards_of in shards:
        steps = jax.random.uniform(jax.random.fold_in(jax.random.fold_in(key, 6), position), (shards_of,), jnp.float32, low / len(shards), high / len(shards))
        loudness = loudness * jnp.repeat(jnp.exp(steps), extent[position] // shards_of).reshape((-1,) + (1,) * (len(extent) - 1 - position))
    return loudness


def gaussian(stream_key, shape, scale, limit, split=(), dtype=jnp.bfloat16):
    level = shard_levels(stream_key, shape, split, -0.22, 0.18) if split else 1.0
    entries = jax.random.normal(stream_key, shape, jnp.float32) * scale * level
    return jnp.minimum(jnp.maximum(entries, -limit), limit).astype(dtype)


def setup_inputs(seed: int = 0) -> dict:
    splits = jax.random.split(jax.random.key(seed), 17)
    return {
        "tokens": gaussian(splits[0], (IMAGES, SEQ, D), 1.0, 6.0, ((0, 8), (1, 4))),
        "cotangent": gaussian(splits[1], (IMAGES, SEQ, D), 1.0, 6.0, ((0, 8), (1, 4))),
        "image_valid": plant((jax.random.randint(splits[2], (IMAGES,), 0, 4) < 3).astype(jnp.int32), jax.random.fold_in(splits[2], 1), 0, 1),
        "token_valid": draw_token_valid(jax.random.fold_in(splits[16], 71), 0),
        "norm1_gain": jnp.clip(1.0 + 0.1 * jax.random.normal(splits[4], (LAYERS, D), jnp.float32), 0.5, 1.5).astype(jnp.bfloat16),
        "norm1_bias": gaussian(splits[5], (LAYERS, D), 0.3, 2.0, ((1, 4),)),
        "w_qkv": gaussian(splits[6], (LAYERS, D, 3 * D), D ** -0.5, 0.1875, ((1, 4),)),
        "b_qv": gaussian(splits[7], (LAYERS, 2 * D), 0.3, 2.0, ((1, 4),)),
        "w_out": gaussian(splits[8], (LAYERS, D, D), (D // 8) ** -0.5, 0.5, ((1, 4),)),
        "b_out": gaussian(splits[9], (LAYERS, D), 0.3, 2.0, ((1, 4),)),
        "norm2_gain": jnp.clip(1.0 + 0.1 * jax.random.normal(splits[10], (LAYERS, D), jnp.float32), 0.5, 1.5).astype(jnp.bfloat16),
        "norm2_bias": gaussian(splits[11], (LAYERS, D), 0.3, 2.0, ((1, 4),)),
        "w_up": gaussian(splits[12], (LAYERS, D, FF), D ** -0.5, 0.1875, ((1, 4),)),
        "b_up": gaussian(splits[13], (LAYERS, FF), 0.3, 2.0, ((1, 4),)),
        "w_down": gaussian(splits[14], (LAYERS, FF, D), FF ** -0.5, 0.09375, ((1, 4),)),
        "b_down": gaussian(splits[15], (LAYERS, D), 0.3, 2.0, ((1, 4),)),
    }


@jax.custom_vjp
def low(v):
    return lax.optimization_barrier(v.astype(jnp.bfloat16)).astype(jnp.float32)

@jax.custom_vjp
def low_back(v):
    return v

def low_keep(v):
    return (low(v), None)

def low_pass(kept, grad):
    return (grad,)

def back_keep(v):
    return (v, None)

def back_low(kept, grad):
    return (low(grad),)
low.defvjp(low_keep, low_pass)
low_back.defvjp(back_keep, back_low)

def normalize(values, gain_vec, shift_vec):
    centre = lax.optimization_barrier(jnp.mean(values, axis=-1, keepdims=True))
    spread = lax.optimization_barrier(jnp.mean(jnp.square(values - centre), axis=-1, keepdims=True))
    return (values - centre) * lax.rsqrt(spread + 1e-06) * gain_vec + shift_vec

def matmul(left, right):
    return jnp.dot(left, right, precision=lax.Precision.HIGHEST)

def vit_block(hidden, weights, key_mask):
    gain_one, shift_one, w_joined, b_joined, w_proj, b_proj, gain_two, shift_two, w_in, b_in, w_back, b_back = weights
    length = hidden.shape[0]
    model_width = hidden.shape[1]
    head_count = model_width // HEAD
    normed = low(normalize(hidden, gain_one, shift_one))
    joined = matmul(normed, w_joined)
    queries = low(low_back(joined[:, :model_width] + b_joined[:model_width]))
    key_rows = low(low_back(joined[:, model_width:2 * model_width]))
    values = low(low_back(joined[:, 2 * model_width:] + b_joined[model_width:]))
    query_heads = queries.reshape(length, head_count, HEAD)
    key_heads = key_rows.reshape(length, head_count, HEAD)
    value_heads = values.reshape(length, head_count, HEAD)
    scores = low_back(jnp.einsum('qhd,khd->hqk', query_heads, key_heads, precision=lax.Precision.HIGHEST) * HEAD ** (-0.5))
    scores = jnp.where(key_mask[None, None, :], scores, -1000000000.0)
    row_max = lax.optimization_barrier(jnp.max(scores, axis=-1, keepdims=True))
    exp_terms = jnp.exp(scores - row_max)
    softmax_out = exp_terms / lax.optimization_barrier(jnp.sum(exp_terms, axis=-1, keepdims=True))
    attended = jnp.einsum('hqk,khd->qhd', low(softmax_out), value_heads, precision=lax.Precision.HIGHEST)
    attended = low(low_back(attended.reshape(length, model_width)))
    middle = hidden + low_back(matmul(attended, w_proj) + b_proj)
    normed_two = low(normalize(middle, gain_two, shift_two))
    pre_active = low_back(matmul(normed_two, w_in) + b_in)
    active = low(jax.nn.gelu(pre_active, approximate=False))
    return middle + low_back(matmul(active, w_back) + b_back)

def reference(tokens, cotangent, image_valid, token_valid, norm1_gain, norm1_bias, w_qkv, b_qv, w_out, b_out, norm2_gain, norm2_bias, w_up, b_up, w_down, b_down):
    stacked = tuple((w.astype(jnp.float32) for w in (norm1_gain, norm1_bias, w_qkv, b_qv, w_out, b_out, norm2_gain, norm2_bias, w_up, b_up, w_down, b_down)))

    def forward(params, image_rows, key_mask):
        hidden = image_rows
        for layer_index in range(LAYERS):
            hidden = vit_block(hidden, tuple((w[layer_index] for w in params)), key_mask)
        return hidden

    def per_image(totals, inputs):
        image_rows, seed_grad, image_flag, token_flags = inputs
        key_mask = token_flags > 0
        result, pullback = jax.vjp(lambda params, rows_in: forward(params, rows_in, key_mask), stacked, image_rows.astype(jnp.float32))
        row_weight = (image_flag * token_flags).astype(jnp.float32)
        grads, grad_image = pullback(seed_grad.astype(jnp.float32) * row_weight[:, None])
        totals = jax.tree.map(jnp.add, totals, grads)
        return (totals, (result.astype(jnp.bfloat16), grad_image.astype(jnp.bfloat16)))
    zero_grads = tuple((jnp.zeros_like(w) for w in stacked))
    totals, (outputs, grad_in) = lax.scan(per_image, zero_grads, (tokens, cotangent, image_valid, token_valid))
    return (outputs, grad_in) + tuple(totals)
```

```python
import functools

import jax
import jax.numpy as jnp
from jax import lax
from jax.experimental import pallas as pl
from jax.experimental.pallas import tpu as pltpu
from jax.sharding import PartitionSpec as P

HEAD = 64
MESH = pl.DeviceIdType.MESH
F32 = jnp.float32
BF16 = jnp.bfloat16
VMEM_LIMIT = 62 * 2**20
G1, B1, BOUT, G2, B2, BDOWN = range(6)


def nn(a, b):
    return lax.dot_general(a, b, (((1,), (0,)), ((), ())), preferred_element_type=F32)


def nt(a, b):
    return lax.dot_general(a, b, (((1,), (1,)), ((), ())), preferred_element_type=F32)


def tn(a, b):
    return lax.dot_general(a, b, (((0,), (0,)), ((), ())), preferred_element_type=F32)


def cols(j, width):
    return pl.ds(pl.multiple_of(j * width, width), width)


def loop(count, body):
    def step(j, carry):
        body(j)
        return carry

    lax.fori_loop(0, count, step, 0)


def mates():
    rep, grp = lax.axis_index("rep"), lax.axis_index("grp")
    return (rep, grp + 1 - 2 * (grp % 2))


def greet():
    barrier = pltpu.get_barrier_semaphore()
    pl.semaphore_signal(barrier, inc=1, device_id=mates(), device_id_type=MESH)
    pl.semaphore_wait(barrier, 1)


def to_mate(src, dst, send, recv, slot):
    return pltpu.make_async_remote_copy(
        src_ref=src,
        dst_ref=dst,
        send_sem=send.at[slot],
        recv_sem=recv.at[slot],
        device_id=mates(),
        device_id_type=MESH,
    )


def norm_rows(v):
    mean = jnp.mean(v, axis=-1, keepdims=True)
    off = v - mean
    rstd = lax.rsqrt(jnp.mean(off * off, axis=-1, keepdims=True) + 1e-6)
    return off * rstd, rstd


def scores_t(k2, qa, mask):
    st = jnp.where(mask > 0, nt(k2, qa), -1e9)
    top = jnp.max(st, axis=0, keepdims=True)
    e = jnp.exp(st - top)
    return e * (1.0 / jnp.sum(e, axis=0, keepdims=True))


def half_lanes(v, a):
    lane = lax.broadcasted_iota(jnp.int32, v.shape, 1)
    return jnp.where((lane >= HEAD) == (a == 1), v, jnp.zeros_like(v))


def fwd_kernel(
    x_ref, vec_ref, bqkv_ref, bup_ref, mask_ref, wqkv_ref, wout_ref, wup_ref, wdown_ref,
    x2_ref, x3_ref, h1_ref, qkv_ref, a_ref, h2_ref, z_ref, gp_ref,
    put_ref, got_ref, send, recv,
):
    rows, d = x_ref.shape
    hc = a_ref.shape[1]
    f = z_ref.shape[1]
    own, sib = pl.ds(0, rows), pl.ds(rows, rows)
    step = 16
    greet()

    def norm_out(src_ref, dst_ref, gain, shift):
        for i in range(rows // step):
            r = pl.ds(i * step, step)
            hat, _ = norm_rows(src_ref[r, :])
            dst_ref[r, :] = (hat * vec_ref[gain:gain + 1, :] + vec_ref[shift:shift + 1, :]).astype(BF16)

    norm_out(x_ref, h1_ref, G1, B1)
    cp = to_mate(h1_ref.at[own], h1_ref.at[sib], send, recv, 0)
    cp.start()

    wide = 256

    def qkv_rows(r):
        def body(j):
            c = cols(j, wide)
            out = nn(h1_ref[r, :], wqkv_ref[:, c]) + bqkv_ref[0:1, c]
            qkv_ref[r, c] = (out * bqkv_ref[1:2, c]).astype(BF16)

        loop(3 * hc // wide, body)

    qkv_rows(own)
    cp.wait()
    qkv_rows(sib)

    mask = mask_ref[:, 0:1]

    def pair(p):
        q2 = qkv_ref[:, pl.ds(pl.multiple_of(p * 128, 128), 128)]
        k2 = qkv_ref[:, pl.ds(pl.multiple_of(hc + p * 128, 128), 128)]
        v2 = qkv_ref[:, pl.ds(pl.multiple_of(2 * hc + p * 128, 128), 128)]
        vt = v2.T
        parts = []
        for a in range(2):
            pt = scores_t(k2, half_lanes(q2, a), mask)
            parts.append(nn(vt[a * HEAD:(a + 1) * HEAD, :], pt.astype(BF16)))
        a_ref[:, pl.ds(pl.multiple_of(p * 128, 128), 128)] = jnp.concatenate(parts, axis=0).T.astype(BF16)

    loop(hc // 128, pair)

    def exchange(left_ref, w_ref, base_ref, bias, out_ref, slot):
        def theirs(j):
            c = cols(j, wide)
            put_ref[slot, :, c] = nn(left_ref[sib, :], w_ref[:, c]).astype(BF16)

        loop(d // wide, theirs)
        cp = to_mate(put_ref.at[slot], got_ref.at[slot], send, recv, 1 + slot)
        cp.start()

        def ours(j):
            c = cols(j, wide)
            out_ref[:, c] = nn(left_ref[own, :], w_ref[:, c]) + base_ref[:, c] + vec_ref[bias:bias + 1, c]

        loop(d // wide, ours)
        cp.wait()
        out_ref[...] += got_ref[slot].astype(F32)

    exchange(a_ref, wout_ref, x_ref, BOUT, x2_ref, 0)
    norm_out(x2_ref, h2_ref, G2, B2)
    cp = to_mate(h2_ref.at[own], h2_ref.at[sib], send, recv, 3)
    cp.start()

    def up_rows(r):
        def body(j):
            c = cols(j, wide)
            u = nn(h2_ref[r, :], wup_ref[:, c]) + bup_ref[0:1, c]
            phi = 0.5 + 0.5 * lax.erf(u * 0.7071067811865476)
            z_ref[r, c] = (u * phi).astype(BF16)
            gp_ref[r, c] = (phi + u * jnp.exp(u * u * -0.5) * 0.3989422804014327).astype(BF16)

        loop(f // wide, body)

    up_rows(own)
    cp.wait()
    up_rows(sib)
    exchange(z_ref, wdown_ref, x2_ref, BDOWN, x3_ref, 1)


def bwd_kernel(
    g3_ref, x_ref, x2_ref, h1_ref, qkv_ref, a_ref, h2_ref, z_ref, gp_ref,
    vec_ref, mask_ref, wqkv_ref, wout_ref, wup_ref, wdown_ref,
    g0_ref, gwqkv_ref, gwout_ref, gwup_ref, gwdown_ref, gvec_ref, gbqkv_ref, gbup_ref,
    dm_ref, du_ref, da_ref, dj_ref, dx2_ref, dh_ref, put_ref, got_ref, send, recv,
):
    rows, d = g3_ref.shape
    hc = a_ref.shape[1]
    f = z_ref.shape[1]
    own, sib = pl.ds(0, rows), pl.ds(rows, rows)
    step = 16
    wide = 256
    greet()

    def send_round(src_ref, sum_row, slot):
        total = jnp.zeros((8, d), F32)
        for i in range(rows // step):
            r = pl.ds(i * step, step)
            low = src_ref[r, :].astype(BF16)
            dm_ref[slot, r, :] = low
            low = low.astype(F32)
            total = total + low[0:8, :] + low[8:16, :]
        gvec_ref[sum_row:sum_row + 1, :] = jnp.sum(total, axis=0, keepdims=True)
        cp = to_mate(dm_ref.at[slot, own], dm_ref.at[slot, sib], send, recv, slot)
        cp.start()
        return cp

    def exchange(left_ref, w_ref, slot):
        def theirs(j):
            c = cols(j, wide)
            put_ref[slot, :, c] = nt(left_ref[sib, :], w_ref[c, :]).astype(BF16)

        loop(d // wide, theirs)
        cp = to_mate(put_ref.at[slot], got_ref.at[slot], send, recv, 2 + slot)
        cp.start()

        def ours(j):
            c = cols(j, wide)
            dh_ref[:, c] = nt(left_ref[own, :], w_ref[c, :])

        loop(d // wide, ours)
        return cp

    def norm_back(value_ref, base_ref, out_ref, gain, shift, slot):
        total_g = jnp.zeros((8, d), F32)
        total_b = jnp.zeros((8, d), F32)
        for i in range(rows // step):
            r = pl.ds(i * step, step)
            hat, rstd = norm_rows(value_ref[r, :])
            dh = dh_ref[r, :] + got_ref[slot, r, :].astype(F32)
            prod = dh * hat
            total_g = total_g + prod[0:8, :] + prod[8:16, :]
            total_b = total_b + dh[0:8, :] + dh[8:16, :]
            dhat = dh * vec_ref[gain:gain + 1, :]
            m1 = jnp.mean(dhat, axis=-1, keepdims=True)
            m2 = jnp.mean(dhat * hat, axis=-1, keepdims=True)
            out_ref[r, :] = base_ref[r, :] + rstd * (dhat - m1 - hat * m2)
        gvec_ref[gain:gain + 1, :] = jnp.sum(total_g, axis=0, keepdims=True)
        gvec_ref[shift:shift + 1, :] = jnp.sum(total_b, axis=0, keepdims=True)

    cp = send_round(g3_ref, BDOWN, 0)

    def dz_rows(r):
        def body(j):
            c = cols(j, wide)
            dz = nt(dm_ref[0, r, :], wdown_ref[c, :])
            du_ref[r, c] = (dz * gp_ref[r, c].astype(F32)).astype(BF16)

        loop(f // wide, body)

    dz_rows(own)
    cp.wait()
    dz_rows(sib)

    def grads_ff(j):
        c = cols(j, wide)
        gwdown_ref[c, :] = tn(z_ref[:, c], dm_ref[0]).astype(BF16)
        du = du_ref[:, c]
        gwup_ref[:, c] = tn(h2_ref[...], du).astype(BF16)
        gbup_ref[0:1, c] = jnp.sum(du.astype(F32), axis=0, keepdims=True)

    cp = exchange(du_ref, wup_ref, 0)
    loop(f // wide, grads_ff)
    cp.wait()
    norm_back(x2_ref, g3_ref, dx2_ref, G2, B2, 0)
    cp = send_round(dx2_ref, BOUT, 1)

    def da_rows(r):
        def body(j):
            c = cols(j, wide)
            da_ref[r, c] = nt(dm_ref[1, r, :], wout_ref[c, :]).astype(BF16)

        loop(hc // wide, body)

    da_rows(own)
    cp.wait()
    da_rows(sib)

    def grads_out(j):
        c = cols(j, wide)
        gwout_ref[c, :] = tn(a_ref[:, c], dm_ref[1]).astype(BF16)

    loop(hc // wide, grads_out)
    mask = mask_ref[:, 0:1]

    def pair(p):
        cq = pl.ds(pl.multiple_of(p * 128, 128), 128)
        ck = pl.ds(pl.multiple_of(hc + p * 128, 128), 128)
        cv = pl.ds(pl.multiple_of(2 * hc + p * 128, 128), 128)
        q2, k2, v2, da2 = qkv_ref[:, cq], qkv_ref[:, ck], qkv_ref[:, cv], da_ref[:, cq]
        kt = k2.T
        dk = dv = None
        parts = []
        for a in range(2):
            qa, daa = half_lanes(q2, a), half_lanes(da2, a)
            pt = scores_t(k2, qa, mask)
            dpt = nt(v2, daa)
            delta = jnp.sum(dpt * pt, axis=0, keepdims=True)
            dst = (pt * (dpt - delta)).astype(BF16)
            dva = nn(pt.astype(BF16), daa)
            dka = nn(dst, qa)
            parts.append(nn(kt[a * HEAD:(a + 1) * HEAD, :], dst))
            dk = dka if dk is None else dk + dka
            dv = dva if dv is None else dv + dva
        dq = (jnp.concatenate(parts, axis=0).T * HEAD ** -0.5).astype(BF16)
        dv = dv.astype(BF16)
        dj_ref[:, cq] = dq
        dj_ref[:, ck] = dk.astype(BF16)
        dj_ref[:, cv] = dv
        gbqkv_ref[0:1, cq] = jnp.sum(dq.astype(F32), axis=0, keepdims=True)
        gbqkv_ref[0:1, cv] = jnp.sum(dv.astype(F32), axis=0, keepdims=True)

    loop(hc // 128, pair)
    cp = exchange(dj_ref, wqkv_ref, 1)

    def grads_qkv(j):
        c = cols(j, wide)
        gwqkv_ref[:, c] = tn(h1_ref[...], dj_ref[:, c]).astype(BF16)

    loop(3 * hc // wide, grads_qkv)
    cp.wait()
    norm_back(x_ref, dx2_ref, g0_ref, G1, B1, 1)


VM = pl.BlockSpec(memory_space=pltpu.VMEM)


def run_fwd(x, vec, bqkv, bup, mask, wqkv, wout, wup, wdown):
    rows, d = x.shape
    hc, f = wout.shape[0], wdown.shape[0]
    both = 2 * rows
    shapes = [
        ((rows, d), F32), ((rows, d), F32), ((both, d), BF16), ((both, 3 * hc), BF16),
        ((both, hc), BF16), ((both, d), BF16), ((both, f), BF16), ((both, f), BF16),
    ]
    args = (x, vec, bqkv, bup, mask, wqkv, wout, wup, wdown)
    return pl.pallas_call(
        fwd_kernel,
        out_shape=[jax.ShapeDtypeStruct(s, t) for s, t in shapes],
        in_specs=[VM] * len(args),
        out_specs=[VM] * len(shapes),
        scratch_shapes=[
            pltpu.VMEM((2, rows, d), BF16), pltpu.VMEM((2, rows, d), BF16),
            pltpu.SemaphoreType.DMA((4,)), pltpu.SemaphoreType.DMA((4,)),
        ],
        compiler_params=pltpu.CompilerParams(
            collective_id=1, has_side_effects=True, vmem_limit_bytes=VMEM_LIMIT
        ),
        cost_estimate=pl.CostEstimate(flops=8 * 10**9, bytes_accessed=20 * 10**6, transcendentals=0),
        name="layer_fwd",
    )(*args)


def run_bwd(g3, saved, vec, mask, wqkv, wout, wup, wdown):
    rows, d = g3.shape
    hc, f = wout.shape[0], wdown.shape[0]
    both = 2 * rows
    shapes = [
        ((rows, d), F32), (wqkv.shape, BF16), (wout.shape, BF16), (wup.shape, BF16), (wdown.shape, BF16),
        ((8, d), F32), ((8, 3 * hc), F32), ((8, f), F32),
    ]
    args = (g3, *saved, vec, mask, wqkv, wout, wup, wdown)
    return pl.pallas_call(
        bwd_kernel,
        out_shape=[jax.ShapeDtypeStruct(s, t) for s, t in shapes],
        in_specs=[VM] * len(args),
        out_specs=[VM] * len(shapes),
        scratch_shapes=[
            pltpu.VMEM((2, both, d), BF16), pltpu.VMEM((both, f), BF16), pltpu.VMEM((both, hc), BF16),
            pltpu.VMEM((both, 3 * hc), BF16), pltpu.VMEM((rows, d), F32), pltpu.VMEM((rows, d), F32),
            pltpu.VMEM((2, rows, d), BF16), pltpu.VMEM((2, rows, d), BF16),
            pltpu.SemaphoreType.DMA((4,)), pltpu.SemaphoreType.DMA((4,)),
        ],
        compiler_params=pltpu.CompilerParams(
            collective_id=2, has_side_effects=True, vmem_limit_bytes=VMEM_LIMIT
        ),
        cost_estimate=pl.CostEstimate(flops=17 * 10**9, bytes_accessed=40 * 10**6, transcendentals=0),
        name="layer_bwd",
    )(*args)


def swap(value, bit):
    return lax.ppermute(value, "grp", [(i, i ^ bit) for i in range(4)])


def pick(value, index, axis):
    return lax.dynamic_index_in_dim(value, index, axis, keepdims=False)


def local(
    tokens, cotangent, image_valid, token_valid,
    norm1_gain, norm1_bias, w_qkv, b_qv, w_out, b_out, norm2_gain, norm2_bias, w_up, b_up, w_down, b_down,
):
    grp = lax.axis_index("grp")
    x, c = grp // 2, grp % 2
    layers, dq, d3 = w_qkv.shape
    d = d3 // 3
    hc = d // 2
    f = 2 * w_down.shape[1] * 1
    seq = tokens.shape[1]
    real = 2 * seq
    rows = -(-real // 16) * 16

    def mine(value):
        got = swap(pick(value, 1 - x, 0), 2)
        return jnp.concatenate([pick(value, x, 0), got], axis=0)

    def pad(value):
        return jnp.pad(value, [(0, rows - real)] + [(0, 0)] * (value.ndim - 1))

    flags = pick(token_valid, x, 0).reshape(2, 2, seq)
    own_flags = pad(jnp.concatenate([pick(pick(flags, x, 0), c, 0), pick(pick(flags, 1 - x, 0), c, 0)]))
    sib_flags = pad(jnp.concatenate([pick(pick(flags, x, 0), 1 - c, 0), pick(pick(flags, 1 - x, 0), 1 - c, 0)]))
    mask = jnp.broadcast_to(jnp.concatenate([own_flags, sib_flags])[:, None], (2 * rows, 128))
    weight = (own_flags * pick(image_valid, x, 0)).astype(F32)
    hidden = pad(mine(tokens)).astype(F32)
    flow = pad(mine(cotangent)).astype(F32) * weight[:, None]

    smalls = [norm1_gain, norm1_bias, b_out, norm2_gain, norm2_bias, b_down, b_qv, b_up]
    widths = [s.shape[1] for s in smalls]
    packed = lax.all_gather(jnp.concatenate(smalls, axis=1), "grp", axis=0)
    parts, at = [], 0
    for width in widths:
        parts.append(packed[:, :, at:at + width].transpose(1, 0, 2).reshape(layers, 4 * width).astype(F32))
        at += width
    vecs = jnp.stack(parts[:6] + [jnp.zeros_like(parts[0])] * 2, axis=1)

    def halves(value, axis):
        return pick(value, c, axis)

    bq = halves(parts[6][:, :d].reshape(layers, 2, 2, d // 4), 2).reshape(layers, hc)
    bv = halves(parts[6][:, d:].reshape(layers, 2, 2, d // 4), 2).reshape(layers, hc)
    bqkv = jnp.concatenate([bq, jnp.zeros_like(bq), bv], axis=1)
    scale = jnp.concatenate([jnp.full_like(bq, HEAD ** -0.5), jnp.ones((layers, 2 * hc), F32)], axis=1)
    bqkv = jnp.pad(jnp.stack([bqkv, scale], axis=1), ((0, 0), (0, 6), (0, 0)))
    bup = halves(parts[7].reshape(layers, 2, 2, -1), 2).reshape(layers, 1, -1)
    bup = jnp.pad(bup, ((0, 0), (0, 7), (0, 0)))

    def by_core(value, other):
        return jnp.where(c == 0, jnp.concatenate([value, other], axis=1), jnp.concatenate([other, value], axis=1))

    def by_chip(value):
        other = swap(value, 2)
        return jnp.where(x == 0, jnp.concatenate([value, other], axis=1), jnp.concatenate([other, value], axis=1))

    def columns(w, groups):
        w = w.reshape(layers, w.shape[1], groups, 2, 2, -1)
        keep = pick(w, c, 4).reshape(layers, w.shape[1], -1)
        give = pick(w, 1 - c, 4).reshape(layers, w.shape[1], -1)
        return by_chip(by_core(keep, swap(give, 1)))

    wqkv = columns(w_qkv, 3)
    wup = columns(w_up, 1)
    wout = by_chip(w_out)
    wdown = by_chip(w_down)

    saved = []
    for l in range(layers):
        x2, x3, *rest = run_fwd(hidden, vecs[l], bqkv[l], bup[l], mask, wqkv[l], wout[l], wup[l], wdown[l])
        saved.append((hidden, x2, *rest))
        hidden = x3

    def give_back(value):
        value = value[:real].astype(BF16).reshape(2, seq, d)
        got = swap(value[1], 2)
        return jnp.where(x == 0, jnp.stack([value[0], got]), jnp.stack([got, value[0]]))

    activations = give_back(hidden)
    grads = [None] * layers
    for l in reversed(range(layers)):
        flow, *grads[l] = run_bwd(flow, saved[l], vecs[l], mask, wqkv[l], wout[l], wup[l], wdown[l])
    grad_tokens = give_back(flow)

    def reduce_big(index):
        g = jnp.stack([grads[l][index] for l in range(layers)])
        n = g.shape[1] // 2
        keep = lax.dynamic_slice_in_dim(g, x * n, n, 1)
        give = lax.dynamic_slice_in_dim(g, (1 - x) * n, n, 1)
        total = (keep.astype(F32) + swap(give, 2).astype(F32)).astype(BF16)
        return lax.psum(total, "rep")

    def uncolumns(g, groups):
        n = g.shape[1] // 2
        keep = lax.dynamic_slice_in_dim(g, c * n, n, 1)
        give = lax.dynamic_slice_in_dim(g, (1 - c) * n, n, 1)
        got = swap(give, 1)
        keep = keep.reshape(layers, n, groups, 2, -1)
        got = got.reshape(layers, n, groups, 2, -1)
        return jnp.where(c == 0, jnp.stack([keep, got], axis=4), jnp.stack([got, keep], axis=4)).reshape(layers, n, -1).astype(F32)

    gqkv = uncolumns(reduce_big(0), 3)
    gout = reduce_big(1).astype(F32)
    gup = uncolumns(reduce_big(2), 1)
    gdown = reduce_big(3).astype(F32)

    gvec = jnp.stack([grads[l][4][:6].reshape(6 * d) for l in range(layers)])
    gb = jnp.stack([grads[l][5][0] for l in range(layers)]).reshape(layers, 3, 2, -1)[:, ::2]
    gu = jnp.stack([grads[l][6][0] for l in range(layers)]).reshape(layers, 2, -1)

    def spread(v):
        z = jnp.zeros_like(v)
        return jnp.where(c == 0, jnp.stack([v, z], axis=-2), jnp.stack([z, v], axis=-2)).reshape(layers, -1)

    small = lax.psum(jnp.concatenate([gvec, spread(gb), spread(gu)], axis=1), ("rep", "grp"))
    outs, at = [], 0
    for width in widths:
        outs.append(lax.dynamic_slice_in_dim(small[:, at:at + 4 * width], grp * width, width, 1))
        at += 4 * width
    gg1, gb1, gbout, gg2, gb2, gbdown, gbqv, gbup = outs
    return (activations, grad_tokens, gg1, gb1, gqkv, gbqv, gout, gbout, gg2, gb2, gup, gbup, gdown, gbdown)


def solution(mesh):
    rows3, mat, vec = P("rep", "grp", None), P(None, "grp", None), P(None, "grp")
    weights = (vec, vec, mat, vec, mat, vec, vec, vec, mat, vec, mat, vec)
    return jax.shard_map(
        local,
        mesh=mesh,
        in_specs=(rows3, rows3, P("rep"), P("rep", None)) + weights,
        out_specs=(rows3, rows3) + weights,
        check_vma=False,
    )
```

```python
import functools

import jax
import jax.numpy as jnp
from jax import lax
from jax.experimental import pallas as pl
from jax.experimental.pallas import tpu as pltpu
from jax.sharding import PartitionSpec as P

HEAD = 64
MESH = pl.DeviceIdType.MESH
F32 = jnp.float32
BF16 = jnp.bfloat16
VMEM_LIMIT = 62 * 2**20
WIDE = 256
STEP = 16
G1, B1, BOUT, G2, B2, BDOWN, BQV, BUP = 0, 1, 2, 3, 4, 5, 6, 8
SMALL = 16


def nn(a, b):
    return lax.dot_general(a, b, (((1,), (0,)), ((), ())), preferred_element_type=F32)


def nt(a, b):
    return lax.dot_general(a, b, (((1,), (1,)), ((), ())), preferred_element_type=F32)


def tn(a, b):
    return lax.dot_general(a, b, (((0,), (0,)), ((), ())), preferred_element_type=F32)


def span(start, size):
    return pl.ds(pl.multiple_of(start, size), size)


def cols(j, width=WIDE):
    return span(j * width, width)


def loop(count, body):
    def step(j, carry):
        body(j)
        return carry

    lax.fori_loop(0, count, step, 0)


class Place:
    def __init__(self):
        self.rep, self.grp = lax.axis_index("rep"), lax.axis_index("grp")
        rep, grp = self.rep, self.grp
        self.x, self.c = grp // 2, grp % 2
        self.y, self.z = rep % 2, (rep // 2) % 4
        self.zlow = self.z % 2
        core, chip = 1 - 2 * self.c, 2 - 4 * self.x
        self.sib = (rep, grp + core)
        self.xn = (rep, grp + chip)
        self.xd = (rep, grp + chip + core)
        yrep = rep + 1 - 2 * self.y
        self.yn = (yrep, grp)
        self.yd = (yrep, grp + core)
        self.zn = (rep + 2 - 4 * self.zlow, grp)
        self.inner = jnp.logical_or(self.z == 1, self.z == 2)
        self.outer = jnp.logical_not(self.inner)
        self.mid = (rep + 6 - 4 * self.z, grp)


def greet(peers):
    barrier = pltpu.get_barrier_semaphore()
    for peer in peers:
        pl.semaphore_signal(barrier, inc=1, device_id=peer, device_id_type=MESH)
    pl.semaphore_wait(barrier, len(peers))


def remote(src, dst, send, recv, peer):
    return pltpu.make_async_remote_copy(
        src_ref=src, dst_ref=dst, send_sem=send, recv_sem=recv, device_id=peer, device_id_type=MESH
    )


def settle(ref, sem):
    pltpu.make_async_copy(ref, ref, sem).wait()


def norm_rows(v):
    mean = jnp.mean(v, axis=-1, keepdims=True)
    off = v - mean
    rstd = lax.rsqrt(jnp.mean(off * off, axis=-1, keepdims=True) + 1e-6)
    return off * rstd, rstd


def scores_t(k2, qa, mask):
    st = jnp.where(mask, nt(k2, qa), -1e9)
    top = jnp.max(st, axis=0, keepdims=True)
    e = jnp.exp(st - top)
    return e * (1.0 / jnp.sum(e, axis=0, keepdims=True))


def half_lanes(v, a):
    lane = lax.broadcasted_iota(jnp.int32, v.shape, 1)
    return jnp.where((lane >= HEAD) == (a == 1), v, jnp.zeros_like(v))


def chip_flags(at, tv_ref, rows, seq):
    lengths = jnp.sum(tv_ref[...], axis=1, keepdims=True)
    length = jnp.where(at.x == 0, lengths[0:1, :], lengths[1:2, :])
    row = lax.broadcasted_iota(jnp.int32, (2 * rows, 1), 0)
    core = jnp.where(row < rows, at.c, 1 - at.c)
    row = jnp.where(row < rows, row, row - rows)
    block = rows // 2
    chip = jnp.where(row < block, at.x, 1 - at.x)
    row = jnp.where(row < block, row, row - block)
    slot = (2 * chip + core) * seq + row
    return jnp.logical_and(row < seq, slot < length)


class Plan:
    def __init__(self):
        self.now, self.events, self.done = 0.0, [], set()

    def add(self, when, name, action):
        self.events.append((when, name, action))

    def order(self):
        self.events.sort(key=lambda e: e[0])

    def poll(self):
        while self.events and self.events[0][0] <= self.now:
            self.fire()

    def fire(self):
        when, name, action = self.events.pop(0)
        self.now = max(self.now, when)
        action()
        self.done.add(name)

    def need(self, name):
        while name not in self.done:
            self.fire()

    def spend(self, us):
        self.now += us
        self.poll()


KINDS = ("qkv", "out", "up", "down")


def fwd_kernel(
    seq, tok_ref, cot_ref, pack_ref, tv_ref, wqkv_in, wout_in, wup_in, wdown_in,
    vqkv, vout, vup, vdown, xs, x2s, h1s, qkvs, as_, h2s, zs, gps, cot_out, act_out, vec_out,
    wqkv, wout, wup, wdown, x_ref, x2_ref, h1, qkv, att, h2, z, gp, put, got, tok, vec, bup,
    s_rx, s_ry, s_rz, s_ra, s_rb, s_rs, s_loc, s_send, s_core, r_core, s_save, s_misc, r_misc,
):
    at = Place()
    layers = vqkv.shape[0]
    rows, d = x_ref.shape
    block = rows // 2
    hc, f = att.shape[1], z.shape[1]
    own, other = pl.ds(0, rows), pl.ds(rows, rows)
    x, c = at.x, at.c
    quarter = at.y * 2 + at.zlow
    ins = dict(qkv=wqkv_in, out=wout_in, up=wup_in, down=wdown_in)
    full = dict(qkv=wqkv, out=wout, up=wup, down=wdown)
    saves = dict(qkv=vqkv, out=vout, up=vup, down=vdown)
    runs = dict(qkv=(d // 4, 6), up=(f // 2, 2))
    plan = Plan()
    index = {}
    for l in range(layers):
        for kind in KINDS:
            index[l, kind] = len(index)

    greet((at.sib, at.xn, at.xd, at.yn, at.zn))

    first = [
        remote(tok_ref.at[1 - x], tok.at[1], s_misc.at[0], r_misc.at[0], at.xn),
        pltpu.make_async_copy(tok_ref.at[x], tok.at[0], s_misc.at[3]),
    ]
    here = vec.at[:, span(at.grp * WIDE, WIDE)]
    first += [
        pltpu.make_async_copy(pack_ref, here, s_misc.at[4]),
        remote(pack_ref, here, s_misc.at[5], r_misc.at[5], at.sib),
        remote(pack_ref, here, s_misc.at[6], r_misc.at[6], at.xn),
        remote(pack_ref, here, s_misc.at[7], r_misc.at[7], at.xd),
    ]
    for copy in first:
        copy.start()

    def launch(l, kind):
        i = index[l, kind]
        src, dst = ins[kind].at[l], full[kind].at[l]
        n = src.shape[0]
        q = n // 4
        part = span(quarter * q, q)
        if kind in runs:
            width, count = runs[kind]
            mine = 2 * x + c
            for j in range(count):
                to = pl.ds(j * width, width)
                keep = span((2 * j + c) * width, width)
                give = span((2 * j + 1 - c) * width, width)
                remote(src.at[part, keep], dst.at[mine, part, to], s_send.at[i], s_rx.at[i], at.xn).start()
                remote(src.at[part, give], dst.at[mine, part, to], s_send.at[i], s_rx.at[i], at.xd).start()
            for j in range(count):
                to = pl.ds(j * width, width)
                keep = span((2 * j + c) * width, width)
                give = span((2 * j + 1 - c) * width, width)
                remote(src.at[:, give], dst.at[mine, :, to], s_send.at[i], s_rs.at[i], at.sib).start()
                pltpu.make_async_copy(src.at[:, keep], dst.at[mine, :, to], s_loc.at[i]).start()
        else:
            remote(src.at[part], dst.at[x, part], s_send.at[i], s_rx.at[i], at.xn).start()
            pltpu.make_async_copy(src, dst.at[x], s_loc.at[i]).start()

    def theirs(l, kind, part):
        dst = full[kind].at[l]
        if kind in runs:
            return dst.at[span(2 * (1 - x), 2), part]
        return dst.at[pl.ds(1 - x, 1), part]

    def part_of(kind, y, zlow, half=None):
        q = full[kind].shape[2] // 4
        if half is None:
            return span((2 * y + zlow) * q, q)
        return span((4 * y + 2 * zlow + half) * (q // 2), q // 2)

    def relay1(l, kind):
        i = index[l, kind]
        piece = theirs(l, kind, part_of(kind, at.y, at.zlow))
        settle(piece, s_rx.at[i])
        remote(piece, piece, s_send.at[i], s_ry.at[i], at.yn).start()
        remote(piece, piece, s_send.at[i], s_rz.at[i], at.zn).start()

    def relay2(l, kind):
        i = index[l, kind]
        settle(theirs(l, kind, part_of(kind, 1 - at.y, at.zlow)), s_ry.at[i])
        piece = theirs(l, kind, part_of(kind, 1 - at.y, at.zlow, 0))
        remote(piece, piece, s_send.at[i], s_ra.at[i], at.zn).start()
        settle(theirs(l, kind, part_of(kind, at.y, 1 - at.zlow)), s_rz.at[i])
        piece = theirs(l, kind, part_of(kind, at.y, 1 - at.zlow, 1))
        remote(piece, piece, s_send.at[i], s_rb.at[i], at.yn).start()

    def ready(l, kind):
        i = index[l, kind]
        settle(theirs(l, kind, part_of(kind, 1 - at.y, 1 - at.zlow, 0)), s_ra.at[i])
        settle(theirs(l, kind, part_of(kind, 1 - at.y, 1 - at.zlow, 1)), s_rb.at[i])
        if kind in runs:
            settle(full[kind].at[l, 0], s_rs.at[i])
        settle(full[kind].at[l, 0], s_loc.at[i])
        pltpu.make_async_copy(full[kind].at[l], saves[kind].at[l], s_loc.at[i]).start()

    x_time, yz_time = 9.0, 16.0
    for l in range(layers):
        for kind in KINDS:
            launch(l, kind)
            mb = full[kind].shape[1] * full[kind].shape[2] * full[kind].shape[3] / 2**20
            mb *= 2
            x_time += mb / 4 / 0.094 * 1.05
            plan.add(x_time + 1.5, ("r1", l, kind), functools.partial(relay1, l, kind))
            yz_time = max(yz_time, x_time + 1.5)
            plan.add(yz_time + mb / 4 / 0.094 + 1.5, ("r2", l, kind), functools.partial(relay2, l, kind))
            yz_time += mb * 3 / 8 / 0.094 * 1.05
            plan.add(yz_time + 4, ("ok", l, kind), functools.partial(ready, l, kind))
    plan.order()
    late = [
        remote(cot_ref.at[1 - x], cot_out.at[1], s_misc.at[1], r_misc.at[1], at.xn),
        pltpu.make_async_copy(cot_ref.at[x], cot_out.at[0], s_misc.at[8]),
    ]
    for copy in late:
        copy.start()

    first[1].wait()
    first[2].wait()
    for copy in (first[0], *first[3:]):
        copy.wait()
    for i in range(2):
        for j in range(block // STEP):
            x_ref[pl.ds(i * block + j * STEP, STEP), :] = tok[i, pl.ds(j * STEP, STEP), :].astype(F32)
    vec_save = pltpu.make_async_copy(vec, vec_out, s_misc.at[9])
    vec_save.start()
    for l in range(layers):
        for j in range(f // WIDE):
            half, sub = divmod(j, f // WIDE // 2)
            bup[l:l + 1, pl.ds(j * WIDE, WIDE)] = vec[
                l * SMALL + BUP + sub:l * SMALL + BUP + sub + 1, span((2 * half + c) * WIDE, WIDE)
            ]
    mask = chip_flags(at, tv_ref, rows, seq)
    plan.now = 12.0
    plan.poll()

    def save(src, dst, slot):
        copy = pltpu.make_async_copy(src, dst, s_save.at[slot])
        copy.start()
        return copy

    pending = {}
    for l in range(layers):
        def row(name, l=l):
            return vec[l * SMALL + name:l * SMALL + name + 1, :]

        def norm_out(src_ref, dst_ref, gain, shift, l=l):
            for i in range(rows // STEP):
                r = pl.ds(i * STEP, STEP)
                hat, _ = norm_rows(src_ref[r, :])
                dst_ref[r, :] = (hat * row(gain) + row(shift)).astype(BF16)

        def weight(kind, cs, l=l):
            w = full[kind][l, :, :, cs]
            return w.reshape(w.shape[0] * w.shape[1], w.shape[2])

        norm_out(x_ref, h1, G1, B1)
        cp = remote(h1.at[own], h1.at[other], s_core.at[0], r_core.at[0], at.sib)
        cp.start()
        x_saved = save(x_ref, xs.at[l], 0)
        plan.spend(2)
        plan.need(("ok", l, "qkv"))
        if l:
            pending["qkv"].wait()
        bq = jnp.where(c == 0, row(BQV), vec[l * SMALL + BQV + 1:l * SMALL + BQV + 2, :])
        scale = HEAD ** -0.5
        parts = (
            (0, bq[:, :hc] * scale, scale), (hc, jnp.zeros((1, hc), F32), 1.0), (2 * hc, bq[:, hc:], 1.0)
        )

        def qkv_rows(r, l=l, parts=parts):
            for base, bias, factor in parts:
                for j in range(hc // WIDE):
                    cs = pl.ds(base + j * WIDE, WIDE)
                    out = nn(h1[r, :], weight("qkv", cs))
                    qkv[r, cs] = (out * factor + bias[:, j * WIDE:(j + 1) * WIDE]).astype(BF16)

        qkv_rows(own)
        plan.spend(2)
        cp.wait()
        qkv_rows(other)
        h1_saved = save(h1, h1s.at[l], 1)
        pending["qkv"] = save(qkv, qkvs.at[l], 2)
        plan.spend(2)
        if l:
            pending["att"].wait()
        for p in range(hc // 128):
            q2 = qkv[:, p * 128:(p + 1) * 128]
            k2 = qkv[:, hc + p * 128:hc + (p + 1) * 128]
            v2 = qkv[:, 2 * hc + p * 128:2 * hc + (p + 1) * 128]
            vt = v2.T
            outs = []
            for a in range(2):
                pt = scores_t(k2, half_lanes(q2, a), mask)
                outs.append(nn(vt[a * HEAD:(a + 1) * HEAD, :], pt.astype(BF16)))
            att[:, p * 128:(p + 1) * 128] = jnp.concatenate(outs, axis=0).T.astype(BF16)
            plan.spend(3)
        pending["att"] = save(att, as_.at[l], 3)

        def exchange(left, kind, base, bias, out, slot):
            def far(j):
                put[:, cols(j)] = nn(left[other, :], weight(kind, cols(j))).astype(BF16)

            loop(d // WIDE, far)
            cp = remote(put, got.at[slot], s_core.at[1], r_core.at[1], at.sib)
            cp.start()

            def near(j):
                out[:, cols(j)] = nn(left[own, :], weight(kind, cols(j))) + base[:, cols(j)] + vec[
                    l * SMALL + bias:l * SMALL + bias + 1, cols(j)
                ]

            loop(d // WIDE, near)
            cp.wait()
            out[...] += got[slot].astype(F32)

        plan.need(("ok", l, "out"))
        if l:
            pending["x2"].wait()
        exchange(att, "out", x_ref, BOUT, x2_ref, 0)
        pending["x2"] = save(x2_ref, x2s.at[l], 4)
        plan.spend(3)
        norm_out(x2_ref, h2, G2, B2)
        cp = remote(h2.at[own], h2.at[other], s_core.at[2], r_core.at[2], at.sib)
        cp.start()
        plan.spend(2)
        plan.need(("ok", l, "up"))
        if l:
            pending["z"].wait()
            pending["gp"].wait()

        def up_rows(r):
            def body(j):
                u = nn(h2[r, :], weight("up", cols(j))) + bup[l:l + 1, cols(j)]
                phi = 0.5 + 0.5 * lax.erf(u * 0.7071067811865476)
                z[r, cols(j)] = (u * phi).astype(BF16)
                gp[r, cols(j)] = (phi + u * jnp.exp(u * u * -0.5) * 0.3989422804014327).astype(BF16)

            loop(f // WIDE, body)

        up_rows(own)
        plan.spend(4)
        cp.wait()
        up_rows(other)
        h2_saved = save(h2, h2s.at[l], 5)
        pending["z"] = save(z, zs.at[l], 6)
        pending["gp"] = save(gp, gps.at[l], 7)
        plan.spend(4)
        plan.need(("ok", l, "down"))
        for copy in (x_saved, h1_saved, h2_saved):
            copy.wait()
        exchange(z, "down", x2_ref, BDOWN, x_ref, 1)
        plan.spend(4)

    for i in range(2):
        for j in range(block // STEP):
            tok[i, pl.ds(j * STEP, STEP), :] = x_ref[pl.ds(i * block + j * STEP, STEP), :].astype(BF16)
    act = [
        remote(tok.at[1], act_out.at[x], s_misc.at[2], r_misc.at[2], at.xn),
        pltpu.make_async_copy(tok.at[0], act_out.at[x], s_misc.at[10]),
    ]
    for copy in act:
        copy.start()
    for copy in (*act, *late, vec_save):
        copy.wait()
    for name in ("qkv", "att", "x2", "z", "gp"):
        pending[name].wait()
    for (l, kind), i in index.items():
        settle(full[kind].at[l, pl.ds(0, 3 if kind in runs else 1)], s_send.at[i])
        settle(full[kind].at[l], s_loc.at[i])


ANY = pl.BlockSpec(memory_space=pl.ANY)
VM = pl.BlockSpec(memory_space=pltpu.VMEM)


def dma(*shape):
    return pltpu.SemaphoreType.DMA(shape)


def run_fwd(tok, cot, pack, tv, w_qkv, w_out, w_up, w_down, seq):
    layers, n, d3 = w_qkv.shape
    d = d3 // 3
    hc, f = d // 2, 2 * w_down.shape[1]
    block = tok.shape[1]
    rows, both = 2 * block, 4 * block
    weights = [(4, n, 3 * hc), (2, n, d), (4, n, f), (2, w_down.shape[1], d)]
    acts = [
        ((rows, d), F32), ((rows, d), F32), ((both, d), BF16), ((both, 3 * hc), BF16),
        ((both, hc), BF16), ((both, d), BF16), ((both, f), BF16), ((both, f), BF16),
    ]
    shapes = [((layers, *s), BF16) for s in weights] + [((layers, *s), t) for s, t in acts]
    shapes += [((2, block, d), BF16), ((2, block, d), BF16), ((layers * SMALL, d), F32)]
    count = layers * len(KINDS)
    return pl.pallas_call(
        functools.partial(fwd_kernel, seq),
        out_shape=[jax.ShapeDtypeStruct(s, t) for s, t in shapes],
        in_specs=[ANY, ANY, VM, VM, ANY, ANY, ANY, ANY],
        out_specs=[ANY] * len(shapes),
        scratch_shapes=[pltpu.VMEM((layers, *s), BF16) for s in weights]
        + [pltpu.VMEM(s, t) for s, t in acts]
        + [
            pltpu.VMEM((rows, d), BF16), pltpu.VMEM((2, rows, d), BF16),
            pltpu.VMEM((2, block, d), BF16), pltpu.VMEM((layers * SMALL, d), F32), pltpu.VMEM((8, f), F32),
        ]
        + [dma(count)] * 8
        + [dma(3), dma(3), dma(8), dma(11), dma(8)],
        compiler_params=pltpu.CompilerParams(
            collective_id=1, has_side_effects=True, vmem_limit_bytes=VMEM_LIMIT
        ),
        cost_estimate=pl.CostEstimate(flops=17 * 10**9, bytes_accessed=80 * 10**6, transcendentals=0),
        name="forward",
    )(tok, cot, pack, tv, w_qkv, w_out, w_up, w_down)


def mates():
    rep, grp = lax.axis_index("rep"), lax.axis_index("grp")
    return (rep, grp + 1 - 2 * (grp % 2))


def greet_mate():
    barrier = pltpu.get_barrier_semaphore()
    pl.semaphore_signal(barrier, inc=1, device_id=mates(), device_id_type=MESH)
    pl.semaphore_wait(barrier, 1)


def to_mate(src, dst, send, recv, slot):
    return pltpu.make_async_remote_copy(
        src_ref=src,
        dst_ref=dst,
        send_sem=send.at[slot],
        recv_sem=recv.at[slot],
        device_id=mates(),
        device_id_type=MESH,
    )


def bwd_kernel(
    g3_ref, x_ref, x2_ref, h1_ref, qkv_ref, a_ref, h2_ref, z_ref, gp_ref,
    vec_ref, mask_ref, wqkv_ref, wout_ref, wup_ref, wdown_ref,
    g0_ref, gwqkv_ref, gwout_ref, gwup_ref, gwdown_ref, gvec_ref, gbqkv_ref, gbup_ref,
    dm_ref, du_ref, da_ref, dj_ref, dx2_ref, dh_ref, put_ref, got_ref, send, recv,
):
    rows, d = g3_ref.shape
    hc = a_ref.shape[1]
    f = z_ref.shape[1]
    own, sib = pl.ds(0, rows), pl.ds(rows, rows)
    step = 16
    wide = 256
    greet_mate()

    def send_round(src_ref, sum_row, slot):
        total = jnp.zeros((8, d), F32)
        for i in range(rows // step):
            r = pl.ds(i * step, step)
            low = src_ref[r, :].astype(BF16)
            dm_ref[slot, r, :] = low
            low = low.astype(F32)
            total = total + low[0:8, :] + low[8:16, :]
        gvec_ref[sum_row:sum_row + 1, :] = jnp.sum(total, axis=0, keepdims=True)
        cp = to_mate(dm_ref.at[slot, own], dm_ref.at[slot, sib], send, recv, slot)
        cp.start()
        return cp

    def exchange(left_ref, w_ref, slot):
        def theirs(j):
            c = cols(j, wide)
            put_ref[slot, :, c] = nt(left_ref[sib, :], w_ref[c, :]).astype(BF16)

        loop(d // wide, theirs)
        cp = to_mate(put_ref.at[slot], got_ref.at[slot], send, recv, 2 + slot)
        cp.start()

        def ours(j):
            c = cols(j, wide)
            dh_ref[:, c] = nt(left_ref[own, :], w_ref[c, :])

        loop(d // wide, ours)
        return cp

    def norm_back(value_ref, base_ref, out_ref, gain, shift, slot):
        total_g = jnp.zeros((8, d), F32)
        total_b = jnp.zeros((8, d), F32)
        for i in range(rows // step):
            r = pl.ds(i * step, step)
            hat, rstd = norm_rows(value_ref[r, :])
            dh = dh_ref[r, :] + got_ref[slot, r, :].astype(F32)
            prod = dh * hat
            total_g = total_g + prod[0:8, :] + prod[8:16, :]
            total_b = total_b + dh[0:8, :] + dh[8:16, :]
            dhat = dh * vec_ref[gain:gain + 1, :]
            m1 = jnp.mean(dhat, axis=-1, keepdims=True)
            m2 = jnp.mean(dhat * hat, axis=-1, keepdims=True)
            out_ref[r, :] = base_ref[r, :] + rstd * (dhat - m1 - hat * m2)
        gvec_ref[gain:gain + 1, :] = jnp.sum(total_g, axis=0, keepdims=True)
        gvec_ref[shift:shift + 1, :] = jnp.sum(total_b, axis=0, keepdims=True)

    cp = send_round(g3_ref, BDOWN, 0)

    def dz_rows(r):
        def body(j):
            c = cols(j, wide)
            dz = nt(dm_ref[0, r, :], wdown_ref[c, :])
            du_ref[r, c] = (dz * gp_ref[r, c].astype(F32)).astype(BF16)

        loop(f // wide, body)

    dz_rows(own)
    cp.wait()
    dz_rows(sib)

    def grads_ff(j):
        c = cols(j, wide)
        gwdown_ref[c, :] = tn(z_ref[:, c], dm_ref[0]).astype(BF16)
        du = du_ref[:, c]
        gwup_ref[:, c] = tn(h2_ref[...], du).astype(BF16)
        gbup_ref[0:1, c] = jnp.sum(du.astype(F32), axis=0, keepdims=True)

    cp = exchange(du_ref, wup_ref, 0)
    loop(f // wide, grads_ff)
    cp.wait()
    norm_back(x2_ref, g3_ref, dx2_ref, G2, B2, 0)
    cp = send_round(dx2_ref, BOUT, 1)

    def da_rows(r):
        def body(j):
            c = cols(j, wide)
            da_ref[r, c] = nt(dm_ref[1, r, :], wout_ref[c, :]).astype(BF16)

        loop(hc // wide, body)

    da_rows(own)
    cp.wait()
    da_rows(sib)

    def grads_out(j):
        c = cols(j, wide)
        gwout_ref[c, :] = tn(a_ref[:, c], dm_ref[1]).astype(BF16)

    loop(hc // wide, grads_out)
    mask = mask_ref[:, 0:1] > 0

    def pair(p):
        cq = pl.ds(pl.multiple_of(p * 128, 128), 128)
        ck = pl.ds(pl.multiple_of(hc + p * 128, 128), 128)
        cv = pl.ds(pl.multiple_of(2 * hc + p * 128, 128), 128)
        q2, k2, v2, da2 = qkv_ref[:, cq], qkv_ref[:, ck], qkv_ref[:, cv], da_ref[:, cq]
        kt = k2.T
        dk = dv = None
        parts = []
        for a in range(2):
            qa, daa = half_lanes(q2, a), half_lanes(da2, a)
            pt = scores_t(k2, qa, mask)
            dpt = nt(v2, daa)
            delta = jnp.sum(dpt * pt, axis=0, keepdims=True)
            dst = (pt * (dpt - delta)).astype(BF16)
            dva = nn(pt.astype(BF16), daa)
            dka = nn(dst, qa)
            parts.append(nn(kt[a * HEAD:(a + 1) * HEAD, :], dst))
            dk = dka if dk is None else dk + dka
            dv = dva if dv is None else dv + dva
        dq = (jnp.concatenate(parts, axis=0).T * HEAD ** -0.5).astype(BF16)
        dv = dv.astype(BF16)
        dj_ref[:, cq] = dq
        dj_ref[:, ck] = dk.astype(BF16)
        dj_ref[:, cv] = dv
        gbqkv_ref[0:1, cq] = jnp.sum(dq.astype(F32), axis=0, keepdims=True)
        gbqkv_ref[0:1, cv] = jnp.sum(dv.astype(F32), axis=0, keepdims=True)

    loop(hc // 128, pair)
    cp = exchange(dj_ref, wqkv_ref, 1)

    def grads_qkv(j):
        c = cols(j, wide)
        gwqkv_ref[:, c] = tn(h1_ref[...], dj_ref[:, c]).astype(BF16)

    loop(3 * hc // wide, grads_qkv)
    cp.wait()
    norm_back(x_ref, dx2_ref, g0_ref, G1, B1, 1)


def run_bwd(g3, saved, vec, mask, wqkv, wout, wup, wdown):
    rows, d = g3.shape
    hc, f = wout.shape[0], wdown.shape[0]
    both = 2 * rows
    shapes = [
        ((rows, d), F32), (wqkv.shape, BF16), (wout.shape, BF16), (wup.shape, BF16), (wdown.shape, BF16),
        ((8, d), F32), ((8, 3 * hc), F32), ((8, f), F32),
    ]
    args = (g3, *saved, vec, mask, wqkv, wout, wup, wdown)
    return pl.pallas_call(
        bwd_kernel,
        out_shape=[jax.ShapeDtypeStruct(s, t) for s, t in shapes],
        in_specs=[VM] * len(args),
        out_specs=[VM] * len(shapes),
        scratch_shapes=[
            pltpu.VMEM((2, both, d), BF16), pltpu.VMEM((both, f), BF16), pltpu.VMEM((both, hc), BF16),
            pltpu.VMEM((both, 3 * hc), BF16), pltpu.VMEM((rows, d), F32), pltpu.VMEM((rows, d), F32),
            pltpu.VMEM((2, rows, d), BF16), pltpu.VMEM((2, rows, d), BF16),
            pltpu.SemaphoreType.DMA((4,)), pltpu.SemaphoreType.DMA((4,)),
        ],
        compiler_params=pltpu.CompilerParams(
            collective_id=2, has_side_effects=True, vmem_limit_bytes=int(63.5 * 2**20)
        ),
        cost_estimate=pl.CostEstimate(flops=17 * 10**9, bytes_accessed=40 * 10**6, transcendentals=0),
        name="layer_bwd",
    )(*args)


def swap(value, bit):
    return lax.ppermute(value, "grp", [(i, i ^ bit) for i in range(4)])


def pick(value, index, axis):
    return lax.dynamic_index_in_dim(value, index, axis, keepdims=False)


def local(
    tokens, cotangent, image_valid, token_valid,
    norm1_gain, norm1_bias, w_qkv, b_qv, w_out, b_out, norm2_gain, norm2_bias, w_up, b_up, w_down, b_down,
):
    grp = lax.axis_index("grp")
    x, c = grp // 2, grp % 2
    layers, dq, d3 = w_qkv.shape
    d = d3 // 3
    hc = d // 2
    f = 2 * w_down.shape[1] * 1
    seq = tokens.shape[1]
    block = -(-seq // 32) * 32
    rows = 2 * block


    def pad(value):
        return jnp.pad(value, ((0, 0), (0, block - seq), (0, 0)))

    layer_rows = [
        w.reshape(layers, -1, d // 4)
        for w in (norm1_gain, norm1_bias, b_out, norm2_gain, norm2_bias, b_down, b_qv, b_up)
    ]
    pack = jnp.concatenate(layer_rows, axis=1).astype(F32)
    pack = jnp.pad(pack, ((0, 0), (0, SMALL - pack.shape[1]), (0, 0))).reshape(layers * SMALL, d // 4)
    (vqkv, vout, vup, vdown, xs, x2s, h1s, qkvs, atts, h2s, zs, gps, cot, act, vec) = run_fwd(
        pad(tokens), pad(cotangent), pack, token_valid, w_qkv, w_out, w_up, w_down, seq
    )
    smalls = [norm1_gain, norm1_bias, b_out, norm2_gain, norm2_bias, b_down, b_qv, b_up]
    widths = [s.shape[1] for s in smalls]
    activations = act[:, :seq]
    flags = pick(token_valid, x, 0).reshape(2, 2, seq)
    pf = lambda a: jnp.pad(a, (0, block - seq))
    own_flags = jnp.concatenate([pf(pick(pick(flags, x, 0), c, 0)), pf(pick(pick(flags, 1 - x, 0), c, 0))])
    sib_flags = jnp.concatenate([pf(pick(pick(flags, x, 0), 1 - c, 0)), pf(pick(pick(flags, 1 - x, 0), 1 - c, 0))])
    mask = jnp.broadcast_to(jnp.concatenate([own_flags, sib_flags])[:, None], (2 * rows, 128))
    weight = (own_flags * pick(image_valid, x, 0)).astype(F32)
    flow = cot.reshape(rows, d).astype(F32) * weight[:, None]
    vecs = vec.reshape(layers, SMALL, d)[:, :8]
    grads = [None] * layers
    for l in reversed(range(layers)):
        saved = (xs[l], x2s[l], h1s[l], qkvs[l], atts[l], h2s[l], zs[l], gps[l])
        wq, wo, wu, wd = (w[l].reshape(-1, w.shape[-1]) for w in (vqkv, vout, vup, vdown))
        flow, *grads[l] = run_bwd(flow, saved, vecs[l], mask, wq, wo, wu, wd)

    def give_back(value):
        value = value.astype(BF16).reshape(2, block, d)[:, :seq]
        got = swap(value[1], 2)
        return jnp.where(x == 0, jnp.stack([value[0], got]), jnp.stack([got, value[0]]))

    grad_tokens = give_back(flow)

    def reduce_big(index):
        g = jnp.stack([grads[l][index] for l in range(layers)])
        n = g.shape[1] // 2
        keep = lax.dynamic_slice_in_dim(g, x * n, n, 1)
        give = lax.dynamic_slice_in_dim(g, (1 - x) * n, n, 1)
        total = (keep.astype(F32) + swap(give, 2).astype(F32)).astype(BF16)
        return lax.psum(total, "rep")

    def uncolumns(g, groups):
        n = g.shape[1] // 2
        keep = lax.dynamic_slice_in_dim(g, c * n, n, 1)
        give = lax.dynamic_slice_in_dim(g, (1 - c) * n, n, 1)
        got = swap(give, 1)
        keep = keep.reshape(layers, n, groups, 2, -1)
        got = got.reshape(layers, n, groups, 2, -1)
        return jnp.where(c == 0, jnp.stack([keep, got], axis=4), jnp.stack([got, keep], axis=4)).reshape(layers, n, -1).astype(F32)

    gqkv = uncolumns(reduce_big(0), 3)
    gout = reduce_big(1).astype(F32)
    gup = uncolumns(reduce_big(2), 1)
    gdown = reduce_big(3).astype(F32)

    gvec = jnp.stack([grads[l][4][:6].reshape(6 * d) for l in range(layers)])
    gb = jnp.stack([grads[l][5][0] for l in range(layers)]).reshape(layers, 3, 2, -1)[:, ::2]
    gu = jnp.stack([grads[l][6][0] for l in range(layers)]).reshape(layers, 2, -1)

    def spread(v):
        z = jnp.zeros_like(v)
        return jnp.where(c == 0, jnp.stack([v, z], axis=-2), jnp.stack([z, v], axis=-2)).reshape(layers, -1)

    small = lax.psum(jnp.concatenate([gvec, spread(gb), spread(gu)], axis=1), ("rep", "grp"))
    outs, at = [], 0
    for width in widths:
        outs.append(lax.dynamic_slice_in_dim(small[:, at:at + 4 * width], grp * width, width, 1))
        at += 4 * width
    gg1, gb1, gbout, gg2, gb2, gbdown, gbqv, gbup = outs
    return (activations, grad_tokens, gg1, gb1, gqkv, gbqv, gout, gbout, gg2, gb2, gup, gbup, gdown, gbdown)


def solution(mesh):
    rows3, mat, vec = P("rep", "grp", None), P(None, "grp", None), P(None, "grp")
    weights = (vec, vec, mat, vec, mat, vec, vec, vec, mat, vec, mat, vec)
    return jax.shard_map(
        local,
        mesh=mesh,
        in_specs=(rows3, rows3, P("rep"), P("rep", None)) + weights,
        out_specs=(rows3, rows3) + weights,
        check_vma=False,
    )
```

```python
import functools

import jax
import jax.numpy as jnp
from jax import lax
from jax.experimental import pallas as pl
from jax.experimental.pallas import tpu as pltpu
from jax.sharding import PartitionSpec as P

HEAD = 64
MESH = pl.DeviceIdType.MESH
F32 = jnp.float32
BF16 = jnp.bfloat16
VMEM_LIMIT = 62 * 2**20
WIDE = 256
STEP = 16
G1, B1, BOUT, G2, B2, BDOWN, BQV, BUP = 0, 1, 2, 3, 4, 5, 6, 8
SMALL = 16


def nn(a, b):
    return lax.dot_general(a, b, (((1,), (0,)), ((), ())), preferred_element_type=F32)


def nt(a, b):
    return lax.dot_general(a, b, (((1,), (1,)), ((), ())), preferred_element_type=F32)


def tn(a, b):
    return lax.dot_general(a, b, (((0,), (0,)), ((), ())), preferred_element_type=F32)


def span(start, size):
    return pl.ds(pl.multiple_of(start, size), size)


def cols(j, width=WIDE):
    return span(j * width, width)


def loop(count, body):
    def step(j, carry):
        body(j)
        return carry

    lax.fori_loop(0, count, step, 0)


class Place:
    def __init__(self):
        self.rep, self.grp = lax.axis_index("rep"), lax.axis_index("grp")
        rep, grp = self.rep, self.grp
        self.x, self.c = grp // 2, grp % 2
        self.y, self.z = rep % 2, (rep // 2) % 4
        self.zlow = self.z % 2
        core, chip = 1 - 2 * self.c, 2 - 4 * self.x
        self.sib = (rep, grp + core)
        self.xn = (rep, grp + chip)
        self.xd = (rep, grp + chip + core)
        yrep = rep + 1 - 2 * self.y
        self.yn = (yrep, grp)
        self.yd = (yrep, grp + core)
        self.zn = (rep + 2 - 4 * self.zlow, grp)
        self.inner = jnp.logical_or(self.z == 1, self.z == 2)
        self.outer = jnp.logical_not(self.inner)
        self.mid = (rep + 6 - 4 * self.z, grp)


def greet(peers):
    barrier = pltpu.get_barrier_semaphore()
    for peer in peers:
        pl.semaphore_signal(barrier, inc=1, device_id=peer, device_id_type=MESH)
    pl.semaphore_wait(barrier, len(peers))


def remote(src, dst, send, recv, peer):
    return pltpu.make_async_remote_copy(
        src_ref=src, dst_ref=dst, send_sem=send, recv_sem=recv, device_id=peer, device_id_type=MESH
    )


def settle(ref, sem):
    pltpu.make_async_copy(ref, ref, sem).wait()


def norm_rows(v):
    mean = jnp.mean(v, axis=-1, keepdims=True)
    off = v - mean
    rstd = lax.rsqrt(jnp.mean(off * off, axis=-1, keepdims=True) + 1e-6)
    return off * rstd, rstd


def scores_t(k2, qa, mask):
    st = jnp.where(mask, nt(k2, qa), -1e9)
    top = jnp.max(st, axis=0, keepdims=True)
    e = jnp.exp(st - top)
    return e * (1.0 / jnp.sum(e, axis=0, keepdims=True))


def half_lanes(v, a):
    lane = lax.broadcasted_iota(jnp.int32, v.shape, 1)
    return jnp.where((lane >= HEAD) == (a == 1), v, jnp.zeros_like(v))


def chip_flags(at, tv_ref, rows, seq):
    lengths = jnp.sum(tv_ref[...], axis=1, keepdims=True)
    length = jnp.where(at.x == 0, lengths[0:1, :], lengths[1:2, :])
    row = lax.broadcasted_iota(jnp.int32, (2 * rows, 1), 0)
    core = jnp.where(row < rows, at.c, 1 - at.c)
    row = jnp.where(row < rows, row, row - rows)
    block = rows // 2
    chip = jnp.where(row < block, at.x, 1 - at.x)
    row = jnp.where(row < block, row, row - block)
    slot = (2 * chip + core) * seq + row
    return jnp.logical_and(row < seq, slot < length)


class Plan:
    def __init__(self):
        self.now, self.events, self.done = 0.0, [], set()

    def add(self, when, name, action):
        self.events.append((when, name, action))

    def order(self):
        self.events.sort(key=lambda e: e[0])

    def poll(self):
        while self.events and self.events[0][0] <= self.now:
            self.fire()

    def fire(self):
        when, name, action = self.events.pop(0)
        self.now = max(self.now, when)
        action()
        self.done.add(name)

    def need(self, name):
        while name not in self.done:
            self.fire()

    def spend(self, us):
        self.now += us
        self.poll()


KINDS = ("qkv", "out", "up", "down")


def fwd_kernel(
    seq, tok_ref, cot_ref, pack_ref, tv_ref, wqkv_in, wout_in, wup_in, wdown_in,
    vqkv, vout, vup, vdown, xs, x2s, h1s, qkvs, as_, h2s, zs, gps, cot_out, act_out, vec_out,
    wqkv, wout, wup, wdown, x_ref, x2_ref, h1, qkv, att, h2, z, gp, put, got, tok, vec, bup,
    s_rx, s_ry, s_rz, s_ra, s_rb, s_rs, s_loc, s_send, s_core, r_core, s_save, s_misc, r_misc,
):
    at = Place()
    layers = vqkv.shape[0]
    rows, d = x_ref.shape
    block = rows // 2
    hc, f = att.shape[1], z.shape[1]
    own, other = pl.ds(0, rows), pl.ds(rows, rows)
    x, c = at.x, at.c
    quarter = at.y * 2 + at.zlow
    ins = dict(qkv=wqkv_in, out=wout_in, up=wup_in, down=wdown_in)
    full = dict(qkv=wqkv, out=wout, up=wup, down=wdown)
    saves = dict(qkv=vqkv, out=vout, up=vup, down=vdown)
    runs = dict(qkv=(d // 4, 6), up=(f // 2, 2))
    plan = Plan()
    index = {}
    for l in range(layers):
        for kind in KINDS:
            index[l, kind] = len(index)

    greet((at.sib, at.xn, at.xd, at.yn, at.zn))

    first = [
        remote(tok_ref.at[1 - x], tok.at[1], s_misc.at[0], r_misc.at[0], at.xn),
        pltpu.make_async_copy(tok_ref.at[x], tok.at[0], s_misc.at[3]),
    ]
    here = vec.at[:, span(at.grp * WIDE, WIDE)]
    first += [
        pltpu.make_async_copy(pack_ref, here, s_misc.at[4]),
        remote(pack_ref, here, s_misc.at[5], r_misc.at[5], at.sib),
        remote(pack_ref, here, s_misc.at[6], r_misc.at[6], at.xn),
        remote(pack_ref, here, s_misc.at[7], r_misc.at[7], at.xd),
    ]
    for copy in first:
        copy.start()

    def launch(l, kind):
        i = index[l, kind]
        src, dst = ins[kind].at[l], full[kind].at[l]
        n = src.shape[0]
        q = n // 4
        part = span(quarter * q, q)
        if kind in runs:
            width, count = runs[kind]
            mine = 2 * x + c
            for j in range(count):
                to = pl.ds(j * width, width)
                keep = span((2 * j + c) * width, width)
                give = span((2 * j + 1 - c) * width, width)
                remote(src.at[part, keep], dst.at[mine, part, to], s_send.at[i], s_rx.at[i], at.xn).start()
                remote(src.at[part, give], dst.at[mine, part, to], s_send.at[i], s_rx.at[i], at.xd).start()
            for j in range(count):
                to = pl.ds(j * width, width)
                keep = span((2 * j + c) * width, width)
                give = span((2 * j + 1 - c) * width, width)
                remote(src.at[:, give], dst.at[mine, :, to], s_send.at[i], s_rs.at[i], at.sib).start()
                pltpu.make_async_copy(src.at[:, keep], dst.at[mine, :, to], s_loc.at[i]).start()
        else:
            remote(src.at[part], dst.at[x, part], s_send.at[i], s_rx.at[i], at.xn).start()
            pltpu.make_async_copy(src, dst.at[x], s_loc.at[i]).start()

    def theirs(l, kind, part):
        dst = full[kind].at[l]
        if kind in runs:
            return dst.at[span(2 * (1 - x), 2), part]
        return dst.at[pl.ds(1 - x, 1), part]

    def part_of(kind, y, zlow, half=None):
        q = full[kind].shape[2] // 4
        if half is None:
            return span((2 * y + zlow) * q, q)
        return span((4 * y + 2 * zlow + half) * (q // 2), q // 2)

    def relay1(l, kind):
        i = index[l, kind]
        piece = theirs(l, kind, part_of(kind, at.y, at.zlow))
        settle(piece, s_rx.at[i])
        remote(piece, piece, s_send.at[i], s_ry.at[i], at.yn).start()
        remote(piece, piece, s_send.at[i], s_rz.at[i], at.zn).start()

    def relay2(l, kind):
        i = index[l, kind]
        settle(theirs(l, kind, part_of(kind, 1 - at.y, at.zlow)), s_ry.at[i])
        piece = theirs(l, kind, part_of(kind, 1 - at.y, at.zlow, 0))
        remote(piece, piece, s_send.at[i], s_ra.at[i], at.zn).start()
        settle(theirs(l, kind, part_of(kind, at.y, 1 - at.zlow)), s_rz.at[i])
        piece = theirs(l, kind, part_of(kind, at.y, 1 - at.zlow, 1))
        remote(piece, piece, s_send.at[i], s_rb.at[i], at.yn).start()

    def ready(l, kind):
        i = index[l, kind]
        settle(theirs(l, kind, part_of(kind, 1 - at.y, 1 - at.zlow, 0)), s_ra.at[i])
        settle(theirs(l, kind, part_of(kind, 1 - at.y, 1 - at.zlow, 1)), s_rb.at[i])
        if kind in runs:
            settle(full[kind].at[l, 0], s_rs.at[i])
        settle(full[kind].at[l, 0], s_loc.at[i])
        pltpu.make_async_copy(full[kind].at[l], saves[kind].at[l], s_loc.at[i]).start()

    x_time, yz_time = 9.0, 16.0
    for l in range(layers):
        for kind in KINDS:
            launch(l, kind)
            mb = full[kind].shape[1] * full[kind].shape[2] * full[kind].shape[3] / 2**20
            mb *= 2
            x_time += mb / 4 / 0.094 * 1.05
            plan.add(x_time + 1.5, ("r1", l, kind), functools.partial(relay1, l, kind))
            yz_time = max(yz_time, x_time + 1.5)
            plan.add(yz_time + mb / 4 / 0.094 + 1.5, ("r2", l, kind), functools.partial(relay2, l, kind))
            yz_time += mb * 3 / 8 / 0.094 * 1.05
            plan.add(yz_time + 4, ("ok", l, kind), functools.partial(ready, l, kind))
    plan.order()
    late = [
        remote(cot_ref.at[1 - x], cot_out.at[1], s_misc.at[1], r_misc.at[1], at.xn),
        pltpu.make_async_copy(cot_ref.at[x], cot_out.at[0], s_misc.at[8]),
    ]
    for copy in late:
        copy.start()

    first[1].wait()
    first[2].wait()
    for copy in (first[0], *first[3:]):
        copy.wait()
    for i in range(2):
        for j in range(block // STEP):
            x_ref[pl.ds(i * block + j * STEP, STEP), :] = tok[i, pl.ds(j * STEP, STEP), :].astype(F32)
    vec_save = pltpu.make_async_copy(vec, vec_out, s_misc.at[9])
    vec_save.start()
    for l in range(layers):
        for j in range(f // WIDE):
            half, sub = divmod(j, f // WIDE // 2)
            bup[l:l + 1, pl.ds(j * WIDE, WIDE)] = vec[
                l * SMALL + BUP + sub:l * SMALL + BUP + sub + 1, span((2 * half + c) * WIDE, WIDE)
            ]
    mask = chip_flags(at, tv_ref, rows, seq)
    plan.now = 12.0
    plan.poll()

    def save(src, dst, slot):
        copy = pltpu.make_async_copy(src, dst, s_save.at[slot])
        copy.start()
        return copy

    pending = {}
    for l in range(layers):
        def row(name, l=l):
            return vec[l * SMALL + name:l * SMALL + name + 1, :]

        def norm_out(src_ref, dst_ref, gain, shift, l=l):
            for i in range(rows // STEP):
                r = pl.ds(i * STEP, STEP)
                hat, _ = norm_rows(src_ref[r, :])
                dst_ref[r, :] = (hat * row(gain) + row(shift)).astype(BF16)

        def weight(kind, cs, l=l):
            w = full[kind][l, :, :, cs]
            return w.reshape(w.shape[0] * w.shape[1], w.shape[2])

        norm_out(x_ref, h1, G1, B1)
        cp = remote(h1.at[own], h1.at[other], s_core.at[0], r_core.at[0], at.sib)
        cp.start()
        x_saved = save(x_ref, xs.at[l], 0)
        plan.spend(2)
        plan.need(("ok", l, "qkv"))
        if l:
            pending["qkv"].wait()
        bq = jnp.where(c == 0, row(BQV), vec[l * SMALL + BQV + 1:l * SMALL + BQV + 2, :])
        scale = HEAD ** -0.5
        parts = (
            (0, bq[:, :hc] * scale, scale), (hc, jnp.zeros((1, hc), F32), 1.0), (2 * hc, bq[:, hc:], 1.0)
        )

        def qkv_rows(r, l=l, parts=parts):
            for base, bias, factor in parts:
                for j in range(hc // WIDE):
                    cs = pl.ds(base + j * WIDE, WIDE)
                    out = nn(h1[r, :], weight("qkv", cs))
                    qkv[r, cs] = (out * factor + bias[:, j * WIDE:(j + 1) * WIDE]).astype(BF16)

        qkv_rows(own)
        plan.spend(2)
        cp.wait()
        qkv_rows(other)
        h1_saved = save(h1, h1s.at[l], 1)
        pending["qkv"] = save(qkv, qkvs.at[l], 2)
        plan.spend(2)
        if l:
            pending["att"].wait()
        for p in range(hc // 128):
            q2 = qkv[:, p * 128:(p + 1) * 128]
            k2 = qkv[:, hc + p * 128:hc + (p + 1) * 128]
            v2 = qkv[:, 2 * hc + p * 128:2 * hc + (p + 1) * 128]
            vt = v2.T
            outs = []
            for a in range(2):
                pt = scores_t(k2, half_lanes(q2, a), mask)
                outs.append(nn(vt[a * HEAD:(a + 1) * HEAD, :], pt.astype(BF16)))
            att[:, p * 128:(p + 1) * 128] = jnp.concatenate(outs, axis=0).T.astype(BF16)
            plan.spend(3)
        pending["att"] = save(att, as_.at[l], 3)

        def exchange(left, kind, base, bias, out, slot):
            def far(j):
                put[:, cols(j)] = nn(left[other, :], weight(kind, cols(j))).astype(BF16)

            loop(d // WIDE, far)
            cp = remote(put, got.at[slot], s_core.at[1], r_core.at[1], at.sib)
            cp.start()

            def near(j):
                out[:, cols(j)] = nn(left[own, :], weight(kind, cols(j))) + base[:, cols(j)] + vec[
                    l * SMALL + bias:l * SMALL + bias + 1, cols(j)
                ]

            loop(d // WIDE, near)
            cp.wait()
            out[...] += got[slot].astype(F32)

        plan.need(("ok", l, "out"))
        if l:
            pending["x2"].wait()
        exchange(att, "out", x_ref, BOUT, x2_ref, 0)
        pending["x2"] = save(x2_ref, x2s.at[l], 4)
        plan.spend(3)
        norm_out(x2_ref, h2, G2, B2)
        cp = remote(h2.at[own], h2.at[other], s_core.at[2], r_core.at[2], at.sib)
        cp.start()
        plan.spend(2)
        plan.need(("ok", l, "up"))
        if l:
            pending["z"].wait()
            pending["gp"].wait()

        def up_rows(r):
            def body(j):
                u = nn(h2[r, :], weight("up", cols(j))) + bup[l:l + 1, cols(j)]
                phi = 0.5 + 0.5 * lax.erf(u * 0.7071067811865476)
                z[r, cols(j)] = (u * phi).astype(BF16)
                gp[r, cols(j)] = (phi + u * jnp.exp(u * u * -0.5) * 0.3989422804014327).astype(BF16)

            loop(f // WIDE, body)

        up_rows(own)
        plan.spend(4)
        cp.wait()
        up_rows(other)
        h2_saved = save(h2, h2s.at[l], 5)
        pending["z"] = save(z, zs.at[l], 6)
        pending["gp"] = save(gp, gps.at[l], 7)
        plan.spend(4)
        plan.need(("ok", l, "down"))
        for copy in (x_saved, h1_saved, h2_saved):
            copy.wait()
        exchange(z, "down", x2_ref, BDOWN, x_ref, 1)
        plan.spend(4)

    for i in range(2):
        for j in range(block // STEP):
            tok[i, pl.ds(j * STEP, STEP), :] = x_ref[pl.ds(i * block + j * STEP, STEP), :].astype(BF16)
    act = [
        remote(tok.at[1], act_out.at[x], s_misc.at[2], r_misc.at[2], at.xn),
        pltpu.make_async_copy(tok.at[0], act_out.at[x], s_misc.at[10]),
    ]
    for copy in act:
        copy.start()
    for copy in (*act, *late, vec_save):
        copy.wait()
    for name in ("qkv", "att", "x2", "z", "gp"):
        pending[name].wait()
    for (l, kind), i in index.items():
        settle(full[kind].at[l, pl.ds(0, 3 if kind in runs else 1)], s_send.at[i])
        settle(full[kind].at[l], s_loc.at[i])


ANY = pl.BlockSpec(memory_space=pl.ANY)
VM = pl.BlockSpec(memory_space=pltpu.VMEM)


def dma(*shape):
    return pltpu.SemaphoreType.DMA(shape)


def run_fwd(tok, cot, pack, tv, w_qkv, w_out, w_up, w_down, seq):
    layers, n, d3 = w_qkv.shape
    d = d3 // 3
    hc, f = d // 2, 2 * w_down.shape[1]
    block = tok.shape[1]
    rows, both = 2 * block, 4 * block
    weights = [(4, n, 3 * hc), (2, n, d), (4, n, f), (2, w_down.shape[1], d)]
    acts = [
        ((rows, d), F32), ((rows, d), F32), ((both, d), BF16), ((both, 3 * hc), BF16),
        ((both, hc), BF16), ((both, d), BF16), ((both, f), BF16), ((both, f), BF16),
    ]
    shapes = [((layers, *s), BF16) for s in weights] + [((layers, *s), t) for s, t in acts]
    shapes += [((2, block, d), BF16), ((2, block, d), BF16), ((layers * SMALL, d), F32)]
    count = layers * len(KINDS)
    return pl.pallas_call(
        functools.partial(fwd_kernel, seq),
        out_shape=[jax.ShapeDtypeStruct(s, t) for s, t in shapes],
        in_specs=[ANY, ANY, VM, VM, ANY, ANY, ANY, ANY],
        out_specs=[ANY] * len(shapes),
        scratch_shapes=[pltpu.VMEM((layers, *s), BF16) for s in weights]
        + [pltpu.VMEM(s, t) for s, t in acts]
        + [
            pltpu.VMEM((rows, d), BF16), pltpu.VMEM((2, rows, d), BF16),
            pltpu.VMEM((2, block, d), BF16), pltpu.VMEM((layers * SMALL, d), F32), pltpu.VMEM((8, f), F32),
        ]
        + [dma(count)] * 8
        + [dma(3), dma(3), dma(8), dma(11), dma(8)],
        compiler_params=pltpu.CompilerParams(
            collective_id=1, has_side_effects=True, vmem_limit_bytes=VMEM_LIMIT
        ),
        cost_estimate=pl.CostEstimate(flops=17 * 10**9, bytes_accessed=80 * 10**6, transcendentals=0),
        name="forward",
    )(tok, cot, pack, tv, w_qkv, w_out, w_up, w_down)


NS, NY, NZ, NT = 6, 3, 4, 6
CHUNK = 256


class Ring:
    def __init__(self, at, plan, chunks, outs, bufs, sems):
        self.at, self.plan, self.chunks, self.outs = at, plan, chunks, outs
        self.g, self.xr, self.yr, self.zr, self.wr, self.t = bufs
        (self.x_send, self.x_recv, self.y_send, self.y_recv, self.z_send, self.z_recv, self.w_send, self.w_recv,
         self.f_send, self.f_recv, self.cx, self.cy, self.cz, self.cw, self.cb) = sems
        self.count = len(chunks)
        self.x_free = 0.0
        self.copies = {}

    def size(self, u):
        return 64 if self.chunks[u][0] == "small" else CHUNK

    def reserve(self, u):
        if u >= NS:
            self.plan.need(("s2", u - NS))

    def launch(self, u):
        n = self.size(u)
        if u >= NS:
            pl.semaphore_wait(self.cx, 1)
        copy = remote(
            self.g.at[u % NS, 0, pl.ds(0, n)], self.xr.at[u % NS, pl.ds(0, n)],
            self.x_send.at[u % NS], self.x_recv.at[u % NS], self.at.xn,
        )
        copy.start()
        self.copies["x", u] = copy
        plan = self.plan
        self.x_free = max(plan.now, self.x_free) + 11.3 * n / CHUNK
        t = self.x_free + 2
        for k, lag in enumerate((0, 8, 16, 24, 32, 43)):
            plan.add(t + lag, (f"s{k + 1}", u), functools.partial(getattr(self, f"s{k + 1}"), u))
        plan.order()

    def credit(self, sem, u, slots, peer):
        if u + slots < self.count:
            pl.semaphore_signal(sem, inc=1, device_id=peer, device_id_type=MESH)

    def claim(self, sem, u, slots):
        if u >= slots:
            pl.semaphore_wait(sem, 1)

    def add(self, dst, src, count, base=None, base_at=None):
        def body(j):
            r = cols(j, 32)
            b = dst[r, :] if base is None else base[pl.ds(pl.multiple_of(base_at + j * 32, 32), 32), :]
            dst[r, :] = (b.astype(F32) + src[r, :].astype(F32)).astype(BF16)

        loop(count // 32, body)

    def s1(self, u):
        n, at = self.size(u), self.at
        slot = u % NS
        self.copies["x", u].wait()
        self.add(self.g.at[slot, 1], self.xr.at[slot], n)
        self.credit(self.cx, u, NS, at.xn)
        self.claim(self.cy, u, NY)
        copy = remote(
            self.g.at[slot, 1, span((1 - at.y) * (n // 2), n // 2)], self.yr.at[u % NY, pl.ds(0, n // 2)],
            self.y_send.at[slot], self.y_recv.at[u % NY], at.yn,
        )
        copy.start()
        self.copies["y", u] = copy

    def part(self, ref, u, slots):
        return ref.at[u % slots, pl.ds(0, self.size(u) // 2)]

    def s2(self, u):
        n, at = self.size(u), self.at
        t = self.part(self.t, u, NT)
        self.copies["y", u].wait()
        self.add(t, self.part(self.yr, u, NY), n // 2, self.g.at[u % NS, 1], at.y * (n // 2))
        self.credit(self.cy, u, NY, at.yn)

        @pl.when(at.outer)
        def _():
            self.claim(self.cz, u, NZ)
            remote(t, self.part(self.zr, u, NZ), self.z_send.at[u % NT], self.z_recv.at[u % NZ], at.zn).start()

    def s3(self, u):
        n, at = self.size(u), self.at
        t = self.part(self.t, u, NT)

        @pl.when(at.outer)
        def _():
            settle(t, self.z_send.at[u % NT])

        @pl.when(at.inner)
        def _():
            got = self.part(self.zr, u, NZ)
            settle(got, self.z_recv.at[u % NZ])
            self.add(t, got, n // 2)
            self.credit(self.cz, u, NZ, at.zn)
            self.claim(self.cw, u, NZ)
            remote(t, self.part(self.wr, u, NZ), self.z_send.at[u % NT], self.w_recv.at[u % NZ], at.mid).start()

    def s4(self, u):
        n, at = self.size(u), self.at

        @pl.when(at.inner)
        def _():
            t = self.part(self.t, u, NT)
            got = self.part(self.wr, u, NZ)
            settle(got, self.w_recv.at[u % NZ])
            settle(t, self.z_send.at[u % NT])
            self.add(t, got, n // 2)
            self.credit(self.cw, u, NZ, at.mid)
            self.claim(self.cb, u, NZ)
            remote(t, self.part(self.zr, u, NZ), self.w_send.at[u % NT], self.z_recv.at[u % NZ], at.zn).start()

    def s5(self, u):
        n, at = self.size(u), self.at
        t = self.part(self.t, u, NT)

        @pl.when(at.outer)
        def _():
            got = self.part(self.zr, u, NZ)
            settle(got, self.z_recv.at[u % NZ])

            def body(j):
                t[cols(j, 32), :] = got[cols(j, 32), :]

            loop(n // 64, body)
            self.credit(self.cb, u, NZ, at.zn)

        kind, l, i = self.chunks[u]
        out = self.outs[kind]
        sent = self.f_send.at[u % NT]
        if kind == "small":
            pltpu.make_async_copy(t, out, sent).start()
            return
        half = n // 2
        width = t.shape[1]

        def deliver(src, dst, mine, kind_index):
            if mine:
                pltpu.make_async_copy(src, dst, sent).start()
                remote(src, dst, sent, self.f_recv.at[kind_index], at.yn).start()
            else:
                remote(src, dst, sent, self.f_recv.at[kind_index], at.sib).start()
                remote(src, dst, sent, self.f_recv.at[kind_index], at.yd).start()

        if kind in ("down", "out"):
            deliver(t, out.at[l, span(i * n + at.y * half, half)], True, KINDS.index(kind))
        elif kind == "up":
            side, run = divmod(i, 2)
            deliver(t, out.at[l, span(at.y * half, half), span((2 * run + at.c) * width, width)], side == 0, 2)
        else:
            for side in range(2):
                for run in range(2):
                    src = t.at[:, pl.ds((2 * side + run) * WIDE, WIDE)]
                    dst = out.at[l, span(at.y * half, half), span(i * width + (2 * run + at.c) * WIDE, WIDE)]
                    deliver(src, dst, side == 0, 0)

    def s6(self, u):
        at = self.at
        t = self.part(self.t, u, NT)
        if self.chunks[u][0] == "small":
            settle(t, self.f_send.at[u % NT])
        else:
            settle(self.g.at[0, 0], self.f_send.at[u % NT])

        @pl.when(at.inner)
        def _():
            settle(t, self.w_send.at[u % NT])

    def finish(self):
        while self.plan.events:
            self.plan.fire()
        for i, kind in enumerate(KINDS):
            out = self.outs[kind]
            rows = out.shape[1]
            settle(out.at[:, pl.ds(0, rows // 2 if kind in ("out", "down") else rows * 3 // 4)], self.f_recv.at[i])


def bwd_kernel(
    seq, cot_ref, vec_ref, tv_ref, iv_ref, vqkv, vout, vup, vdown, xs, x2s, h1s, qkvs, as_, h2s, zs, gps,
    oqkv, oout, oup, odown, osmall, otok,
    wqkv, wout, wup, wdown, x_ref, x2_ref, h1, qkv, att, h2, z, gp,
    tok, g_ref, dm, da, dj, dx2, dh, put, got, small, small_put, small_got, ring_g, ring_x, ring_y, ring_z, ring_w, ring_t,
    s_load, s_core, r_core, s_misc, r_misc, *ring_sems,
):
    at = Place()
    layers = vqkv.shape[0]
    rows, d = x_ref.shape
    block = rows // 2
    hc, f = att.shape[1], z.shape[1]
    own, other = pl.ds(0, rows), pl.ds(rows, rows)
    x, c = at.x, at.c
    plan = Plan()
    chunks = []
    for l in reversed(range(layers)):
        chunks += [("down", l, i) for i in range(4)] + [("up", l, i) for i in range(4)]
        chunks += [("out", l, 0)] + [("qkv", l, i) for i in range(3)]
    chunks.append(("small", 0, 0))
    ring = Ring(
        at, plan, chunks, dict(qkv=oqkv, out=oout, up=oup, down=odown, small=osmall),
        (ring_g, ring_x, ring_y, ring_z, ring_w, ring_t), ring_sems,
    )
    number = {chunk: u for u, chunk in enumerate(chunks)}

    stores = dict(
        z=(zs, z), wdown=(vdown, wdown), gp=(gps, gp), h2=(h2s, h2), wup=(vup, wup), x2=(x2s, x2_ref),
        wout=(vout, wout), att=(as_, att), qkv=(qkvs, qkv), wqkv=(vqkv, wqkv), h1=(h1s, h1), x=(xs, x_ref),
    )
    slots = {name: i for i, name in enumerate(stores)}
    loads = {}

    def load(name, l):
        if l < 0:
            return
        src, dst = stores[name]
        loads[name, l] = pltpu.make_async_copy(src.at[l], dst, s_load.at[slots[name]])
        loads[name, l].start()

    cot_load = pltpu.make_async_copy(cot_ref, tok, s_misc.at[0])
    cot_load.start()
    for name in stores:
        load(name, layers - 1)
    greet((at.sib, at.xn, at.yn, at.yd, at.zn, at.mid))

    def by_half(hh):
        return hh * x + (1 - hh) * (1 - x)

    mask = chip_flags(at, tv_ref, rows, seq)
    valid = jnp.where(x == 0, iv_ref[0:1, 0:1], iv_ref[1:2, 0:1]).astype(F32)
    weight = mask[:rows].astype(F32) * valid
    small[...] = jnp.zeros_like(small)
    cot_load.wait()
    for i in range(2):
        for j in range(block // STEP):
            r = i * block + j * STEP
            g_ref[pl.ds(r, STEP), :] = tok[i, pl.ds(j * STEP, STEP), :].astype(F32) * weight[r:r + STEP, :]

    for l in reversed(range(layers)):
        def row(name, l=l):
            return vec_ref[l * SMALL + name:l * SMALL + name + 1, :]

        def set_small(name, value, l=l):
            small[l * SMALL + name:l * SMALL + name + 1, :] = value

        def send_round(src_ref, name, slot):
            total = jnp.zeros((8, d), F32)
            for i in range(rows // STEP):
                r = pl.ds(i * STEP, STEP)
                low = src_ref[r, :].astype(BF16)
                dm[slot, r, :] = low
                low = low.astype(F32)
                total = total + low[0:8, :] + low[8:16, :]
            set_small(name, jnp.sum(total, axis=0, keepdims=True))
            copy = remote(dm.at[slot, own], dm.at[slot, other], s_core.at[slot], r_core.at[slot], at.sib)
            copy.start()
            return copy

        def exchange(left, w):
            per = w.shape[1]

            def piece(j):
                b = j // (per // WIDE)
                return w[b, span((j % (per // WIDE)) * WIDE, WIDE), :]

            def far(j):
                put[:, cols(j)] = nt(left[other, :], piece(j)).astype(BF16)

            loop(d // WIDE, far)
            copy = remote(put, got, s_core.at[2], r_core.at[2], at.sib)
            copy.start()

            def near(j):
                dh[:, cols(j)] = nt(left[own, :], piece(j))

            loop(d // WIDE, near)
            copy.wait()

        def norm_back(value_ref, base_ref, out_ref, gain, shift):
            total_g = jnp.zeros((8, d), F32)
            total_b = jnp.zeros((8, d), F32)
            for i in range(rows // STEP):
                r = pl.ds(i * STEP, STEP)
                hat, rstd = norm_rows(value_ref[r, :])
                grad = dh[r, :] + got[r, :].astype(F32)
                prod = grad * hat
                total_g = total_g + prod[0:8, :] + prod[8:16, :]
                total_b = total_b + grad[0:8, :] + grad[8:16, :]
                dhat = grad * row(gain)
                m1 = jnp.mean(dhat, axis=-1, keepdims=True)
                m2 = jnp.mean(dhat * hat, axis=-1, keepdims=True)
                out_ref[r, :] = base_ref[r, :] + rstd * (dhat - m1 - hat * m2)
            set_small(gain, jnp.sum(total_g, axis=0, keepdims=True))
            set_small(shift, jnp.sum(total_b, axis=0, keepdims=True))

        def produce(chunk, maker, us):
            u = number[chunk]
            ring.reserve(u)
            loop(2, lambda hh: maker(ring_g.at[u % NS, hh], by_half(hh)))
            ring.launch(u)
            plan.spend(us)

        copy = send_round(g_ref, BDOWN, 0)
        loads["z", l].wait()
        plan.spend(2)
        copy.wait()
        for i in range(4):
            def make(dst, h, i=i):
                dst[...] = tn(z[:, span(h * (f // 2) + i * CHUNK, CHUNK)], dm[0]).astype(BF16)

            produce(("down", l, i), make, 1.3)
        load("z", l - 1)
        loads["wdown", l].wait()
        loads["gp", l].wait()

        def dz_body(j):
            b = j // (f // 2 // WIDE)
            w = wdown[b, span((j % (f // 2 // WIDE)) * WIDE, WIDE), :]
            for r in (own, other):
                low = (nt(dm[0, r, :], w) * gp[r, cols(j)].astype(F32)).astype(BF16)
                gp[r, cols(j)] = low

        loop(f // WIDE, dz_body)
        plan.spend(4)
        load("wdown", l - 1)
        for j in range(f // WIDE):
            half, sub = divmod(j, f // WIDE // 2)
            small[l * SMALL + BUP + sub:l * SMALL + BUP + sub + 1, span((2 * half + c) * WIDE, WIDE)] = jnp.sum(
                gp[:, j * WIDE:(j + 1) * WIDE].astype(F32), axis=0, keepdims=True
            )
        loads["h2", l].wait()
        loads["wup", l].wait()
        for i in range(4):
            side, run = divmod(i, 2)

            def make(dst, h, side=side, run=run):
                rh = c if side == 0 else 1 - c
                left = h2[:, span(h * (d // 2) + rh * CHUNK, CHUNK)]
                dst[...] = tn(left, gp[:, run * (f // 2):(run + 1) * (f // 2)]).astype(BF16)

            if i == 2:
                exchange(gp, wup)
                load("wup", l - 1)
                loads["x2", l].wait()
                plan.spend(4)
                norm_back(x2_ref, g_ref, dx2, G2, B2)
                load("x2", l - 1)
                plan.spend(3)
                copy = send_round(dx2, BOUT, 1)
            produce(("up", l, i), make, 1.3)
        load("gp", l - 1)
        load("h2", l - 1)

        loads["wout", l].wait()
        loads["att", l].wait()
        copy.wait()
        for j in range(hc // WIDE):
            for r in (own, other):
                da[r, pl.ds(j * WIDE, WIDE)] = nt(dm[1, r, :], wout[j]).astype(BF16)
        load("wout", l - 1)

        def make(dst, h):
            dst[...] = tn(att[:, span(h * CHUNK, CHUNK)], dm[1]).astype(BF16)

        produce(("out", l, 0), make, 2)
        load("att", l - 1)
        loads["qkv", l].wait()
        sums = {}
        for p in range(hc // 128):
            cq, ck, cv = (pl.ds(k * hc + p * 128, 128) for k in range(3))
            q2, k2, v2, da2 = qkv[:, cq], qkv[:, ck], qkv[:, cv], da[:, cq]
            kt = k2.T
            dk = dv = None
            parts = []
            for a in range(2):
                qa, daa = half_lanes(q2, a), half_lanes(da2, a)
                pt = scores_t(k2, qa, mask)
                dpt = nt(v2, daa)
                delta = jnp.sum(dpt * pt, axis=0, keepdims=True)
                dst = (pt * (dpt - delta)).astype(BF16)
                dva = nn(pt.astype(BF16), daa)
                dka = nn(dst, qa)
                parts.append(nn(kt[a * HEAD:(a + 1) * HEAD, :], dst))
                dk = dka if dk is None else dk + dka
                dv = dva if dv is None else dv + dva
            dq = (jnp.concatenate(parts, axis=0).T * HEAD ** -0.5).astype(BF16)
            dv = dv.astype(BF16)
            dj[:, cq] = dq
            dj[:, ck] = dk.astype(BF16)
            dj[:, cv] = dv
            for k, value in ((0, dq), (1, dv)):
                total = jnp.sum(value.astype(F32), axis=0, keepdims=True)
                for core in range(2):
                    r = l * SMALL + BQV + core
                    small[r:r + 1, k * hc + p * 128:k * hc + (p + 1) * 128] = jnp.where(
                        c == core, total, jnp.zeros_like(total)
                    )
            plan.spend(5.5)
        load("qkv", l - 1)
        loads["wqkv", l].wait()
        loads["h1", l].wait()
        for i in range(3):
            def make(dst, h, i=i):
                for side in range(2):
                    rh = c if side == 0 else 1 - c
                    left = h1[:, span(h * (d // 2) + rh * CHUNK, CHUNK)]
                    dst[:, side * hc:(side + 1) * hc] = tn(left, dj[:, i * hc:(i + 1) * hc]).astype(BF16)

            if i == 1:
                exchange(dj, wqkv)
                load("wqkv", l - 1)
                loads["x", l].wait()
                plan.spend(4)
                norm_back(x_ref, dx2, g_ref, G1, B1)
                load("x", l - 1)
                plan.spend(3)
            produce(("qkv", l, i), make, 1.3)
        load("h1", l - 1)

    for i in range(2):
        for j in range(block // STEP):
            tok[i, pl.ds(j * STEP, STEP), :] = g_ref[pl.ds(i * block + j * STEP, STEP), :].astype(BF16)
    back = [
        remote(tok.at[1], otok.at[x], s_misc.at[1], r_misc.at[1], at.xn),
        pltpu.make_async_copy(tok.at[0], otok.at[x], s_misc.at[2]),
    ]
    small_put[...] = small[...].astype(BF16)
    copy = remote(small_put, small_got, s_misc.at[3], r_misc.at[3], at.sib)
    copy.start()
    copy.wait()
    total = (small_put[...].astype(F32) + small_got[...].astype(F32)).astype(BF16)
    u = number["small", 0, 0]
    ring.reserve(u)
    n = total.shape[0]
    for hh in range(2):
        for k in range(2):
            ring_g[u % NS, hh, k * n:(k + 1) * n, :] = total
    ring.launch(u)
    for copy in back:
        copy.start()
    ring.finish()
    for copy in back:
        copy.wait()


def run_bwd(cot, vec, tv, iv, weights, acts, seq):
    layers, _, n, hc3 = weights[0].shape
    d = acts[0].shape[2]
    rows = acts[0].shape[1]
    block, both = rows // 2, 2 * rows
    hc, f = hc3 // 3, weights[2].shape[3]
    outs = [(layers, n, 3 * d), (layers, n, d), (layers, n, 2 * f), (layers, f // 2, d), (layers * SMALL, d), (2, block, d)]
    args = (cot, vec, tv, iv, *weights, *acts)
    return pl.pallas_call(
        functools.partial(bwd_kernel, seq),
        out_shape=[jax.ShapeDtypeStruct(s, BF16) for s in outs],
        in_specs=[ANY, VM, VM, VM] + [ANY] * 12,
        out_specs=[ANY] * len(outs),
        scratch_shapes=[pltpu.VMEM(w.shape[1:], w.dtype) for w in (*weights, *acts)]
        + [
            pltpu.VMEM((2, block, d), BF16), pltpu.VMEM((rows, d), F32), pltpu.VMEM((2, both, d), BF16),
            pltpu.VMEM((both, hc), BF16), pltpu.VMEM((both, 3 * hc), BF16), pltpu.VMEM((rows, d), F32),
            pltpu.VMEM((rows, d), F32), pltpu.VMEM((rows, d), BF16), pltpu.VMEM((rows, d), BF16),
            pltpu.VMEM((layers * SMALL, d), F32), pltpu.VMEM((layers * SMALL, d), BF16),
            pltpu.VMEM((layers * SMALL, d), BF16),
            pltpu.VMEM((NS, 2, CHUNK, d), BF16), pltpu.VMEM((NS, CHUNK, d), BF16),
            pltpu.VMEM((NY, CHUNK // 2, d), BF16), pltpu.VMEM((NZ, CHUNK // 2, d), BF16),
            pltpu.VMEM((NZ, CHUNK // 2, d), BF16), pltpu.VMEM((NT, CHUNK // 2, d), BF16),
            dma(12), dma(3), dma(3), dma(4), dma(4),
            dma(NS), dma(NS), dma(NS), dma(NY), dma(NT), dma(NZ), dma(NT), dma(NZ), dma(NT), dma(4),
        ]
        + [pltpu.SemaphoreType.REGULAR] * 5,
        compiler_params=pltpu.CompilerParams(
            collective_id=2, has_side_effects=True, vmem_limit_bytes=VMEM_LIMIT
        ),
        cost_estimate=pl.CostEstimate(flops=34 * 10**9, bytes_accessed=120 * 10**6, transcendentals=0),
        name="backward",
    )(*args)


def local(
    tokens, cotangent, image_valid, token_valid,
    norm1_gain, norm1_bias, w_qkv, b_qv, w_out, b_out, norm2_gain, norm2_bias, w_up, b_up, w_down, b_down,
):
    grp = lax.axis_index("grp")
    layers, n, _ = w_qkv.shape
    seq, d = tokens.shape[1:]
    block = -(-seq // 32) * 32

    def pad(value):
        return jnp.pad(value, ((0, 0), (0, block - seq), (0, 0)))

    smalls = (norm1_gain, norm1_bias, b_out, norm2_gain, norm2_bias, b_down, b_qv, b_up)
    pack = jnp.concatenate([w.reshape(layers, -1, d // 4) for w in smalls], axis=1).astype(F32)
    pack = jnp.pad(pack, ((0, 0), (0, SMALL - pack.shape[1]), (0, 0))).reshape(layers * SMALL, d // 4)
    res = run_fwd(pad(tokens), pad(cotangent), pack, token_valid, w_qkv, w_out, w_up, w_down, seq)
    weights, acts, (cot, act, vec) = res[:4], res[4:12], res[12:]
    gqkv, gout, gup, gdown, gsmall, gtok = run_bwd(
        cot, vec, token_valid, image_valid[:, None], weights, acts, seq
    )
    blocks = lax.axis_size("rep") // 8
    if blocks > 1:
        groups = [[i + 8 * b for b in range(blocks)] for i in range(8)]
        gqkv, gout, gup, gdown, gsmall = (
            lax.psum(g, "rep", axis_index_groups=groups) for g in (gqkv, gout, gup, gdown, gsmall)
        )
    gsmall = lax.dynamic_slice_in_dim(gsmall, grp * (d // 4), d // 4, 1).astype(F32).reshape(layers, SMALL, d // 4)
    outs, at = [], 0
    for w in smalls:
        take = w.shape[1] // (d // 4)
        outs.append(gsmall[:, at:at + take].reshape(layers, -1))
        at += take
    gg1, gb1, gbout, gg2, gb2, gbdown, gbqv, gbup = outs
    return (
        act[:, :seq], gtok[:, :seq], gg1, gb1, gqkv.astype(F32), gbqv, gout.astype(F32), gbout, gg2, gb2,
        gup.astype(F32), gbup, gdown.astype(F32), gbdown,
    )


def solution(mesh):
    rows3, mat, vec = P("rep", "grp", None), P(None, "grp", None), P(None, "grp")
    weights = (vec, vec, mat, vec, mat, vec, vec, vec, mat, vec, mat, vec)
    return jax.shard_map(
        local,
        mesh=mesh,
        in_specs=(rows3, rows3, P("rep"), P("rep", None)) + weights,
        out_specs=(rows3, rows3) + weights,
        check_vma=False,
    )
```

```python
import functools

import jax
import jax.numpy as jnp
from jax import lax
from jax.experimental import pallas as pl
from jax.experimental.pallas import tpu as pltpu
from jax.sharding import PartitionSpec as P

HEAD = 64
MESH = pl.DeviceIdType.MESH
F32 = jnp.float32
BF16 = jnp.bfloat16
VMEM_LIMIT = 62 * 2**20
WIDE = 256
STEP = 16
G1, B1, BOUT, G2, B2, BDOWN, BQV, BUP = 0, 1, 2, 3, 4, 5, 6, 8
SMALL = 16
WIDER = ("down",)


def nn(a, b):
    return lax.dot_general(a, b, (((1,), (0,)), ((), ())), preferred_element_type=F32)


def nt(a, b):
    return lax.dot_general(a, b, (((1,), (1,)), ((), ())), preferred_element_type=F32)


def tn(a, b):
    return lax.dot_general(a, b, (((0,), (0,)), ((), ())), preferred_element_type=F32)


def span(start, size):
    return pl.ds(pl.multiple_of(start, size), size)


def cols(j, width=WIDE):
    return span(j * width, width)


def loop(count, body):
    def step(j, carry):
        body(j)
        return carry

    lax.fori_loop(0, count, step, 0)


class Place:
    def __init__(self):
        self.rep, self.grp = lax.axis_index("rep"), lax.axis_index("grp")
        rep, grp = self.rep, self.grp
        self.x, self.c = grp // 2, grp % 2
        self.y, self.z = rep % 2, (rep // 2) % 4
        self.zlow = self.z % 2
        core, chip = 1 - 2 * self.c, 2 - 4 * self.x
        self.sib = (rep, grp + core)
        self.xn = (rep, grp + chip)
        self.xd = (rep, grp + chip + core)
        yrep = rep + 1 - 2 * self.y
        self.yn = (yrep, grp)
        self.yd = (yrep, grp + core)
        self.zn = (rep + 2 - 4 * self.zlow, grp)
        self.inner = jnp.logical_or(self.z == 1, self.z == 2)
        self.outer = jnp.logical_not(self.inner)
        self.mid = (rep + 6 - 4 * self.z, grp)


def greet(peers):
    barrier = pltpu.get_barrier_semaphore()
    for peer in peers:
        pl.semaphore_signal(barrier, inc=1, device_id=peer, device_id_type=MESH)
    pl.semaphore_wait(barrier, len(peers))


def remote(src, dst, send, recv, peer):
    return pltpu.make_async_remote_copy(
        src_ref=src, dst_ref=dst, send_sem=send, recv_sem=recv, device_id=peer, device_id_type=MESH
    )


def settle(ref, sem):
    pltpu.make_async_copy(ref, ref, sem).wait()


def norm_rows(v):
    mean = jnp.mean(v, axis=-1, keepdims=True)
    off = v - mean
    rstd = lax.rsqrt(jnp.mean(off * off, axis=-1, keepdims=True) + 1e-6)
    return off * rstd, rstd


def scores_t(k2, qa, mask):
    st = jnp.where(mask, nt(k2, qa), -1e9)
    top = jnp.max(st, axis=0, keepdims=True)
    e = jnp.exp(st - top)
    return e * (1.0 / jnp.sum(e, axis=0, keepdims=True))


def half_lanes(v, a):
    lane = lax.broadcasted_iota(jnp.int32, v.shape, 1)
    return jnp.where((lane >= HEAD) == (a == 1), v, jnp.zeros_like(v))


def chip_flags(at, tv_ref, rows, seq):
    lengths = jnp.sum(tv_ref[...], axis=1, keepdims=True)
    length = jnp.where(at.x == 0, lengths[0:1, :], lengths[1:2, :])
    row = lax.broadcasted_iota(jnp.int32, (2 * rows, 1), 0)
    core = jnp.where(row < rows, at.c, 1 - at.c)
    row = jnp.where(row < rows, row, row - rows)
    block = rows // 2
    chip = jnp.where(row < block, at.x, 1 - at.x)
    row = jnp.where(row < block, row, row - block)
    slot = (2 * chip + core) * seq + row
    return jnp.logical_and(row < seq, slot < length)


class Plan:
    def __init__(self):
        self.now, self.events, self.done = 0.0, [], set()

    def add(self, when, name, action):
        self.events.append((when, name, action))

    def order(self):
        self.events.sort(key=lambda e: e[0])

    def poll(self):
        while self.events and self.events[0][0] <= self.now:
            self.fire()

    def fire(self):
        when, name, action = self.events.pop(0)
        self.now = max(self.now, when)
        action()
        self.done.add(name)

    def need(self, name):
        while name not in self.done:
            self.fire()

    def spend(self, us):
        self.now += us
        self.poll()


KINDS = ("qkv", "out", "up", "down")


def fwd_kernel(
    seq, tok_ref, cot_ref, g1_in, b1_in, bo_in, g2_in, b2_in, bd_in, bqv_in, bup_in, tv_ref, iv_ref, wqkv_in, wout_in, wup_in, wdown_in,
    vqkv, vout, vup, vdown, xs, x2s, h1s, qkvs, as_, h2s, zs, gps, dm_out, act_out, vec_out,
    wqkv, wout, wup, wdown, x_ref, x2_ref, h1, qkv, att, h2, z, gp, put, got, tok, vec, bup, cot, dm, pack_ref,
    s_rx, s_ry, s_rz, s_ra, s_rb, s_rs, s_loc, s_send, s_core, r_core, s_save, s_misc, r_misc,
):
    at = Place()
    layers = vqkv.shape[0]
    rows, d = x_ref.shape
    block = rows // 2
    hc, f = att.shape[1], z.shape[1]
    own, other = pl.ds(0, rows), pl.ds(rows, rows)
    x, c = at.x, at.c
    quarter = at.y * 2 + at.zlow
    ins = dict(qkv=wqkv_in, out=wout_in, up=wup_in, down=wdown_in)
    full = dict(qkv=wqkv, out=wout, up=wup, down=wdown)
    saves = dict(qkv=vqkv, out=vout, up=vup, down=vdown)
    runs = dict(qkv=(d // 4, 6), up=(f // 2, 2))
    plan = Plan()
    index = {}
    for l in range(layers):
        for kind in KINDS:
            index[l, kind] = len(index)

    at_row = 0
    for ref in (g1_in, b1_in, bo_in, g2_in, b2_in, bd_in, bqv_in, bup_in):
        values = ref[...].astype(F32)
        for j in range(ref.shape[1] // WIDE):
            for l in range(layers):
                pack_ref[l * SMALL + at_row:l * SMALL + at_row + 1, :] = values[l:l + 1, j * WIDE:(j + 1) * WIDE]
            at_row += 1
    for l in range(layers):
        pack_ref[l * SMALL + at_row:(l + 1) * SMALL, :] = jnp.zeros((SMALL - at_row, WIDE), F32)
    greet((at.sib, at.xn, at.xd, at.yn, at.zn))

    here = vec.at[:, span(at.grp * WIDE, WIDE)]
    packs = [
        pltpu.make_async_copy(pack_ref, here, s_misc.at[4]),
        remote(pack_ref, here, s_misc.at[5], r_misc.at[5], at.sib),
        remote(pack_ref, here, s_misc.at[6], r_misc.at[6], at.xn),
        remote(pack_ref, here, s_misc.at[7], r_misc.at[7], at.xd),
    ]
    for copy in packs:
        copy.start()

    def wider_parts(kind, y=at.y, zlow=at.zlow):
        q = full[kind].shape[2] // 4
        return span(y * q, q), span((2 + zlow) * q, q)

    def launch(l, kind):
        i = index[l, kind]
        src, dst = ins[kind].at[l], full[kind].at[l]
        n = src.shape[0]
        q = n // 4
        part = span(quarter * q, q)
        if kind in runs:
            width, count = runs[kind]
            mine = 2 * x + c
            for j in range(count):
                to = pl.ds(j * width, width)
                keep = span((2 * j + c) * width, width)
                give = span((2 * j + 1 - c) * width, width)
                remote(src.at[part, keep], dst.at[mine, part, to], s_send.at[i], s_rx.at[i], at.xn).start()
                remote(src.at[part, give], dst.at[mine, part, to], s_send.at[i], s_rx.at[i], at.xd).start()
            for j in range(count):
                to = pl.ds(j * width, width)
                keep = span((2 * j + c) * width, width)
                give = span((2 * j + 1 - c) * width, width)
                remote(src.at[:, give], dst.at[mine, :, to], s_send.at[i], s_rs.at[i], at.sib).start()
                pltpu.make_async_copy(src.at[:, keep], dst.at[mine, :, to], s_loc.at[i]).start()
        else:
            for part in wider_parts(kind) if kind in WIDER else (part,):
                remote(src.at[part], dst.at[x, part], s_send.at[i], s_rx.at[i], at.xn).start()
            pltpu.make_async_copy(src, dst.at[x], s_loc.at[i]).start()

    def theirs(l, kind, part):
        dst = full[kind].at[l]
        if kind in runs:
            return dst.at[span(2 * (1 - x), 2), part]
        return dst.at[pl.ds(1 - x, 1), part]

    def part_of(kind, y, zlow, half=None):
        q = full[kind].shape[2] // 4
        if half is None:
            return span((2 * y + zlow) * q, q)
        return span((4 * y + 2 * zlow + half) * (q // 2), q // 2)

    def relay1(l, kind):
        i = index[l, kind]
        if kind in WIDER:
            settle(theirs(l, kind, pl.ds(0, full[kind].shape[2] // 2)), s_rx.at[i])
            by_y, by_z = (theirs(l, kind, part) for part in wider_parts(kind))
            remote(by_y, by_y, s_send.at[i], s_ry.at[i], at.yn).start()
            remote(by_z, by_z, s_send.at[i], s_rz.at[i], at.zn).start()
            return
        piece = theirs(l, kind, part_of(kind, at.y, at.zlow))
        settle(piece, s_rx.at[i])
        remote(piece, piece, s_send.at[i], s_ry.at[i], at.yn).start()
        remote(piece, piece, s_send.at[i], s_rz.at[i], at.zn).start()

    def relay2(l, kind):
        i = index[l, kind]
        settle(theirs(l, kind, part_of(kind, 1 - at.y, at.zlow)), s_ry.at[i])
        piece = theirs(l, kind, part_of(kind, 1 - at.y, at.zlow, 0))
        remote(piece, piece, s_send.at[i], s_ra.at[i], at.zn).start()
        settle(theirs(l, kind, part_of(kind, at.y, 1 - at.zlow)), s_rz.at[i])
        piece = theirs(l, kind, part_of(kind, at.y, 1 - at.zlow, 1))
        remote(piece, piece, s_send.at[i], s_rb.at[i], at.yn).start()

    def ready(l, kind):
        i = index[l, kind]
        if kind in WIDER:
            by_y, by_z = (theirs(l, kind, part) for part in wider_parts(kind, 1 - at.y, 1 - at.zlow))
            settle(by_y, s_ry.at[i])
            settle(by_z, s_rz.at[i])
        else:
            settle(theirs(l, kind, part_of(kind, 1 - at.y, 1 - at.zlow, 0)), s_ra.at[i])
            settle(theirs(l, kind, part_of(kind, 1 - at.y, 1 - at.zlow, 1)), s_rb.at[i])
        if kind in runs:
            settle(full[kind].at[l, 0], s_rs.at[i])
        settle(full[kind].at[l, 0], s_loc.at[i])
        pltpu.make_async_copy(full[kind].at[l], saves[kind].at[l], s_loc.at[i]).start()

    line = list(index)
    tokens = [
        remote(tok_ref.at[1 - x], tok.at[1], s_misc.at[0], r_misc.at[0], at.xn),
        pltpu.make_async_copy(tok_ref.at[x], tok.at[0], s_misc.at[3]),
    ]
    x_time, yz_time = 4.0, 0.0
    for n, (l, kind) in enumerate(line):
        if n == 2:
            for copy in tokens:
                copy.start()
            x_time += 7.3
        launch(l, kind)
        mb = 2 * full[kind].shape[1] * full[kind].shape[2] * full[kind].shape[3] / 2**20
        hop = mb / 4 / 0.094 * 1.05
        x_time += 2 * hop if kind in WIDER else hop
        plan.add(x_time + 1, ("r1", l, kind), functools.partial(relay1, l, kind))
        yz_time = max(yz_time, x_time + 1.5)
        if kind in WIDER:
            yz_time += hop
        else:
            plan.add(yz_time + hop + 1.5, ("r2", l, kind), functools.partial(relay2, l, kind))
            yz_time += 1.5 * hop
        plan.add(yz_time + 3, ("ok", l, kind), functools.partial(ready, l, kind))
    late = [
        remote(cot_ref.at[1 - x], cot.at[1], s_misc.at[1], r_misc.at[1], at.xn),
        pltpu.make_async_copy(cot_ref.at[x], cot.at[0], s_misc.at[8]),
    ]
    for copy in late:
        copy.start()
    mask = chip_flags(at, tv_ref, rows, seq)
    saved = []

    def seed():
        for copy in late:
            copy.wait()
        valid = jnp.where(x == 0, iv_ref[0:1, 0:1], iv_ref[0:1, 1:2]).astype(F32)
        weight = mask[:rows].astype(F32) * valid
        for i in range(2):
            for j in range(block // STEP):
                r = i * block + j * STEP
                dm[pl.ds(r, STEP), :] = (
                    cot[i, pl.ds(j * STEP, STEP), :].astype(F32) * weight[r:r + STEP, :]
                ).astype(BF16)
        copy = remote(dm.at[own], dm.at[other], s_misc.at[2], r_misc.at[2], at.sib)
        copy.start()
        saved.append(copy)

    def seeded():
        saved[0].wait()
        copy = pltpu.make_async_copy(dm, dm_out, s_misc.at[10])
        copy.start()
        saved.append(copy)

    plan.add(x_time + 9, "seed", seed)
    plan.add(x_time + 14, "seeded", seeded)
    plan.order()

    for copy in packs:
        copy.wait()
    vec_save = pltpu.make_async_copy(vec, vec_out, s_misc.at[9])
    vec_save.start()
    for l in range(layers):
        for j in range(f // WIDE):
            half, sub = divmod(j, f // WIDE // 2)
            bup[l:l + 1, pl.ds(j * WIDE, WIDE)] = vec[
                l * SMALL + BUP + sub:l * SMALL + BUP + sub + 1, span((2 * half + c) * WIDE, WIDE)
            ]
    plan.now = 18.0
    plan.poll()
    for copy in tokens:
        copy.wait()
    for i in range(2):
        for j in range(block // STEP):
            x_ref[pl.ds(i * block + j * STEP, STEP), :] = tok[i, pl.ds(j * STEP, STEP), :].astype(F32)
    plan.spend(1)

    def save(src, dst, slot):
        copy = pltpu.make_async_copy(src, dst, s_save.at[slot])
        copy.start()
        return copy

    pending = {}
    for l in range(layers):
        def row(name, l=l):
            return vec[l * SMALL + name:l * SMALL + name + 1, :]

        def norm_out(src_ref, dst_ref, gain, shift, l=l):
            for i in range(rows // STEP):
                r = pl.ds(i * STEP, STEP)
                hat, _ = norm_rows(src_ref[r, :])
                dst_ref[r, :] = (hat * row(gain) + row(shift)).astype(BF16)

        def weight(kind, cs, l=l):
            w = full[kind][l, :, :, cs]
            return w.reshape(w.shape[0] * w.shape[1], w.shape[2])

        norm_out(x_ref, h1, G1, B1)
        cp = remote(h1.at[own], h1.at[other], s_core.at[0], r_core.at[0], at.sib)
        cp.start()
        x_saved = save(x_ref, xs.at[l], 0)
        plan.spend(2)
        plan.need(("ok", l, "qkv"))
        if l:
            pending["qkv"].wait()
        bq = jnp.where(c == 0, row(BQV), vec[l * SMALL + BQV + 1:l * SMALL + BQV + 2, :])
        scale = HEAD ** -0.5
        parts = (
            (0, bq[:, :hc] * scale, scale), (hc, jnp.zeros((1, hc), F32), 1.0), (2 * hc, bq[:, hc:], 1.0)
        )

        def qkv_rows(r, l=l, parts=parts):
            for base, bias, factor in parts:
                for j in range(hc // WIDE):
                    cs = pl.ds(base + j * WIDE, WIDE)
                    out = nn(h1[r, :], weight("qkv", cs))
                    qkv[r, cs] = (out * factor + bias[:, j * WIDE:(j + 1) * WIDE]).astype(BF16)
                    plan.spend(0.35)

        qkv_rows(own)
        cp.wait()
        qkv_rows(other)
        h1_saved = save(h1, h1s.at[l], 1)
        pending["qkv"] = save(qkv, qkvs.at[l], 2)
        if l:
            pending["att"].wait()
        for p in range(hc // 128):
            q2 = qkv[:, p * 128:(p + 1) * 128]
            k2 = qkv[:, hc + p * 128:hc + (p + 1) * 128]
            v2 = qkv[:, 2 * hc + p * 128:2 * hc + (p + 1) * 128]
            vt = v2.T
            outs = []
            for a in range(2):
                pt = scores_t(k2, half_lanes(q2, a), mask)
                outs.append(nn(vt[a * HEAD:(a + 1) * HEAD, :], pt.astype(BF16)))
                plan.spend(1.4)
            att[:, p * 128:(p + 1) * 128] = jnp.concatenate(outs, axis=0).T.astype(BF16)
        pending["att"] = save(att, as_.at[l], 3)

        def exchange(left, kind, base, bias, out, slot):
            def far(j):
                put[:, cols(j)] = nn(left[other, :], weight(kind, cols(j))).astype(BF16)

            loop(d // WIDE, far)
            cp = remote(put, got.at[slot], s_core.at[1], r_core.at[1], at.sib)
            cp.start()
            plan.spend(1)

            def near(j):
                out[:, cols(j)] = nn(left[own, :], weight(kind, cols(j))) + base[:, cols(j)] + vec[
                    l * SMALL + bias:l * SMALL + bias + 1, cols(j)
                ]

            loop(d // WIDE, near)
            plan.spend(1)
            cp.wait()
            out[...] += got[slot].astype(F32)
            plan.spend(1)

        plan.need(("ok", l, "out"))
        if l:
            pending["x2"].wait()
        exchange(att, "out", x_ref, BOUT, x2_ref, 0)
        pending["x2"] = save(x2_ref, x2s.at[l], 4)
        norm_out(x2_ref, h2, G2, B2)
        cp = remote(h2.at[own], h2.at[other], s_core.at[2], r_core.at[2], at.sib)
        cp.start()
        plan.spend(2)
        plan.need(("ok", l, "up"))
        if l:
            pending["z"].wait()
            pending["gp"].wait()

        def up_rows(r):
            def body(j):
                u = nn(h2[r, :], weight("up", cols(j))) + bup[l:l + 1, cols(j)]
                phi = 0.5 + 0.5 * lax.erf(u * 0.7071067811865476)
                z[r, cols(j)] = (u * phi).astype(BF16)
                gp[r, cols(j)] = (phi + u * jnp.exp(u * u * -0.5) * 0.3989422804014327).astype(BF16)

            for part in range(2):
                loop(f // WIDE // 2, lambda j: body(j + part * (f // WIDE // 2)))
                plan.spend(1.9)

        up_rows(own)
        cp.wait()
        up_rows(other)
        h2_saved = save(h2, h2s.at[l], 5)
        pending["z"] = save(z, zs.at[l], 6)
        pending["gp"] = save(gp, gps.at[l], 7)
        plan.need(("ok", l, "down"))
        for copy in (x_saved, h1_saved, h2_saved):
            copy.wait()
        exchange(z, "down", x2_ref, BDOWN, x_ref, 1)

    for i in range(2):
        for j in range(block // STEP):
            tok[i, pl.ds(j * STEP, STEP), :] = x_ref[pl.ds(i * block + j * STEP, STEP), :].astype(BF16)
    act = pltpu.make_async_copy(tok, act_out, s_misc.at[11])
    act.start()
    while plan.events:
        plan.fire()
    for copy in (act, vec_save, saved[1]):
        copy.wait()
    for name in ("qkv", "att", "x2", "z", "gp"):
        pending[name].wait()
    for (l, kind), i in index.items():
        settle(full[kind].at[l, pl.ds(0, 3 if kind in runs else 1)], s_send.at[i])
        settle(full[kind].at[l], s_loc.at[i])


ANY = pl.BlockSpec(memory_space=pl.ANY)
VM = pl.BlockSpec(memory_space=pltpu.VMEM)


def dma(*shape):
    return pltpu.SemaphoreType.DMA(shape)


def run_fwd(tok, cot, smalls, tv, iv, w_qkv, w_out, w_up, w_down, seq):
    layers, n, d3 = w_qkv.shape
    d = d3 // 3
    hc, f = d // 2, 2 * w_down.shape[1]
    block = tok.shape[1]
    rows, both = 2 * block, 4 * block
    weights = [(4, n, 3 * hc), (2, n, d), (4, n, f), (2, w_down.shape[1], d)]
    acts = [
        ((rows, d), F32), ((rows, d), F32), ((both, d), BF16), ((both, 3 * hc), BF16),
        ((both, hc), BF16), ((both, d), BF16), ((both, f), BF16), ((both, f), BF16),
    ]
    shapes = [((layers, *s), BF16) for s in weights] + [((layers, *s), t) for s, t in acts]
    shapes += [((both, d), BF16), ((2, block, d), BF16), ((layers * SMALL, d), F32)]
    count = layers * len(KINDS)
    return pl.pallas_call(
        functools.partial(fwd_kernel, seq),
        out_shape=[jax.ShapeDtypeStruct(s, t) for s, t in shapes],
        in_specs=[ANY, ANY] + [VM] * 10 + [ANY] * 4,
        out_specs=[ANY] * len(shapes),
        scratch_shapes=[pltpu.VMEM((layers, *s), BF16) for s in weights]
        + [pltpu.VMEM(s, t) for s, t in acts]
        + [
            pltpu.VMEM((rows, d), BF16), pltpu.VMEM((2, rows, d), BF16),
            pltpu.VMEM((2, block, d), BF16), pltpu.VMEM((layers * SMALL, d), F32), pltpu.VMEM((8, f), F32),
            pltpu.VMEM((2, block, d), BF16), pltpu.VMEM((both, d), BF16), pltpu.VMEM((layers * SMALL, WIDE), F32),
        ]
        + [dma(count)] * 8
        + [dma(3), dma(3), dma(8), dma(12), dma(8)],
        compiler_params=pltpu.CompilerParams(
            collective_id=1, has_side_effects=True, vmem_limit_bytes=VMEM_LIMIT
        ),
        cost_estimate=pl.CostEstimate(flops=17 * 10**9, bytes_accessed=80 * 10**6, transcendentals=0),
        name="forward",
    )(tok, cot, *smalls, tv, iv, w_qkv, w_out, w_up, w_down)


NS, NY, NZ, NT = 6, 3, 4, 6
CHUNK = 256


def chunks_of(layers):
    chunks = []
    for l in reversed(range(layers)):
        chunks += [("down", l, i) for i in range(4)] + [("up", l, i) for i in range(4)]
        chunks += [("out", l, 0)] + [("qkv", l, i) for i in range(3)]
    return chunks + [("small", 0, 0)]


def units_of(chunks):
    units, first, last = [], [], []
    for k, (kind, l, i) in enumerate(chunks):
        pieces = {("qkv", 0, 1): (128, 128), ("qkv", 0, 2): (128, 64, 64), ("small", 0, 0): (64,)}
        start = 0
        first.append(len(units))
        for n in pieces.get((kind, l, i), (CHUNK,)):
            units.append((k, start, n))
            start += n
        last.append(len(units) - 1)
    return units, first, last


class Ring:
    def __init__(self, at, plan, chunks, outs, bufs, sems):
        self.at, self.plan, self.chunks, self.outs = at, plan, chunks, outs
        self.g, self.xr, self.yr, self.zr, self.wr, self.t = bufs
        (self.x_send, self.x_recv, self.y_send, self.y_recv, self.z_send, self.z_recv, self.w_send, self.w_recv,
         self.f_send, self.f_recv, self.cx, self.cy, self.cz, self.cw, self.cb) = sems
        self.units, self.first, self.last = units_of(chunks)
        self.count = len(self.units)
        self.x_free = 0.0
        self.copies, self.done, self.when = {}, set(), {}

    def size(self, u):
        return self.units[u][2]

    def reserve(self, k):
        if k >= NS:
            self.plan.now = max(self.plan.now, self.when[2, self.last[k - NS]])
            self.plan.poll()

    def launch(self, k):
        if k >= NS:
            pl.semaphore_wait(self.cx, 1)
        plan = self.plan
        for u in range(self.first[k], self.last[k] + 1):
            _, start, n = self.units[u]
            copy = remote(
                self.g.at[k % NS, 0, pl.ds(start, n)], self.xr.at[k % NS, pl.ds(start, n)],
                self.x_send.at[u], self.x_recv.at[u], self.at.xn,
            )
            copy.start()
            self.copies["x", u] = copy
            part = n / CHUNK
            self.x_free = max(plan.now, self.x_free) + 11.3 * part
            t = self.x_free + 1.5
            for i, lag in enumerate((0, 8 * part + 1.5, *[6 * part + 2] * 3, 11 * part + 2)):
                t += lag
                self.when[i + 1, u] = t
                plan.add(t, (i + 1, u), functools.partial(self.run, i + 1, u))
        plan.order()

    def run(self, stage, u):
        if u < 0 or (stage, u) in self.done:
            return
        self.done.add((stage, u))
        if stage > 1:
            self.run(stage - 1, u)
        self.run(stage, u - 1)
        free = {1: ((2, NY),), 2: ((3, NZ), (6, NT)), 3: ((4, NZ),), 4: ((5, NZ),)}
        for other, slots in free.get(stage, ()):
            self.run(other, u - slots)
        (self.s1, self.s2, self.s3, self.s4, self.s5, self.s6)[stage - 1](u)

    def credit(self, sem, u, slots, peer):
        if u + slots < self.count:
            pl.semaphore_signal(sem, inc=1, device_id=peer, device_id_type=MESH)

    def claim(self, sem, u, slots):
        if u >= slots:
            pl.semaphore_wait(sem, 1)

    def add(self, dst, src, count, base=None, base_at=None):
        def body(j):
            r = cols(j, 32)
            b = dst[r, :] if base is None else base[pl.ds(pl.multiple_of(base_at + j * 32, 32), 32), :]
            dst[r, :] = (b.astype(F32) + src[r, :].astype(F32)).astype(BF16)

        loop(count // 32, body)

    def s1(self, u):
        at = self.at
        k, start, n = self.units[u]
        slot = k % NS
        self.copies["x", u].wait()
        self.add(self.g.at[slot, 1, pl.ds(start, n)], self.xr.at[slot, pl.ds(start, n)], n)
        if u == self.last[k] and k + NS < len(self.chunks):
            pl.semaphore_signal(self.cx, inc=1, device_id=at.xn, device_id_type=MESH)
        self.claim(self.cy, u, NY)
        copy = remote(
            self.g.at[slot, 1, span(start + (1 - at.y) * (n // 2), n // 2)], self.yr.at[u % NY, pl.ds(0, n // 2)],
            self.y_send.at[u], self.y_recv.at[u % NY], at.yn,
        )
        copy.start()
        self.copies["y", u] = copy

    def part(self, ref, u, slots):
        return ref.at[u % slots, pl.ds(0, self.size(u) // 2)]

    def s2(self, u):
        at = self.at
        k, start, n = self.units[u]
        t = self.part(self.t, u, NT)
        self.copies["y", u].wait()
        self.add(t, self.part(self.yr, u, NY), n // 2, self.g.at[k % NS, 1], start + at.y * (n // 2))
        self.credit(self.cy, u, NY, at.yn)

        @pl.when(at.outer)
        def _():
            self.claim(self.cz, u, NZ)
            remote(t, self.part(self.zr, u, NZ), self.z_send.at[u % NT], self.z_recv.at[u % NZ], at.zn).start()

    def s3(self, u):
        n, at = self.size(u), self.at
        t = self.part(self.t, u, NT)

        @pl.when(at.outer)
        def _():
            settle(t, self.z_send.at[u % NT])

        @pl.when(at.inner)
        def _():
            got = self.part(self.zr, u, NZ)
            settle(got, self.z_recv.at[u % NZ])
            self.add(t, got, n // 2)
            self.credit(self.cz, u, NZ, at.zn)
            self.claim(self.cw, u, NZ)
            remote(t, self.part(self.wr, u, NZ), self.z_send.at[u % NT], self.w_recv.at[u % NZ], at.mid).start()

    def s4(self, u):
        n, at = self.size(u), self.at

        @pl.when(at.inner)
        def _():
            t = self.part(self.t, u, NT)
            got = self.part(self.wr, u, NZ)
            settle(got, self.w_recv.at[u % NZ])
            settle(t, self.z_send.at[u % NT])
            self.add(t, got, n // 2)
            self.credit(self.cw, u, NZ, at.mid)
            self.claim(self.cb, u, NZ)
            remote(t, self.part(self.zr, u, NZ), self.w_send.at[u % NT], self.z_recv.at[u % NZ], at.zn).start()

    def s5(self, u):
        n, at = self.size(u), self.at
        t = self.part(self.t, u, NT)

        @pl.when(at.outer)
        def _():
            got = self.part(self.zr, u, NZ)
            settle(got, self.z_recv.at[u % NZ])

            def body(j):
                t[cols(j, 32), :] = got[cols(j, 32), :]

            loop(n // 64, body)
            self.credit(self.cb, u, NZ, at.zn)

        k, start, n = self.units[u]
        kind, l, i = self.chunks[k]
        out = self.outs[kind]
        sent = self.f_send.at[u % NT]
        if kind == "small":
            pltpu.make_async_copy(t, out, sent).start()
            return
        half = n // 2
        width = t.shape[1]

        def deliver(src, dst, mine, kind_index):
            if mine:
                pltpu.make_async_copy(src, dst, sent).start()
                remote(src, dst, sent, self.f_recv.at[kind_index], at.yn).start()
            else:
                remote(src, dst, sent, self.f_recv.at[kind_index], at.sib).start()
                remote(src, dst, sent, self.f_recv.at[kind_index], at.yd).start()

        if kind in ("down", "out"):
            deliver(t, out.at[l, span(i * CHUNK + start + at.y * half, half)], True, KINDS.index(kind))
        elif kind == "up":
            side, run = divmod(i, 2)
            deliver(t, out.at[l, span(start + at.y * half, half), span((2 * run + at.c) * width, width)], side == 0, 2)
        else:
            for side in range(2):
                for run in range(2):
                    src = t.at[:, pl.ds((2 * side + run) * WIDE, WIDE)]
                    dst = out.at[l, span(start + at.y * half, half), span(i * width + (2 * run + at.c) * WIDE, WIDE)]
                    deliver(src, dst, side == 0, 0)

    def s6(self, u):
        at = self.at
        t = self.part(self.t, u, NT)
        k, _, n = self.units[u]
        settle(t if self.chunks[k][0] == "small" else self.g.at[0, 0, pl.ds(0, n)], self.f_send.at[u % NT])

        @pl.when(at.inner)
        def _():
            settle(t, self.w_send.at[u % NT])

    def finish(self):
        while self.plan.events:
            self.plan.fire()
        for i, kind in enumerate(KINDS):
            out = self.outs[kind]
            rows = out.shape[1]
            settle(out.at[:, pl.ds(0, rows // 2 if kind in ("out", "down") else rows * 3 // 4)], self.f_recv.at[i])


def bwd_kernel(
    seq, dm_ref, act_ref, vec_ref, tv_ref, vqkv, vout, vup, vdown, xs, x2s, h1s, qkvs, as_, h2s, zs, gps,
    oqkv, oout, oup, odown, osmall, otok, oact,
    wqkv, wout, wup, wdown, x_ref, x2_ref, h1, qkv, att, h2, z, gp,
    tok, g_ref, dm, da, dj, dx2, dh, put, got, small, small_put, small_got, ring_g, ring_x, ring_y, ring_z, ring_w, ring_t,
    s_load, s_core, r_core, s_misc, r_misc, *ring_sems,
):
    at = Place()
    layers = vqkv.shape[0]
    rows, d = x_ref.shape
    block = rows // 2
    hc, f = att.shape[1], z.shape[1]
    own, other = pl.ds(0, rows), pl.ds(rows, rows)
    x, c = at.x, at.c
    plan = Plan()
    chunks = chunks_of(layers)
    ring = Ring(
        at, plan, chunks, dict(qkv=oqkv, out=oout, up=oup, down=odown, small=osmall),
        (ring_g, ring_x, ring_y, ring_z, ring_w, ring_t), ring_sems,
    )
    number = {chunk: u for u, chunk in enumerate(chunks)}

    stores = dict(
        z=(zs, z), wdown=(vdown, wdown), gp=(gps, gp), h2=(h2s, h2), wup=(vup, wup), x2=(x2s, x2_ref),
        wout=(vout, wout), att=(as_, att), qkv=(qkvs, qkv), wqkv=(vqkv, wqkv), h1=(h1s, h1), x=(xs, x_ref),
    )
    slots = {name: i for i, name in enumerate(stores)}
    loads = {}

    def load(name, l):
        if l < 0:
            return
        src, dst = stores[name]
        loads[name, l] = pltpu.make_async_copy(src.at[l], dst, s_load.at[slots[name]])
        loads[name, l].start()

    dm_load = pltpu.make_async_copy(dm_ref, dm.at[0], s_misc.at[0])
    dm_load.start()
    for name in stores:
        load(name, layers - 1)
    greet((at.sib, at.xn, at.yn, at.yd, at.zn, at.mid))

    def by_half(hh):
        return hh * x + (1 - hh) * (1 - x)

    mask = chip_flags(at, tv_ref, rows, seq)
    small[...] = jnp.zeros_like(small)
    act = [
        remote(act_ref.at[1], oact.at[x], s_misc.at[4], r_misc.at[4], at.xn),
        pltpu.make_async_copy(act_ref.at[0], oact.at[x], s_misc.at[5]),
    ]
    for l in reversed(range(layers)):
        def row(name, l=l):
            return vec_ref[l * SMALL + name:l * SMALL + name + 1, :]

        def set_small(name, value, l=l):
            small[l * SMALL + name:l * SMALL + name + 1, :] = value

        def round_rows(src_ref, name, slot):
            total = jnp.zeros((8, d), F32)
            for i in range(rows // STEP):
                r = pl.ds(i * STEP, STEP)
                if src_ref is None:
                    low = dm[slot, r, :].astype(F32)
                    g_ref[r, :] = low
                else:
                    low = src_ref[r, :].astype(BF16)
                    dm[slot, r, :] = low
                    low = low.astype(F32)
                total = total + low[0:8, :] + low[8:16, :]
            set_small(name, jnp.sum(total, axis=0, keepdims=True))

        def send_round(src_ref, name, slot):
            round_rows(src_ref, name, slot)
            copy = remote(dm.at[slot, own], dm.at[slot, other], s_core.at[slot], r_core.at[slot], at.sib)
            copy.start()
            return copy

        def exchange(left, w):
            per = w.shape[1]

            def piece(j):
                b = j // (per // WIDE)
                return w[b, span((j % (per // WIDE)) * WIDE, WIDE), :]

            def far(j):
                put[:, cols(j)] = nt(left[other, :], piece(j)).astype(BF16)

            loop(d // WIDE, far)
            plan.spend(1.5)
            copy = remote(put, got, s_core.at[2], r_core.at[2], at.sib)
            copy.start()

            def near(j):
                dh[:, cols(j)] = nt(left[own, :], piece(j))

            loop(d // WIDE, near)
            plan.spend(1.5)
            copy.wait()
            plan.spend(0.5)

        def norm_back(value_ref, base_ref, out_ref, gain, shift):
            total_g = jnp.zeros((8, d), F32)
            total_b = jnp.zeros((8, d), F32)
            for i in range(rows // STEP):
                r = pl.ds(i * STEP, STEP)
                hat, rstd = norm_rows(value_ref[r, :])
                grad = dh[r, :] + got[r, :].astype(F32)
                prod = grad * hat
                total_g = total_g + prod[0:8, :] + prod[8:16, :]
                total_b = total_b + grad[0:8, :] + grad[8:16, :]
                dhat = grad * row(gain)
                m1 = jnp.mean(dhat, axis=-1, keepdims=True)
                m2 = jnp.mean(dhat * hat, axis=-1, keepdims=True)
                out_ref[r, :] = base_ref[r, :] + rstd * (dhat - m1 - hat * m2)
            set_small(gain, jnp.sum(total_g, axis=0, keepdims=True))
            set_small(shift, jnp.sum(total_b, axis=0, keepdims=True))

        def produce(chunk, maker, us):
            u = number[chunk]
            ring.reserve(u)
            loop(2, lambda hh: maker(ring_g.at[u % NS, hh], by_half(hh)))
            ring.launch(u)
            plan.spend(us)

        if l == layers - 1:
            dm_load.wait()
            loads["z", l].wait()
        else:
            copy = send_round(g_ref, BDOWN, 0)
            loads["z", l].wait()
            plan.spend(2)
            copy.wait()
        for i in range(4):
            def make(dst, h, i=i):
                dst[...] = tn(z[:, span(h * (f // 2) + i * CHUNK, CHUNK)], dm[0]).astype(BF16)

            produce(("down", l, i), make, 1.3)
        if l == layers - 1:
            round_rows(None, BDOWN, 0)
            for copy in act:
                copy.start()
        load("z", l - 1)
        loads["wdown", l].wait()
        loads["gp", l].wait()

        def dz_body(j):
            b = j // (f // 2 // WIDE)
            w = wdown[b, span((j % (f // 2 // WIDE)) * WIDE, WIDE), :]
            for r in (own, other):
                low = (nt(dm[0, r, :], w) * gp[r, cols(j)].astype(F32)).astype(BF16)
                gp[r, cols(j)] = low

        for part in range(2):
            loop(f // WIDE // 2, lambda j: dz_body(j + part * (f // WIDE // 2)))
            plan.spend(2)
        load("wdown", l - 1)
        for j in range(f // WIDE):
            half, sub = divmod(j, f // WIDE // 2)
            small[l * SMALL + BUP + sub:l * SMALL + BUP + sub + 1, span((2 * half + c) * WIDE, WIDE)] = jnp.sum(
                gp[:, j * WIDE:(j + 1) * WIDE].astype(F32), axis=0, keepdims=True
            )
        loads["h2", l].wait()
        loads["wup", l].wait()
        for i in range(4):
            side, run = divmod(i, 2)

            def make(dst, h, side=side, run=run):
                rh = c if side == 0 else 1 - c
                left = h2[:, span(h * (d // 2) + rh * CHUNK, CHUNK)]
                dst[...] = tn(left, gp[:, run * (f // 2):(run + 1) * (f // 2)]).astype(BF16)

            if i == 2:
                exchange(gp, wup)
                load("wup", l - 1)
                loads["x2", l].wait()
                norm_back(x2_ref, g_ref, dx2, G2, B2)
                load("x2", l - 1)
                plan.spend(3)
                copy = send_round(dx2, BOUT, 1)
            produce(("up", l, i), make, 1.3)
        load("gp", l - 1)
        load("h2", l - 1)

        loads["wout", l].wait()
        loads["att", l].wait()
        copy.wait()
        for j in range(hc // WIDE):
            for r in (own, other):
                da[r, pl.ds(j * WIDE, WIDE)] = nt(dm[1, r, :], wout[j]).astype(BF16)
        load("wout", l - 1)

        def make(dst, h):
            dst[...] = tn(att[:, span(h * CHUNK, CHUNK)], dm[1]).astype(BF16)

        produce(("out", l, 0), make, 2)
        load("att", l - 1)
        loads["qkv", l].wait()
        sums = {}
        for p in range(hc // 128):
            cq, ck, cv = (pl.ds(k * hc + p * 128, 128) for k in range(3))
            q2, k2, v2, da2 = qkv[:, cq], qkv[:, ck], qkv[:, cv], da[:, cq]
            kt = k2.T
            dk = dv = None
            parts = []
            for a in range(2):
                qa, daa = half_lanes(q2, a), half_lanes(da2, a)
                pt = scores_t(k2, qa, mask)
                dpt = nt(v2, daa)
                delta = jnp.sum(dpt * pt, axis=0, keepdims=True)
                dst = (pt * (dpt - delta)).astype(BF16)
                dva = nn(pt.astype(BF16), daa)
                dka = nn(dst, qa)
                parts.append(nn(kt[a * HEAD:(a + 1) * HEAD, :], dst))
                dk = dka if dk is None else dk + dka
                dv = dva if dv is None else dv + dva
                plan.spend(2.7)
            dq = (jnp.concatenate(parts, axis=0).T * HEAD ** -0.5).astype(BF16)
            dv = dv.astype(BF16)
            dj[:, cq] = dq
            dj[:, ck] = dk.astype(BF16)
            dj[:, cv] = dv
            for k, value in ((0, dq), (1, dv)):
                total = jnp.sum(value.astype(F32), axis=0, keepdims=True)
                for core in range(2):
                    r = l * SMALL + BQV + core
                    small[r:r + 1, k * hc + p * 128:k * hc + (p + 1) * 128] = jnp.where(
                        c == core, total, jnp.zeros_like(total)
                    )
        load("qkv", l - 1)
        loads["wqkv", l].wait()
        loads["h1", l].wait()
        for i in range(3):
            def make(dst, h, i=i):
                for side in range(2):
                    rh = c if side == 0 else 1 - c
                    left = h1[:, span(h * (d // 2) + rh * CHUNK, CHUNK)]
                    dst[:, side * hc:(side + 1) * hc] = tn(left, dj[:, i * hc:(i + 1) * hc]).astype(BF16)

            if i == 1:
                exchange(dj, wqkv)
                load("wqkv", l - 1)
                loads["x", l].wait()
                norm_back(x_ref, dx2, g_ref, G1, B1)
                load("x", l - 1)
                plan.spend(3)
            produce(("qkv", l, i), make, 1.3)
        load("h1", l - 1)

    for i in range(2):
        for j in range(block // STEP):
            tok[i, pl.ds(j * STEP, STEP), :] = g_ref[pl.ds(i * block + j * STEP, STEP), :].astype(BF16)
    back = [
        remote(tok.at[1], otok.at[x], s_misc.at[1], r_misc.at[1], at.xn),
        pltpu.make_async_copy(tok.at[0], otok.at[x], s_misc.at[2]),
    ]
    small_put[...] = small[...].astype(BF16)
    copy = remote(small_put, small_got, s_misc.at[3], r_misc.at[3], at.sib)
    copy.start()
    copy.wait()
    total = (small_put[...].astype(F32) + small_got[...].astype(F32)).astype(BF16)
    u = number["small", 0, 0]
    ring.reserve(u)
    n = total.shape[0]
    for hh in range(2):
        for k in range(2):
            ring_g[u % NS, hh, k * n:(k + 1) * n, :] = total
    ring.launch(u)
    for copy in back:
        copy.start()
    ring.finish()
    for copy in (*back, *act):
        copy.wait()


def run_bwd(dm, act, vec, tv, weights, acts, seq):
    layers, _, n, hc3 = weights[0].shape
    d = acts[0].shape[2]
    rows = acts[0].shape[1]
    block, both = rows // 2, 2 * rows
    hc, f = hc3 // 3, weights[2].shape[3]
    units = len(units_of(chunks_of(layers))[0])
    outs = [(layers, n, 3 * d), (layers, n, d), (layers, n, 2 * f), (layers, f // 2, d), (layers * SMALL, d)]
    outs += [(2, block, d)] * 2
    args = (dm, act, vec, tv, *weights, *acts)
    return pl.pallas_call(
        functools.partial(bwd_kernel, seq),
        out_shape=[jax.ShapeDtypeStruct(s, BF16) for s in outs],
        in_specs=[ANY, ANY, VM, VM] + [ANY] * 12,
        out_specs=[ANY] * len(outs),
        scratch_shapes=[pltpu.VMEM(w.shape[1:], w.dtype) for w in (*weights, *acts)]
        + [
            pltpu.VMEM((2, block, d), BF16), pltpu.VMEM((rows, d), F32), pltpu.VMEM((2, both, d), BF16),
            pltpu.VMEM((both, hc), BF16), pltpu.VMEM((both, 3 * hc), BF16), pltpu.VMEM((rows, d), F32),
            pltpu.VMEM((rows, d), F32), pltpu.VMEM((rows, d), BF16), pltpu.VMEM((rows, d), BF16),
            pltpu.VMEM((layers * SMALL, d), F32), pltpu.VMEM((layers * SMALL, d), BF16),
            pltpu.VMEM((layers * SMALL, d), BF16),
            pltpu.VMEM((NS, 2, CHUNK, d), BF16), pltpu.VMEM((NS, CHUNK, d), BF16),
            pltpu.VMEM((NY, CHUNK // 2, d), BF16), pltpu.VMEM((NZ, CHUNK // 2, d), BF16),
            pltpu.VMEM((NZ, CHUNK // 2, d), BF16), pltpu.VMEM((NT, CHUNK // 2, d), BF16),
            dma(12), dma(3), dma(3), dma(6), dma(6),
            dma(units), dma(units), dma(units), dma(NY), dma(NT), dma(NZ), dma(NT), dma(NZ), dma(NT), dma(4),
        ]
        + [pltpu.SemaphoreType.REGULAR] * 5,
        compiler_params=pltpu.CompilerParams(
            collective_id=2, has_side_effects=True, vmem_limit_bytes=VMEM_LIMIT
        ),
        cost_estimate=pl.CostEstimate(flops=34 * 10**9, bytes_accessed=120 * 10**6, transcendentals=0),
        name="backward",
    )(*args)


def finish_kernel(gqkv, gout, gup, gdown, small, oqkv, oout, oup, odown, *vectors):
    for src, dst in ((gqkv, oqkv), (gout, oout), (gup, oup), (gdown, odown)):
        dst[...] = src[...].astype(F32)
    mine = span(lax.axis_index("grp") * WIDE, WIDE)
    layers = vectors[0].shape[0]
    rows = [small[l * SMALL:(l + 1) * SMALL, mine].astype(F32) for l in range(layers)]
    at = 0
    for out in vectors:
        for j in range(out.shape[1] // WIDE):
            for l in range(layers):
                out[l:l + 1, j * WIDE:(j + 1) * WIDE] = rows[l][at:at + 1, :]
            at += 1


def run_finish(gqkv, gout, gup, gdown, small, widths):
    bigs = (gqkv, gout, gup, gdown)
    layers = gqkv.shape[0]
    steps = 4

    def big(g):
        return pl.BlockSpec((1, g.shape[1] // steps, g.shape[2]), lambda l, s: (l, s, 0))

    def flat(shape):
        return pl.BlockSpec(shape, lambda l, s: (0, 0))

    vectors = [(layers, w) for w in widths]
    return pl.pallas_call(
        finish_kernel,
        grid=(layers, steps),
        out_shape=[jax.ShapeDtypeStruct(g.shape, F32) for g in bigs]
        + [jax.ShapeDtypeStruct(v, F32) for v in vectors],
        in_specs=[big(g) for g in bigs] + [flat(small.shape)],
        out_specs=[big(g) for g in bigs] + [flat(v) for v in vectors],
        compiler_params=pltpu.CompilerParams(vmem_limit_bytes=VMEM_LIMIT),
        name="finish",
    )(*bigs, small)


def local(
    tokens, cotangent, image_valid, token_valid,
    norm1_gain, norm1_bias, w_qkv, b_qv, w_out, b_out, norm2_gain, norm2_bias, w_up, b_up, w_down, b_down,
):
    seq = tokens.shape[1]
    block = -(-seq // 32) * 32

    def pad(value):
        return jnp.pad(value, ((0, 0), (0, block - seq), (0, 0)))

    smalls = (norm1_gain, norm1_bias, b_out, norm2_gain, norm2_bias, b_down, b_qv, b_up)
    res = run_fwd(
        pad(tokens), pad(cotangent), smalls, token_valid, image_valid[None, :], w_qkv, w_out, w_up, w_down, seq
    )
    weights, acts, (dm, act, vec) = res[:4], res[4:12], res[12:]
    gqkv, gout, gup, gdown, gsmall, gtok, act = run_bwd(dm, act, vec, token_valid, weights, acts, seq)
    blocks = lax.axis_size("rep") // 8
    if blocks > 1:
        groups = [[i + 8 * b for b in range(blocks)] for i in range(8)]
        gqkv, gout, gup, gdown, gsmall = (
            lax.psum(g, "rep", axis_index_groups=groups) for g in (gqkv, gout, gup, gdown, gsmall)
        )
    gqkv, gout, gup, gdown, *vectors = run_finish(gqkv, gout, gup, gdown, gsmall, [w.shape[1] for w in smalls])
    gg1, gb1, gbout, gg2, gb2, gbdown, gbqv, gbup = vectors
    return (
        act[:, :seq], gtok[:, :seq], gg1, gb1, gqkv, gbqv, gout, gbout, gg2, gb2, gup, gbup, gdown, gbdown,
    )


def solution(mesh):
    rows3, mat, vec = P("rep", "grp", None), P(None, "grp", None), P(None, "grp")
    weights = (vec, vec, mat, vec, mat, vec, vec, vec, mat, vec, mat, vec)
    return jax.shard_map(
        local,
        mesh=mesh,
        in_specs=(rows3, rows3, P("rep"), P("rep", None)) + weights,
        out_specs=(rows3, rows3) + weights,
        check_vma=False,
    )
```

```python
import functools

import jax
import jax.numpy as jnp
from jax import lax
from jax.experimental import pallas as pl
from jax.experimental.pallas import tpu as pltpu
from jax.sharding import PartitionSpec as P

HEAD = 64
MESH = pl.DeviceIdType.MESH
F32 = jnp.float32
BF16 = jnp.bfloat16
VMEM_LIMIT = 62 * 2**20
WIDE = 256
STEP = 16
G1, B1, BOUT, G2, B2, BDOWN, BQV, BUP = 0, 1, 2, 3, 4, 5, 6, 8
SMALL = 16
WIDER = ("down",)


def nn(a, b):
    return lax.dot_general(a, b, (((1,), (0,)), ((), ())), preferred_element_type=F32)


def nt(a, b):
    return lax.dot_general(a, b, (((1,), (1,)), ((), ())), preferred_element_type=F32)


def tn(a, b):
    return lax.dot_general(a, b, (((0,), (0,)), ((), ())), preferred_element_type=F32)


def span(start, size):
    return pl.ds(pl.multiple_of(start, size), size)


def cols(j, width=WIDE):
    return span(j * width, width)


def loop(count, body):
    def step(j, carry):
        body(j)
        return carry

    lax.fori_loop(0, count, step, 0)


class Place:
    def __init__(self):
        self.rep, self.grp = lax.axis_index("rep"), lax.axis_index("grp")
        rep, grp = self.rep, self.grp
        self.x, self.c = grp // 2, grp % 2
        self.y, self.z = rep % 2, (rep // 2) % 4
        self.zlow = self.z % 2
        core, chip = 1 - 2 * self.c, 2 - 4 * self.x
        self.sib = (rep, grp + core)
        self.xn = (rep, grp + chip)
        self.xd = (rep, grp + chip + core)
        yrep = rep + 1 - 2 * self.y
        self.yn = (yrep, grp)
        self.yd = (yrep, grp + core)
        self.zn = (rep + 2 - 4 * self.zlow, grp)
        self.inn = ((self.z + 1) // 2) % 2
        self.inner = self.inn == 1
        self.outer = self.inn == 0
        self.mid = (rep + 6 - 4 * self.z, grp)


def greet(peers):
    barrier = pltpu.get_barrier_semaphore()
    for peer in peers:
        pl.semaphore_signal(barrier, inc=1, device_id=peer, device_id_type=MESH)
    pl.semaphore_wait(barrier, len(peers))


def remote(src, dst, send, recv, peer):
    return pltpu.make_async_remote_copy(
        src_ref=src, dst_ref=dst, send_sem=send, recv_sem=recv, device_id=peer, device_id_type=MESH
    )


def settle(ref, sem):
    pltpu.make_async_copy(ref, ref, sem).wait()


def norm_rows(v):
    mean = jnp.mean(v, axis=-1, keepdims=True)
    off = v - mean
    rstd = lax.rsqrt(jnp.mean(off * off, axis=-1, keepdims=True) + 1e-6)
    return off * rstd, rstd


def scores_t(k2, qa, mask):
    st = jnp.where(mask, nt(k2, qa), -1e9)
    top = jnp.max(st, axis=0, keepdims=True)
    e = jnp.exp(st - top)
    return e * (1.0 / jnp.sum(e, axis=0, keepdims=True))


def half_lanes(v, a):
    lane = lax.broadcasted_iota(jnp.int32, v.shape, 1)
    return jnp.where((lane >= HEAD) == (a == 1), v, jnp.zeros_like(v))


def chip_flags(at, tv_ref, rows, seq):
    lengths = jnp.sum(tv_ref[...], axis=1, keepdims=True)
    length = jnp.where(at.x == 0, lengths[0:1, :], lengths[1:2, :])
    row = lax.broadcasted_iota(jnp.int32, (2 * rows, 1), 0)
    core = jnp.where(row < rows, at.c, 1 - at.c)
    row = jnp.where(row < rows, row, row - rows)
    block = rows // 2
    chip = jnp.where(row < block, at.x, 1 - at.x)
    row = jnp.where(row < block, row, row - block)
    slot = (2 * chip + core) * seq + row
    return jnp.logical_and(row < seq, slot < length)


class Plan:
    def __init__(self):
        self.now, self.events, self.done = 0.0, [], set()

    def add(self, when, name, action):
        self.events.append((when, name, action))

    def order(self):
        self.events.sort(key=lambda e: e[0])

    def poll(self):
        while self.events and self.events[0][0] <= self.now:
            self.fire()

    def fire(self):
        when, name, action = self.events.pop(0)
        self.now = max(self.now, when)
        action()
        self.done.add(name)

    def need(self, name):
        while name not in self.done:
            self.fire()

    def spend(self, us):
        self.now += us
        self.poll()


KINDS = ("qkv", "out", "up", "down")


def fwd_kernel(
    seq, tok_ref, cot_ref, g1_in, b1_in, bo_in, g2_in, b2_in, bd_in, bqv_in, bup_in, tv_ref, iv_ref, wqkv_in, wout_in, wup_in, wdown_in,
    vqkv, vout, vup, vdown, xs, x2s, h1s, qkvs, as_, h2s, zs, gps, dm_out, act_out, vec_out,
    wqkv, wout, wup, wdown, x_ref, x2_ref, h1, qkv, att, h2, z, gp, put, got, tok, vec, bup, cot, dm, pack_ref,
    s_rx, s_ry, s_rz, s_ra, s_rb, s_rs, s_loc, s_send, s_core, r_core, s_save, s_misc, r_misc,
):
    at = Place()
    layers = vqkv.shape[0]
    rows, d = x_ref.shape
    block = rows // 2
    hc, f = att.shape[1], z.shape[1]
    own, other = pl.ds(0, rows), pl.ds(rows, rows)
    x, c = at.x, at.c
    quarter = at.y * 2 + at.zlow
    ins = dict(qkv=wqkv_in, out=wout_in, up=wup_in, down=wdown_in)
    full = dict(qkv=wqkv, out=wout, up=wup, down=wdown)
    saves = dict(qkv=vqkv, out=vout, up=vup, down=vdown)
    runs = dict(qkv=(d // 4, 6), up=(f // 2, 2))
    plan = Plan()
    index = {}
    for l in range(layers):
        for kind in KINDS:
            index[l, kind] = len(index)

    at_row = 0
    for ref in (g1_in, b1_in, bo_in, g2_in, b2_in, bd_in, bqv_in, bup_in):
        values = ref[...].astype(F32)
        for j in range(ref.shape[1] // WIDE):
            for l in range(layers):
                pack_ref[l * SMALL + at_row:l * SMALL + at_row + 1, :] = values[l:l + 1, j * WIDE:(j + 1) * WIDE]
            at_row += 1
    for l in range(layers):
        pack_ref[l * SMALL + at_row:(l + 1) * SMALL, :] = jnp.zeros((SMALL - at_row, WIDE), F32)
    greet((at.sib, at.xn, at.xd, at.yn, at.zn))

    here = vec.at[:, span(at.grp * WIDE, WIDE)]
    packs = [
        pltpu.make_async_copy(pack_ref, here, s_misc.at[4]),
        remote(pack_ref, here, s_misc.at[5], r_misc.at[5], at.sib),
        remote(pack_ref, here, s_misc.at[6], r_misc.at[6], at.xn),
        remote(pack_ref, here, s_misc.at[7], r_misc.at[7], at.xd),
    ]
    for copy in packs:
        copy.start()

    def wider_parts(kind, y=at.y, zlow=at.zlow):
        q = full[kind].shape[2] // 4
        return span(y * q, q), span((2 + zlow) * q, q)

    def launch(l, kind):
        i = index[l, kind]
        src, dst = ins[kind].at[l], full[kind].at[l]
        n = src.shape[0]
        q = n // 4
        part = span(quarter * q, q)
        if kind in runs:
            width, count = runs[kind]
            mine = 2 * x + c
            for j in range(count):
                to = pl.ds(j * width, width)
                keep = span((2 * j + c) * width, width)
                give = span((2 * j + 1 - c) * width, width)
                remote(src.at[part, keep], dst.at[mine, part, to], s_send.at[i], s_rx.at[i], at.xn).start()
                remote(src.at[part, give], dst.at[mine, part, to], s_send.at[i], s_rx.at[i], at.xd).start()
            for j in range(count):
                to = pl.ds(j * width, width)
                keep = span((2 * j + c) * width, width)
                give = span((2 * j + 1 - c) * width, width)
                remote(src.at[:, give], dst.at[mine, :, to], s_send.at[i], s_rs.at[i], at.sib).start()
                pltpu.make_async_copy(src.at[:, keep], dst.at[mine, :, to], s_loc.at[i]).start()
        else:
            for part in wider_parts(kind) if kind in WIDER else (part,):
                remote(src.at[part], dst.at[x, part], s_send.at[i], s_rx.at[i], at.xn).start()
            pltpu.make_async_copy(src, dst.at[x], s_loc.at[i]).start()

    def theirs(l, kind, part):
        dst = full[kind].at[l]
        if kind in runs:
            return dst.at[span(2 * (1 - x), 2), part]
        return dst.at[pl.ds(1 - x, 1), part]

    def part_of(kind, y, zlow, half=None):
        q = full[kind].shape[2] // 4
        if half is None:
            return span((2 * y + zlow) * q, q)
        return span((4 * y + 2 * zlow + half) * (q // 2), q // 2)

    def relay1(l, kind):
        i = index[l, kind]
        if kind in WIDER:
            settle(theirs(l, kind, pl.ds(0, full[kind].shape[2] // 2)), s_rx.at[i])
            by_y, by_z = (theirs(l, kind, part) for part in wider_parts(kind))
            remote(by_y, by_y, s_send.at[i], s_ry.at[i], at.yn).start()
            remote(by_z, by_z, s_send.at[i], s_rz.at[i], at.zn).start()
            return
        piece = theirs(l, kind, part_of(kind, at.y, at.zlow))
        settle(piece, s_rx.at[i])
        remote(piece, piece, s_send.at[i], s_ry.at[i], at.yn).start()
        remote(piece, piece, s_send.at[i], s_rz.at[i], at.zn).start()

    def relay2(l, kind):
        i = index[l, kind]
        settle(theirs(l, kind, part_of(kind, 1 - at.y, at.zlow)), s_ry.at[i])
        piece = theirs(l, kind, part_of(kind, 1 - at.y, at.zlow, 0))
        remote(piece, piece, s_send.at[i], s_ra.at[i], at.zn).start()
        settle(theirs(l, kind, part_of(kind, at.y, 1 - at.zlow)), s_rz.at[i])
        piece = theirs(l, kind, part_of(kind, at.y, 1 - at.zlow, 1))
        remote(piece, piece, s_send.at[i], s_rb.at[i], at.yn).start()

    def ready(l, kind):
        i = index[l, kind]
        if kind in WIDER:
            by_y, by_z = (theirs(l, kind, part) for part in wider_parts(kind, 1 - at.y, 1 - at.zlow))
            settle(by_y, s_ry.at[i])
            settle(by_z, s_rz.at[i])
        else:
            settle(theirs(l, kind, part_of(kind, 1 - at.y, 1 - at.zlow, 0)), s_ra.at[i])
            settle(theirs(l, kind, part_of(kind, 1 - at.y, 1 - at.zlow, 1)), s_rb.at[i])
        if kind in runs:
            settle(full[kind].at[l, 0], s_rs.at[i])
        settle(full[kind].at[l, 0], s_loc.at[i])
        pltpu.make_async_copy(full[kind].at[l], saves[kind].at[l], s_loc.at[i]).start()

    line = list(index)
    tokens = [
        remote(tok_ref.at[1 - x], tok.at[1], s_misc.at[0], r_misc.at[0], at.xn),
        pltpu.make_async_copy(tok_ref.at[x], tok.at[0], s_misc.at[3]),
    ]
    x_time, yz_time = 4.0, 0.0
    for n, (l, kind) in enumerate(line):
        if n == 2:
            for copy in tokens:
                copy.start()
            x_time += 7.3
        launch(l, kind)
        mb = 2 * full[kind].shape[1] * full[kind].shape[2] * full[kind].shape[3] / 2**20
        hop = mb / 4 / 0.094 * 1.05
        x_time += 2 * hop if kind in WIDER else hop
        plan.add(x_time + 1, ("r1", l, kind), functools.partial(relay1, l, kind))
        yz_time = max(yz_time, x_time + 1.5)
        if kind in WIDER:
            yz_time += hop
        else:
            plan.add(yz_time + hop + 1.5, ("r2", l, kind), functools.partial(relay2, l, kind))
            yz_time += 1.5 * hop
        plan.add(yz_time + 3, ("ok", l, kind), functools.partial(ready, l, kind))
    late = [
        remote(cot_ref.at[1 - x], cot.at[1], s_misc.at[1], r_misc.at[1], at.xn),
        pltpu.make_async_copy(cot_ref.at[x], cot.at[0], s_misc.at[8]),
    ]
    for copy in late:
        copy.start()
    mask = chip_flags(at, tv_ref, rows, seq)
    saved = []

    def seed():
        for copy in late:
            copy.wait()
        valid = jnp.where(x == 0, iv_ref[0:1, 0:1], iv_ref[0:1, 1:2]).astype(F32)
        weight = mask[:rows].astype(F32) * valid
        for i in range(2):
            for j in range(block // STEP):
                r = i * block + j * STEP
                dm[pl.ds(r, STEP), :] = (
                    cot[i, pl.ds(j * STEP, STEP), :].astype(F32) * weight[r:r + STEP, :]
                ).astype(BF16)
        copy = remote(dm.at[own], dm.at[other], s_misc.at[2], r_misc.at[2], at.sib)
        copy.start()
        saved.append(copy)

    def seeded():
        saved[0].wait()
        copy = pltpu.make_async_copy(dm, dm_out, s_misc.at[10])
        copy.start()
        saved.append(copy)

    plan.add(x_time + 9, "seed", seed)
    plan.add(x_time + 14, "seeded", seeded)
    plan.order()

    for copy in packs:
        copy.wait()
    vec_save = pltpu.make_async_copy(vec, vec_out, s_misc.at[9])
    vec_save.start()
    for l in range(layers):
        for j in range(f // WIDE):
            half, sub = divmod(j, f // WIDE // 2)
            bup[l:l + 1, pl.ds(j * WIDE, WIDE)] = vec[
                l * SMALL + BUP + sub:l * SMALL + BUP + sub + 1, span((2 * half + c) * WIDE, WIDE)
            ]
    plan.now = 18.0
    plan.poll()
    for copy in tokens:
        copy.wait()
    for i in range(2):
        for j in range(block // STEP):
            x_ref[pl.ds(i * block + j * STEP, STEP), :] = tok[i, pl.ds(j * STEP, STEP), :].astype(F32)
    plan.spend(1)

    def save(src, dst, slot):
        copy = pltpu.make_async_copy(src, dst, s_save.at[slot])
        copy.start()
        return copy

    pending = {}
    for l in range(layers):
        def row(name, l=l):
            return vec[l * SMALL + name:l * SMALL + name + 1, :]

        def norm_out(src_ref, dst_ref, gain, shift, l=l):
            for i in range(rows // STEP):
                r = pl.ds(i * STEP, STEP)
                hat, _ = norm_rows(src_ref[r, :])
                dst_ref[r, :] = (hat * row(gain) + row(shift)).astype(BF16)

        def weight(kind, cs, l=l):
            w = full[kind][l, :, :, cs]
            return w.reshape(w.shape[0] * w.shape[1], w.shape[2])

        norm_out(x_ref, h1, G1, B1)
        cp = remote(h1.at[own], h1.at[other], s_core.at[0], r_core.at[0], at.sib)
        cp.start()
        x_saved = save(x_ref, xs.at[l], 0)
        plan.spend(2)
        plan.need(("ok", l, "qkv"))
        if l:
            pending["qkv"].wait()
        bq = jnp.where(c == 0, row(BQV), vec[l * SMALL + BQV + 1:l * SMALL + BQV + 2, :])
        scale = HEAD ** -0.5
        parts = (
            (0, bq[:, :hc] * scale, scale), (hc, jnp.zeros((1, hc), F32), 1.0), (2 * hc, bq[:, hc:], 1.0)
        )

        def qkv_rows(r, l=l, parts=parts):
            for base, bias, factor in parts:
                for j in range(hc // WIDE):
                    cs = pl.ds(base + j * WIDE, WIDE)
                    out = nn(h1[r, :], weight("qkv", cs))
                    qkv[r, cs] = (out * factor + bias[:, j * WIDE:(j + 1) * WIDE]).astype(BF16)
                    plan.spend(0.35)

        qkv_rows(own)
        cp.wait()
        qkv_rows(other)
        h1_saved = save(h1, h1s.at[l], 1)
        pending["qkv"] = save(qkv, qkvs.at[l], 2)
        if l:
            pending["att"].wait()
        for p in range(hc // 128):
            q2 = qkv[:, p * 128:(p + 1) * 128]
            k2 = qkv[:, hc + p * 128:hc + (p + 1) * 128]
            v2 = qkv[:, 2 * hc + p * 128:2 * hc + (p + 1) * 128]
            vt = v2.T
            outs = []
            for a in range(2):
                pt = scores_t(k2, half_lanes(q2, a), mask)
                outs.append(nn(vt[a * HEAD:(a + 1) * HEAD, :], pt.astype(BF16)))
                plan.spend(1.4)
            att[:, p * 128:(p + 1) * 128] = jnp.concatenate(outs, axis=0).T.astype(BF16)
        pending["att"] = save(att, as_.at[l], 3)

        def exchange(left, kind, base, bias, out, slot):
            def far(j):
                put[:, cols(j)] = nn(left[other, :], weight(kind, cols(j))).astype(BF16)

            loop(d // WIDE, far)
            cp = remote(put, got.at[slot], s_core.at[1], r_core.at[1], at.sib)
            cp.start()
            plan.spend(1)

            def near(j):
                out[:, cols(j)] = nn(left[own, :], weight(kind, cols(j))) + base[:, cols(j)] + vec[
                    l * SMALL + bias:l * SMALL + bias + 1, cols(j)
                ]

            loop(d // WIDE, near)
            plan.spend(1)
            cp.wait()
            out[...] += got[slot].astype(F32)
            plan.spend(1)

        plan.need(("ok", l, "out"))
        if l:
            pending["x2"].wait()
        exchange(att, "out", x_ref, BOUT, x2_ref, 0)
        pending["x2"] = save(x2_ref, x2s.at[l], 4)
        norm_out(x2_ref, h2, G2, B2)
        cp = remote(h2.at[own], h2.at[other], s_core.at[2], r_core.at[2], at.sib)
        cp.start()
        plan.spend(2)
        plan.need(("ok", l, "up"))
        if l:
            pending["z"].wait()
            pending["gp"].wait()

        def up_rows(r):
            def body(j):
                u = nn(h2[r, :], weight("up", cols(j))) + bup[l:l + 1, cols(j)]
                phi = 0.5 + 0.5 * lax.erf(u * 0.7071067811865476)
                z[r, cols(j)] = (u * phi).astype(BF16)
                gp[r, cols(j)] = (phi + u * jnp.exp(u * u * -0.5) * 0.3989422804014327).astype(BF16)

            for part in range(2):
                loop(f // WIDE // 2, lambda j: body(j + part * (f // WIDE // 2)))
                plan.spend(1.9)

        up_rows(own)
        cp.wait()
        up_rows(other)
        h2_saved = save(h2, h2s.at[l], 5)
        pending["z"] = save(z, zs.at[l], 6)
        pending["gp"] = save(gp, gps.at[l], 7)
        plan.need(("ok", l, "down"))
        for copy in (x_saved, h1_saved, h2_saved):
            copy.wait()
        exchange(z, "down", x2_ref, BDOWN, x_ref, 1)

    for i in range(2):
        for j in range(block // STEP):
            tok[i, pl.ds(j * STEP, STEP), :] = x_ref[pl.ds(i * block + j * STEP, STEP), :].astype(BF16)
    act = pltpu.make_async_copy(tok, act_out, s_misc.at[11])
    act.start()
    while plan.events:
        plan.fire()
    for copy in (act, vec_save, saved[1]):
        copy.wait()
    for name in ("qkv", "att", "x2", "z", "gp"):
        pending[name].wait()
    for (l, kind), i in index.items():
        settle(full[kind].at[l, pl.ds(0, 3 if kind in runs else 1)], s_send.at[i])
        settle(full[kind].at[l], s_loc.at[i])


ANY = pl.BlockSpec(memory_space=pl.ANY)
VM = pl.BlockSpec(memory_space=pltpu.VMEM)


def dma(*shape):
    return pltpu.SemaphoreType.DMA(shape)


def run_fwd(tok, cot, smalls, tv, iv, w_qkv, w_out, w_up, w_down, seq):
    layers, n, d3 = w_qkv.shape
    d = d3 // 3
    hc, f = d // 2, 2 * w_down.shape[1]
    block = tok.shape[1]
    rows, both = 2 * block, 4 * block
    weights = [(4, n, 3 * hc), (2, n, d), (4, n, f), (2, w_down.shape[1], d)]
    acts = [
        ((rows, d), F32), ((rows, d), F32), ((both, d), BF16), ((both, 3 * hc), BF16),
        ((both, hc), BF16), ((both, d), BF16), ((both, f), BF16), ((both, f), BF16),
    ]
    shapes = [((layers, *s), BF16) for s in weights] + [((layers, *s), t) for s, t in acts]
    shapes += [((both, d), BF16), ((2, block, d), BF16), ((layers * SMALL, d), F32)]
    count = layers * len(KINDS)
    return pl.pallas_call(
        functools.partial(fwd_kernel, seq),
        out_shape=[jax.ShapeDtypeStruct(s, t) for s, t in shapes],
        in_specs=[ANY, ANY] + [VM] * 10 + [ANY] * 4,
        out_specs=[ANY] * len(shapes),
        scratch_shapes=[pltpu.VMEM((layers, *s), BF16) for s in weights]
        + [pltpu.VMEM(s, t) for s, t in acts]
        + [
            pltpu.VMEM((rows, d), BF16), pltpu.VMEM((2, rows, d), BF16),
            pltpu.VMEM((2, block, d), BF16), pltpu.VMEM((layers * SMALL, d), F32), pltpu.VMEM((8, f), F32),
            pltpu.VMEM((2, block, d), BF16), pltpu.VMEM((both, d), BF16), pltpu.VMEM((layers * SMALL, WIDE), F32),
        ]
        + [dma(count)] * 8
        + [dma(3), dma(3), dma(8), dma(12), dma(8)],
        compiler_params=pltpu.CompilerParams(
            collective_id=1, has_side_effects=True, vmem_limit_bytes=VMEM_LIMIT
        ),
        cost_estimate=pl.CostEstimate(flops=17 * 10**9, bytes_accessed=80 * 10**6, transcendentals=0),
        name="forward",
    )(tok, cot, *smalls, tv, iv, w_qkv, w_out, w_up, w_down)


LINK, HOP, STAGE = 11.5, 2.5, 0.6
NS, NY, NZ, NT = 6, 3, 3, 6
CHUNK = 256
CROSS = (("down", 1), ("down", 3), ("up", 1))


def chunks_of(layers):
    chunks = []
    for l in reversed(range(layers)):
        chunks += [("down", l, i) for i in range(4)] + [("up", l, i) for i in range(4)]
        chunks += [("out", l, 0)] + [("qkv", l, i) for i in range(3)]
    return chunks + [("small", 0, 0)]


def crossed(chunk):
    return (chunk[0], chunk[2]) in CROSS


def units_of(chunks):
    units, first, last = [], {}, {}
    for k, (kind, l, i) in enumerate(chunks):
        if crossed(chunks[k]):
            continue
        pieces = {("qkv", 0, 1): (128, 128), ("qkv", 0, 2): (128, 64, 64), ("small", 0, 0): (64,)}
        start = 0
        first[k] = len(units)
        for n in pieces.get((kind, l, i), (CHUNK,)):
            units.append((k, start, n))
            start += n
        last[k] = len(units) - 1
    return units, first, last


class Ring:
    def __init__(self, at, plan, chunks, outs, bufs, sems):
        self.at, self.plan, self.chunks, self.outs = at, plan, chunks, outs
        self.g, self.xr, self.yr, self.zr, self.wr, self.t, self.zd, self.xd, self.yd, self.cd, self.td = bufs
        (self.x_send, self.x_recv, self.y_send, self.y_recv, self.z_send, self.z_recv, self.w_send, self.w_recv,
         self.f_send, self.f_recv) = sems[:10]
        self.d_send, self.d_recv, self.d_out, self.cx, self.cy, self.cz, self.cw, self.cb = sems[10:]
        self.units, self.first, self.last = units_of(chunks)
        self.turn = {k: a for a, k in enumerate(self.first)}
        self.cross = [k for k, chunk in enumerate(chunks) if crossed(chunk)]
        self.count = len(self.units)
        self.link = dict(x=0.0, y=0.0, out=0.0, mid=0.0, back=0.0)
        self.copies, self.done, self.ready = {}, set(), {}

    def size(self, u):
        return self.units[u][2]

    def send(self, links, rows):
        t = max(self.plan.now, *(self.link[name] for name in links)) + LINK * rows / CHUNK
        for name in links:
            self.link[name] = t
        return t + HOP

    def pick(self, limit):
        best = None
        for (stage, u), t in self.ready.items():
            if t > limit or (best and best[0] <= t):
                continue
            ahead = [(stage, u - 1)]
            ahead += {1: [(2, u - NY)], 2: [(3, u - NZ), (6, u - NT)], 3: [(4, u - NZ)], 4: [(5, u - NZ)]}.get(stage, [])
            if all(v < 0 or (other, v) in self.done for other, v in ahead):
                best = (t, stage, u)
        return best

    def step(self, best):
        t, stage, u = best
        del self.ready[stage, u]
        self.plan.now = max(self.plan.now, t) + STAGE
        if stage > 10:
            (self.d2, self.d3, self.d4, self.d5, self.d6, self.d7)[stage - 12](u)
            links, rows = {
                12: (("x",), 128), 13: (("y",), 64), 14: (("mid", "out", "back"), 96), 15: (("y",), 64),
                16: (("out", "back"), 128),
            }.get(stage, (None, 0))
        else:
            (self.s1, self.s2, self.s3, self.s4, self.s5, self.s6)[stage - 1](u)
            links = {1: ("y",), 2: ("out",), 3: ("mid",), 4: ("back",), 5: ("y",)}.get(stage)
            rows = self.size(u) // 2
        self.done.add((stage, u))
        if links:
            self.ready[stage + 1, u] = self.send(links, rows)

    def poll(self):
        while best := self.pick(self.plan.now):
            self.step(best)

    def catch_up(self, stage, u):
        while (stage, u) not in self.done:
            self.step(self.pick(float("inf")))

    def reserve(self, k):
        if k >= NS:
            old = k - NS
            if old in self.turn:
                self.catch_up(2, self.last[old])
            else:
                self.catch_up(14, self.cross.index(old))
        if self.turn.get(k, 0) >= NS:
            self.catch_up(1, self.last[list(self.turn)[self.turn[k] - NS]])

    def launch(self, k):
        if k not in self.turn:
            d = self.cross.index(k)
            self.move(d, 0, self.g.at[k % NS, :, self.rows_of(1 - self.at.inn)], self.zd.at[d], self.at.zn)
            self.ready[12, d] = self.send(("out", "back"), CHUNK)
            return
        a = self.turn[k]
        if a >= NS:
            pl.semaphore_wait(self.cx, 1)
        for u in range(self.first[k], self.last[k] + 1):
            _, start, n = self.units[u]
            copy = remote(
                self.g.at[k % NS, 0, pl.ds(start, n)], self.xr.at[a % NS, pl.ds(start, n)],
                self.x_send.at[u], self.x_recv.at[u], self.at.xn,
            )
            copy.start()
            self.copies["x", u] = copy
            self.ready[1, u] = self.send(("x",), n)

    def rows_of(self, part):
        return span(part * (CHUNK // 2), CHUNK // 2)

    def move(self, d, hop, src, dst, peer):
        copy = remote(src, dst, self.d_send.at[hop, d], self.d_recv.at[hop, d], peer)
        copy.start()
        self.copies[hop, d] = copy

    def d2(self, d):
        slot, mine = self.cross[d] % NS, self.rows_of(self.at.inn)
        self.copies[0, d].wait()
        for hh in range(2):
            self.add(self.g.at[slot, hh, mine], self.zd.at[d, hh], CHUNK // 2)
        self.move(d, 1, self.g.at[slot, 0, mine], self.xd.at[d], self.at.xn)

    def d3(self, d):
        slot, mine, quarter = self.cross[d] % NS, self.rows_of(self.at.inn), CHUNK // 4
        self.copies[1, d].wait()
        self.add(self.g.at[slot, 1, mine], self.xd.at[d], CHUNK // 2)
        give = span((2 * self.at.inn + 1 - self.at.y) * quarter, quarter)
        self.move(d, 2, self.g.at[slot, 1, give], self.yd.at[d], self.at.yn)

    def d4(self, d):
        slot, quarter = self.cross[d] % NS, CHUNK // 4
        t = self.td.at[d, span(self.at.y * quarter, quarter)]
        self.copies[2, d].wait()
        self.add(t, self.yd.at[d], quarter, self.g.at[slot, 1], (2 * self.at.inn + self.at.y) * quarter)
        self.move(d, 3, t, self.cd.at[d], self.at.mid)

    def d5(self, d):
        quarter = CHUNK // 4
        t = self.td.at[d, span(self.at.y * quarter, quarter)]
        self.copies[3, d].wait()
        self.add(t, self.cd.at[d], quarter)
        self.move(d, 4, t, t, self.at.yn)

    def d6(self, d):
        at = self.at
        kind, l, i = self.chunks[self.cross[d]]
        out = self.outs[kind]
        self.copies[4, d].wait()
        if kind == "down":
            dst = out.at[l, span((2 * i + at.inn) * (CHUNK // 2), CHUNK // 2)]
        else:
            width = self.td.shape[2]
            dst = out.at[l, self.rows_of(at.inn), span((2 * (i % 2) + at.c) * width, width)]
        sent = self.d_out.at[d]
        pltpu.make_async_copy(self.td.at[d], dst, sent).start()
        remote(self.td.at[d], dst, sent, self.f_recv.at[KINDS.index(kind)], at.zn).start()

    def d7(self, d):
        settle(self.zd.at[d], self.d_out.at[d])

    def credit(self, sem, u, slots, peer):
        if u + slots < self.count:
            pl.semaphore_signal(sem, inc=1, device_id=peer, device_id_type=MESH)

    def claim(self, sem, u, slots):
        if u >= slots:
            pl.semaphore_wait(sem, 1)

    def add(self, dst, src, count, base=None, base_at=None):
        def body(j):
            r = cols(j, 32)
            b = dst[r, :] if base is None else base[pl.ds(pl.multiple_of(base_at + j * 32, 32), 32), :]
            dst[r, :] = (b.astype(F32) + src[r, :].astype(F32)).astype(BF16)

        loop(count // 32, body)

    def s1(self, u):
        at = self.at
        k, start, n = self.units[u]
        slot, a = k % NS, self.turn[k]
        self.copies["x", u].wait()
        self.add(self.g.at[slot, 1, pl.ds(start, n)], self.xr.at[a % NS, pl.ds(start, n)], n)
        if u == self.last[k] and a + NS < len(self.turn):
            pl.semaphore_signal(self.cx, inc=1, device_id=at.xn, device_id_type=MESH)
        self.claim(self.cy, u, NY)
        copy = remote(
            self.g.at[slot, 1, span(start + (1 - at.y) * (n // 2), n // 2)], self.yr.at[u % NY, pl.ds(0, n // 2)],
            self.y_send.at[u], self.y_recv.at[u % NY], at.yn,
        )
        copy.start()
        self.copies["y", u] = copy

    def part(self, ref, u, slots):
        return ref.at[u % slots, pl.ds(0, self.size(u) // 2)]

    def s2(self, u):
        at = self.at
        k, start, n = self.units[u]
        t = self.part(self.t, u, NT)
        self.copies["y", u].wait()
        self.add(t, self.part(self.yr, u, NY), n // 2, self.g.at[k % NS, 1], start + at.y * (n // 2))
        self.credit(self.cy, u, NY, at.yn)

        @pl.when(at.outer)
        def _():
            self.claim(self.cz, u, NZ)
            remote(t, self.part(self.zr, u, NZ), self.z_send.at[u % NT], self.z_recv.at[u % NZ], at.zn).start()

    def s3(self, u):
        n, at = self.size(u), self.at
        t = self.part(self.t, u, NT)

        @pl.when(at.outer)
        def _():
            settle(t, self.z_send.at[u % NT])

        @pl.when(at.inner)
        def _():
            got = self.part(self.zr, u, NZ)
            settle(got, self.z_recv.at[u % NZ])
            self.add(t, got, n // 2)
            self.credit(self.cz, u, NZ, at.zn)
            self.claim(self.cw, u, NZ)
            remote(t, self.part(self.wr, u, NZ), self.z_send.at[u % NT], self.w_recv.at[u % NZ], at.mid).start()

    def s4(self, u):
        n, at = self.size(u), self.at

        @pl.when(at.inner)
        def _():
            t = self.part(self.t, u, NT)
            got = self.part(self.wr, u, NZ)
            settle(got, self.w_recv.at[u % NZ])
            settle(t, self.z_send.at[u % NT])
            self.add(t, got, n // 2)
            self.credit(self.cw, u, NZ, at.mid)
            self.claim(self.cb, u, NZ)
            remote(t, self.part(self.zr, u, NZ), self.w_send.at[u % NT], self.z_recv.at[u % NZ], at.zn).start()

    def s5(self, u):
        n, at = self.size(u), self.at
        t = self.part(self.t, u, NT)

        @pl.when(at.outer)
        def _():
            got = self.part(self.zr, u, NZ)
            settle(got, self.z_recv.at[u % NZ])

            def body(j):
                t[cols(j, 32), :] = got[cols(j, 32), :]

            loop(n // 64, body)
            self.credit(self.cb, u, NZ, at.zn)

        k, start, n = self.units[u]
        kind, l, i = self.chunks[k]
        out = self.outs[kind]
        sent = self.f_send.at[u % NT]
        if kind == "small":
            pltpu.make_async_copy(t, out, sent).start()
            return
        half = n // 2
        width = t.shape[1]

        def deliver(src, dst, mine, kind_index):
            if mine:
                pltpu.make_async_copy(src, dst, sent).start()
                remote(src, dst, sent, self.f_recv.at[kind_index], at.yn).start()
            else:
                remote(src, dst, sent, self.f_recv.at[kind_index], at.sib).start()
                remote(src, dst, sent, self.f_recv.at[kind_index], at.yd).start()

        if kind in ("down", "out"):
            deliver(t, out.at[l, span(i * CHUNK + start + at.y * half, half)], True, KINDS.index(kind))
        elif kind == "up":
            side, run = divmod(i, 2)
            deliver(t, out.at[l, span(start + at.y * half, half), span((2 * run + at.c) * width, width)], side == 0, 2)
        else:
            for side in range(2):
                for run in range(2):
                    src = t.at[:, pl.ds((2 * side + run) * WIDE, WIDE)]
                    dst = out.at[l, span(start + at.y * half, half), span(i * width + (2 * run + at.c) * WIDE, WIDE)]
                    deliver(src, dst, side == 0, 0)

    def s6(self, u):
        at = self.at
        t = self.part(self.t, u, NT)
        k, _, n = self.units[u]
        settle(t if self.chunks[k][0] == "small" else self.g.at[0, 0, pl.ds(0, n)], self.f_send.at[u % NT])

        @pl.when(at.inner)
        def _():
            settle(t, self.w_send.at[u % NT])

    def finish(self):
        while best := self.pick(float("inf")):
            self.step(best)
        for i, kind in enumerate(KINDS):
            out = self.outs[kind]
            rows = out.shape[1]
            settle(out.at[:, pl.ds(0, rows // 2 if kind in ("out", "down") else rows * 3 // 4)], self.f_recv.at[i])


def bwd_kernel(
    seq, dm_ref, act_ref, vec_ref, tv_ref, vqkv, vout, vup, vdown, xs, x2s, h1s, qkvs, as_, h2s, zs, gps,
    oqkv, oout, oup, odown, osmall, otok, oact,
    wqkv, wout, wup, wdown, x_ref, x2_ref, h1, qkv, att, h2, z, gp,
    g_ref, dm, da, dj, dx2, dh, put, got, small, small_put, small_got, s_load, s_core, r_core, s_misc, r_misc, *rest,
):
    at = Place()
    layers = vqkv.shape[0]
    rows, d = x_ref.shape
    block = rows // 2
    hc, f = att.shape[1], z.shape[1]
    own, other = pl.ds(0, rows), pl.ds(rows, rows)
    x, c = at.x, at.c
    plan = Plan()
    chunks = chunks_of(layers)
    rings, ring_sems = rest[:11], rest[11:]
    ring_g = rings[0]
    ring = Ring(
        at, plan, chunks, dict(qkv=oqkv, out=oout, up=oup, down=odown, small=osmall),
        rings, ring_sems,
    )
    plan.poll = ring.poll
    number = {chunk: u for u, chunk in enumerate(chunks)}

    stores = dict(
        z=(zs, z), wdown=(vdown, wdown), gp=(gps, gp), h2=(h2s, h2), wup=(vup, wup), x2=(x2s, x2_ref),
        wout=(vout, wout), att=(as_, att), qkv=(qkvs, qkv), wqkv=(vqkv, wqkv), h1=(h1s, h1), x=(xs, x_ref),
    )
    slots = {name: i for i, name in enumerate(stores)}
    loads = {}

    def load(name, l):
        if l < 0:
            return
        src, dst = stores[name]
        loads[name, l] = pltpu.make_async_copy(src.at[l], dst, s_load.at[slots[name]])
        loads[name, l].start()

    dm_load = pltpu.make_async_copy(dm_ref, dm.at[0], s_misc.at[0])
    dm_load.start()
    for name in stores:
        load(name, layers - 1)
    greet((at.sib, at.xn, at.yn, at.yd, at.zn, at.mid))

    def by_half(hh):
        return hh * x + (1 - hh) * (1 - x)

    mask = chip_flags(at, tv_ref, rows, seq)
    small[...] = jnp.zeros_like(small)
    act = [
        remote(act_ref.at[1], oact.at[x], s_misc.at[4], r_misc.at[4], at.xn),
        pltpu.make_async_copy(act_ref.at[0], oact.at[x], s_misc.at[5]),
    ]
    for l in reversed(range(layers)):
        def row(name, l=l):
            return vec_ref[l * SMALL + name:l * SMALL + name + 1, :]

        def set_small(name, value, l=l):
            small[l * SMALL + name:l * SMALL + name + 1, :] = value

        def round_rows(src_ref, name, slot):
            total = jnp.zeros((8, d), F32)
            for i in range(rows // STEP):
                r = pl.ds(i * STEP, STEP)
                if src_ref is None:
                    low = dm[slot, r, :].astype(F32)
                    g_ref[r, :] = low
                else:
                    low = src_ref[r, :].astype(BF16)
                    dm[slot, r, :] = low
                    low = low.astype(F32)
                total = total + low[0:8, :] + low[8:16, :]
            set_small(name, jnp.sum(total, axis=0, keepdims=True))

        def send_round(src_ref, name, slot):
            round_rows(src_ref, name, slot)
            copy = remote(dm.at[slot, own], dm.at[slot, other], s_core.at[slot], r_core.at[slot], at.sib)
            copy.start()
            return copy

        def exchange(left, w):
            per = w.shape[1]

            def piece(j):
                b = j // (per // WIDE)
                return w[b, span((j % (per // WIDE)) * WIDE, WIDE), :]

            def far(j):
                put[:, cols(j)] = nt(left[other, :], piece(j)).astype(BF16)

            loop(d // WIDE, far)
            plan.spend(1.5)
            copy = remote(put, got, s_core.at[2], r_core.at[2], at.sib)
            copy.start()

            def near(j):
                dh[:, cols(j)] = nt(left[own, :], piece(j))

            loop(d // WIDE, near)
            plan.spend(1.5)
            copy.wait()
            plan.spend(0.5)

        def norm_back(value_ref, base_ref, out_ref, gain, shift):
            total_g = jnp.zeros((8, d), F32)
            total_b = jnp.zeros((8, d), F32)
            for i in range(rows // STEP):
                r = pl.ds(i * STEP, STEP)
                hat, rstd = norm_rows(value_ref[r, :])
                grad = dh[r, :] + got[r, :].astype(F32)
                prod = grad * hat
                total_g = total_g + prod[0:8, :] + prod[8:16, :]
                total_b = total_b + grad[0:8, :] + grad[8:16, :]
                dhat = grad * row(gain)
                m1 = jnp.mean(dhat, axis=-1, keepdims=True)
                m2 = jnp.mean(dhat * hat, axis=-1, keepdims=True)
                out_ref[r, :] = base_ref[r, :] + rstd * (dhat - m1 - hat * m2)
            set_small(gain, jnp.sum(total_g, axis=0, keepdims=True))
            set_small(shift, jnp.sum(total_b, axis=0, keepdims=True))

        def produce(chunk, maker, us):
            u = number[chunk]
            ring.reserve(u)
            loop(2, lambda hh: maker(ring_g.at[u % NS, hh], by_half(hh)))
            ring.launch(u)
            plan.spend(us)

        if l == layers - 1:
            dm_load.wait()
            loads["z", l].wait()
        else:
            copy = send_round(g_ref, BDOWN, 0)
            loads["z", l].wait()
            plan.spend(2)
            copy.wait()
        for i in range(4):
            def make(dst, h, i=i):
                dst[...] = tn(z[:, span(h * (f // 2) + i * CHUNK, CHUNK)], dm[0]).astype(BF16)

            produce(("down", l, i), make, 1.3)
        if l == layers - 1:
            round_rows(None, BDOWN, 0)
            for copy in act:
                copy.start()
        load("z", l - 1)
        loads["wdown", l].wait()
        loads["gp", l].wait()

        def dz_body(j):
            b = j // (f // 2 // WIDE)
            w = wdown[b, span((j % (f // 2 // WIDE)) * WIDE, WIDE), :]
            for r in (own, other):
                low = (nt(dm[0, r, :], w) * gp[r, cols(j)].astype(F32)).astype(BF16)
                gp[r, cols(j)] = low

        for part in range(2):
            loop(f // WIDE // 2, lambda j: dz_body(j + part * (f // WIDE // 2)))
            plan.spend(2)
        load("wdown", l - 1)
        for j in range(f // WIDE):
            half, sub = divmod(j, f // WIDE // 2)
            small[l * SMALL + BUP + sub:l * SMALL + BUP + sub + 1, span((2 * half + c) * WIDE, WIDE)] = jnp.sum(
                gp[:, j * WIDE:(j + 1) * WIDE].astype(F32), axis=0, keepdims=True
            )
        loads["h2", l].wait()
        loads["wup", l].wait()
        for i in range(4):
            side, run = divmod(i, 2)

            def make(dst, h, side=side, run=run):
                rh = c if side == 0 else 1 - c
                left = h2[:, span(h * (d // 2) + rh * CHUNK, CHUNK)]
                dst[...] = tn(left, gp[:, run * (f // 2):(run + 1) * (f // 2)]).astype(BF16)

            if i == 2:
                exchange(gp, wup)
                load("wup", l - 1)
                loads["x2", l].wait()
                norm_back(x2_ref, g_ref, dx2, G2, B2)
                load("x2", l - 1)
                plan.spend(3)
                copy = send_round(dx2, BOUT, 1)
            produce(("up", l, i), make, 1.3)
        load("gp", l - 1)
        load("h2", l - 1)

        loads["wout", l].wait()
        loads["att", l].wait()
        copy.wait()
        for j in range(hc // WIDE):
            for r in (own, other):
                da[r, pl.ds(j * WIDE, WIDE)] = nt(dm[1, r, :], wout[j]).astype(BF16)
        load("wout", l - 1)

        def make(dst, h):
            dst[...] = tn(att[:, span(h * CHUNK, CHUNK)], dm[1]).astype(BF16)

        produce(("out", l, 0), make, 2)
        load("att", l - 1)
        loads["qkv", l].wait()
        sums = {}
        for p in range(hc // 128):
            cq, ck, cv = (pl.ds(k * hc + p * 128, 128) for k in range(3))
            q2, k2, v2, da2 = qkv[:, cq], qkv[:, ck], qkv[:, cv], da[:, cq]
            kt = k2.T
            dk = dv = None
            parts = []
            for a in range(2):
                qa, daa = half_lanes(q2, a), half_lanes(da2, a)
                pt = scores_t(k2, qa, mask)
                dpt = nt(v2, daa)
                delta = jnp.sum(dpt * pt, axis=0, keepdims=True)
                dst = (pt * (dpt - delta)).astype(BF16)
                dva = nn(pt.astype(BF16), daa)
                dka = nn(dst, qa)
                parts.append(nn(kt[a * HEAD:(a + 1) * HEAD, :], dst))
                dk = dka if dk is None else dk + dka
                dv = dva if dv is None else dv + dva
                plan.spend(2.7)
            dq = (jnp.concatenate(parts, axis=0).T * HEAD ** -0.5).astype(BF16)
            dv = dv.astype(BF16)
            dj[:, cq] = dq
            dj[:, ck] = dk.astype(BF16)
            dj[:, cv] = dv
            for k, value in ((0, dq), (1, dv)):
                total = jnp.sum(value.astype(F32), axis=0, keepdims=True)
                for core in range(2):
                    r = l * SMALL + BQV + core
                    small[r:r + 1, k * hc + p * 128:k * hc + (p + 1) * 128] = jnp.where(
                        c == core, total, jnp.zeros_like(total)
                    )
        load("qkv", l - 1)
        loads["wqkv", l].wait()
        loads["h1", l].wait()
        for i in range(3):
            def make(dst, h, i=i):
                for side in range(2):
                    rh = c if side == 0 else 1 - c
                    left = h1[:, span(h * (d // 2) + rh * CHUNK, CHUNK)]
                    dst[:, side * hc:(side + 1) * hc] = tn(left, dj[:, i * hc:(i + 1) * hc]).astype(BF16)

            if i == 1:
                exchange(dj, wqkv)
                load("wqkv", l - 1)
                loads["x", l].wait()
                norm_back(x_ref, dx2, g_ref, G1, B1)
                load("x", l - 1)
                plan.spend(3)
            produce(("qkv", l, i), make, 1.3)
        load("h1", l - 1)

    for j in range(rows // STEP):
        put[pl.ds(j * STEP, STEP), :] = g_ref[pl.ds(j * STEP, STEP), :].astype(BF16)
    back = [
        remote(put.at[pl.ds(block, block)], otok.at[x], s_misc.at[1], r_misc.at[1], at.xn),
        pltpu.make_async_copy(put.at[pl.ds(0, block)], otok.at[x], s_misc.at[2]),
    ]
    small_put[...] = small[...].astype(BF16)
    copy = remote(small_put, small_got, s_misc.at[3], r_misc.at[3], at.sib)
    copy.start()
    copy.wait()
    total = (small_put[...].astype(F32) + small_got[...].astype(F32)).astype(BF16)
    u = number["small", 0, 0]
    ring.reserve(u)
    n = total.shape[0]
    for hh in range(2):
        for k in range(2):
            ring_g[u % NS, hh, k * n:(k + 1) * n, :] = total
    ring.launch(u)
    for copy in back:
        copy.start()
    ring.finish()
    for copy in (*back, *act):
        copy.wait()


def run_bwd(dm, act, vec, tv, weights, acts, seq):
    layers, _, n, hc3 = weights[0].shape
    d = acts[0].shape[2]
    rows = acts[0].shape[1]
    block, both = rows // 2, 2 * rows
    hc, f = hc3 // 3, weights[2].shape[3]
    chunks = chunks_of(layers)
    units = len(units_of(chunks)[0])
    crosses = sum(crossed(chunk) for chunk in chunks)
    outs = [(layers, n, 3 * d), (layers, n, d), (layers, n, 2 * f), (layers, f // 2, d), (layers * SMALL, d)]
    outs += [(2, block, d)] * 2
    args = (dm, act, vec, tv, *weights, *acts)
    return pl.pallas_call(
        functools.partial(bwd_kernel, seq),
        out_shape=[jax.ShapeDtypeStruct(s, BF16) for s in outs],
        in_specs=[ANY, ANY, VM, VM] + [ANY] * 12,
        out_specs=[ANY] * len(outs),
        scratch_shapes=[pltpu.VMEM(w.shape[1:], w.dtype) for w in (*weights, *acts)]
        + [
            pltpu.VMEM((rows, d), F32), pltpu.VMEM((2, both, d), BF16),
            pltpu.VMEM((both, hc), BF16), pltpu.VMEM((both, 3 * hc), BF16), pltpu.VMEM((rows, d), F32),
            pltpu.VMEM((rows, d), F32), pltpu.VMEM((rows, d), BF16), pltpu.VMEM((rows, d), BF16),
            pltpu.VMEM((layers * SMALL, d), F32), pltpu.VMEM((layers * SMALL, d), BF16),
            pltpu.VMEM((layers * SMALL, d), BF16),
            dma(12), dma(3), dma(3), dma(6), dma(6),
            pltpu.VMEM((NS, 2, CHUNK, d), BF16), pltpu.VMEM((NS, CHUNK, d), BF16),
            pltpu.VMEM((NY, CHUNK // 2, d), BF16), pltpu.VMEM((NZ, CHUNK // 2, d), BF16),
            pltpu.VMEM((NZ, CHUNK // 2, d), BF16), pltpu.VMEM((NT, CHUNK // 2, d), BF16),
            pltpu.VMEM((crosses, 2, CHUNK // 2, d), BF16), pltpu.VMEM((crosses, CHUNK // 2, d), BF16),
            pltpu.VMEM((crosses, CHUNK // 4, d), BF16), pltpu.VMEM((crosses, CHUNK // 4, d), BF16),
            pltpu.VMEM((crosses, CHUNK // 2, d), BF16),
            dma(units), dma(units), dma(units), dma(NY), dma(NT), dma(NZ), dma(NT), dma(NZ), dma(NT), dma(4),
            dma(5, crosses), dma(5, crosses), dma(crosses),
        ]
        + [pltpu.SemaphoreType.REGULAR] * 5,
        compiler_params=pltpu.CompilerParams(
            collective_id=2, has_side_effects=True, vmem_limit_bytes=VMEM_LIMIT
        ),
        cost_estimate=pl.CostEstimate(flops=34 * 10**9, bytes_accessed=120 * 10**6, transcendentals=0),
        name="backward",
    )(*args)


def finish_kernel(gqkv, gout, gup, gdown, small, oqkv, oout, oup, odown, *vectors):
    for src, dst in ((gqkv, oqkv), (gout, oout), (gup, oup), (gdown, odown)):
        dst[...] = src[...].astype(F32)
    mine = span(lax.axis_index("grp") * WIDE, WIDE)
    layers = vectors[0].shape[0]
    rows = [small[l * SMALL:(l + 1) * SMALL, mine].astype(F32) for l in range(layers)]
    at = 0
    for out in vectors:
        for j in range(out.shape[1] // WIDE):
            for l in range(layers):
                out[l:l + 1, j * WIDE:(j + 1) * WIDE] = rows[l][at:at + 1, :]
            at += 1


def run_finish(gqkv, gout, gup, gdown, small, widths):
    bigs = (gqkv, gout, gup, gdown)
    layers = gqkv.shape[0]
    steps = 4

    def big(g):
        return pl.BlockSpec((1, g.shape[1] // steps, g.shape[2]), lambda l, s: (l, s, 0))

    def flat(shape):
        return pl.BlockSpec(shape, lambda l, s: (0, 0))

    vectors = [(layers, w) for w in widths]
    return pl.pallas_call(
        finish_kernel,
        grid=(layers, steps),
        out_shape=[jax.ShapeDtypeStruct(g.shape, F32) for g in bigs]
        + [jax.ShapeDtypeStruct(v, F32) for v in vectors],
        in_specs=[big(g) for g in bigs] + [flat(small.shape)],
        out_specs=[big(g) for g in bigs] + [flat(v) for v in vectors],
        compiler_params=pltpu.CompilerParams(vmem_limit_bytes=VMEM_LIMIT),
        name="finish",
    )(*bigs, small)


def local(
    tokens, cotangent, image_valid, token_valid,
    norm1_gain, norm1_bias, w_qkv, b_qv, w_out, b_out, norm2_gain, norm2_bias, w_up, b_up, w_down, b_down,
):
    seq = tokens.shape[1]
    block = -(-seq // 32) * 32

    def pad(value):
        return jnp.pad(value, ((0, 0), (0, block - seq), (0, 0)))

    smalls = (norm1_gain, norm1_bias, b_out, norm2_gain, norm2_bias, b_down, b_qv, b_up)
    res = run_fwd(
        pad(tokens), pad(cotangent), smalls, token_valid, image_valid[None, :], w_qkv, w_out, w_up, w_down, seq
    )
    weights, acts, (dm, act, vec) = res[:4], res[4:12], res[12:]
    gqkv, gout, gup, gdown, gsmall, gtok, act = run_bwd(dm, act, vec, token_valid, weights, acts, seq)
    blocks = lax.axis_size("rep") // 8
    if blocks > 1:
        groups = [[i + 8 * b for b in range(blocks)] for i in range(8)]
        gqkv, gout, gup, gdown, gsmall = (
            lax.psum(g, "rep", axis_index_groups=groups) for g in (gqkv, gout, gup, gdown, gsmall)
        )
    gqkv, gout, gup, gdown, *vectors = run_finish(gqkv, gout, gup, gdown, gsmall, [w.shape[1] for w in smalls])
    gg1, gb1, gbout, gg2, gb2, gbdown, gbqv, gbup = vectors
    return (
        act[:, :seq], gtok[:, :seq], gg1, gb1, gqkv, gbqv, gout, gbout, gg2, gb2, gup, gbup, gdown, gbdown,
    )


def solution(mesh):
    rows3, mat, vec = P("rep", "grp", None), P(None, "grp", None), P(None, "grp")
    weights = (vec, vec, mat, vec, mat, vec, vec, vec, mat, vec, mat, vec)
    return jax.shard_map(
        local,
        mesh=mesh,
        in_specs=(rows3, rows3, P("rep"), P("rep", None)) + weights,
        out_specs=(rows3, rows3) + weights,
        check_vma=False,
    )
```

```python
import functools

import jax
import jax.numpy as jnp
from jax import lax
from jax.experimental import pallas as pl
from jax.experimental.pallas import tpu as pltpu
from jax.sharding import PartitionSpec as P

HEAD = 64
MESH = pl.DeviceIdType.MESH
F32 = jnp.float32
BF16 = jnp.bfloat16
VMEM_LIMIT = 62 * 2**20
WIDE = 256
STEP = 16
G1, B1, BOUT, G2, B2, BDOWN, BQV, BUP = 0, 1, 2, 3, 4, 5, 6, 8
SMALL = 16
PIECES = dict(qkv=2, out=1, up=2, down=2)
WIDER = ((0, "down", 0), (0, "down", 1), (1, "down", 0))


def nn(a, b):
    return lax.dot_general(a, b, (((1,), (0,)), ((), ())), preferred_element_type=F32)


def nt(a, b):
    return lax.dot_general(a, b, (((1,), (1,)), ((), ())), preferred_element_type=F32)


def tn(a, b):
    return lax.dot_general(a, b, (((0,), (0,)), ((), ())), preferred_element_type=F32)


def span(start, size):
    return pl.ds(pl.multiple_of(start, size), size)


def cols(j, width=WIDE):
    return span(j * width, width)


def loop(count, body):
    def step(j, carry):
        body(j)
        return carry

    lax.fori_loop(0, count, step, 0)


class Place:
    def __init__(self):
        self.rep, self.grp = lax.axis_index("rep"), lax.axis_index("grp")
        rep, grp = self.rep, self.grp
        self.x, self.c = grp // 2, grp % 2
        self.y, self.z = rep % 2, (rep // 2) % 4
        self.zlow = self.z % 2
        core, chip = 1 - 2 * self.c, 2 - 4 * self.x
        self.sib = (rep, grp + core)
        self.xn = (rep, grp + chip)
        self.xd = (rep, grp + chip + core)
        yrep = rep + 1 - 2 * self.y
        self.yn = (yrep, grp)
        self.yd = (yrep, grp + core)
        self.zn = (rep + 2 - 4 * self.zlow, grp)
        self.inn = ((self.z + 1) // 2) % 2
        self.inner = self.inn == 1
        self.outer = self.inn == 0
        self.mid = (rep + 6 - 4 * self.z, grp)


def greet(peers):
    barrier = pltpu.get_barrier_semaphore()
    for peer in peers:
        pl.semaphore_signal(barrier, inc=1, device_id=peer, device_id_type=MESH)
    pl.semaphore_wait(barrier, len(peers))


def remote(src, dst, send, recv, peer):
    return pltpu.make_async_remote_copy(
        src_ref=src, dst_ref=dst, send_sem=send, recv_sem=recv, device_id=peer, device_id_type=MESH
    )


def settle(ref, sem):
    pltpu.make_async_copy(ref, ref, sem).wait()


def norm_rows(v):
    mean = jnp.mean(v, axis=-1, keepdims=True)
    off = v - mean
    rstd = lax.rsqrt(jnp.mean(off * off, axis=-1, keepdims=True) + 1e-6)
    return off * rstd, rstd


def scores_t(k2, qa, mask):
    st = jnp.where(mask, nt(k2, qa), -1e9)
    top = jnp.max(st, axis=0, keepdims=True)
    e = jnp.exp(st - top)
    return e * (1.0 / jnp.sum(e, axis=0, keepdims=True))


def half_lanes(v, a):
    lane = lax.broadcasted_iota(jnp.int32, v.shape, 1)
    return jnp.where((lane >= HEAD) == (a == 1), v, jnp.zeros_like(v))


def chip_flags(at, tv_ref, rows, seq):
    lengths = jnp.sum(tv_ref[...], axis=1, keepdims=True)
    length = jnp.where(at.x == 0, lengths[0:1, :], lengths[1:2, :])
    row = lax.broadcasted_iota(jnp.int32, (2 * rows, 1), 0)
    core = jnp.where(row < rows, at.c, 1 - at.c)
    row = jnp.where(row < rows, row, row - rows)
    block = rows // 2
    chip = jnp.where(row < block, at.x, 1 - at.x)
    row = jnp.where(row < block, row, row - block)
    slot = (2 * chip + core) * seq + row
    return jnp.logical_and(row < seq, slot < length)


class Plan:
    def __init__(self):
        self.now, self.events, self.done = 0.0, [], set()

    def add(self, when, name, action):
        self.events.append((when, name, action))

    def order(self):
        self.events.sort(key=lambda e: e[0])

    def poll(self):
        while self.events and self.events[0][0] <= self.now:
            self.fire()

    def fire(self):
        when, name, action = self.events.pop(0)
        self.now = max(self.now, when)
        action()
        self.done.add(name)

    def need(self, name):
        while name not in self.done:
            self.fire()

    def spend(self, us):
        self.now += us
        self.poll()


KINDS = ("qkv", "out", "up", "down")


def fwd_kernel(
    seq, tok_in, cot_in, g1_in, b1_in, bo_in, g2_in, b2_in, bd_in, bqv_in, bup_in, tv_ref, iv_ref, wqkv_in, wout_in, wup_in, wdown_in,
    vqkv, vout, vup, vdown, xs, x2s, h1s, qkvs, as_, h2s, zs, gps, dm_out, act_out, vec_out,
    wqkv, wout, wup, wdown, x_ref, x2_ref, h1, qkv, att, h2, z, gp, put, got, tok, vec, bup, cot, dm, pack_ref, tok_ref, cot_ref,
    s_rx, s_ry, s_rz, s_ra, s_rb, s_rs, s_loc, s_send, s_core, r_core, s_save, s_misc, r_misc,
):
    at = Place()
    layers = vqkv.shape[0]
    rows, d = x_ref.shape
    block = rows // 2
    hc, f = att.shape[1], z.shape[1]
    own, other = pl.ds(0, rows), pl.ds(rows, rows)
    x, c = at.x, at.c
    quarter = at.y * 2 + at.zlow
    ins = dict(qkv=wqkv_in, out=wout_in, up=wup_in, down=wdown_in)
    full = dict(qkv=wqkv, out=wout, up=wup, down=wdown)
    saves = dict(qkv=vqkv, out=vout, up=vup, down=vdown)
    runs = dict(qkv=(d // 4, 6), up=(f // 2, 2))
    plan = Plan()
    index = {}
    piece_index = {}
    for l in range(layers):
        for kind in KINDS:
            index[l, kind] = len(index)
            for p in range(PIECES[kind]):
                piece_index[l, kind, p] = len(piece_index)

    for src, dst in ((tok_in, tok_ref), (cot_in, cot_ref)):
        for i in range(2):
            dst[i, seq // STEP * STEP:, :] = jnp.zeros((block - seq // STEP * STEP, d), BF16)
            dst[i, 0:seq, :] = src[:, i, :]
    at_row = 0
    for ref in (g1_in, b1_in, bo_in, g2_in, b2_in, bd_in, bqv_in, bup_in):
        values = ref[...].astype(F32)
        for j in range(ref.shape[1] // WIDE):
            for l in range(layers):
                pack_ref[l * SMALL + at_row:l * SMALL + at_row + 1, :] = values[l:l + 1, j * WIDE:(j + 1) * WIDE]
            at_row += 1
    for l in range(layers):
        pack_ref[l * SMALL + at_row:(l + 1) * SMALL, :] = jnp.zeros((SMALL - at_row, WIDE), F32)
    greet((at.sib, at.xn, at.xd, at.yn, at.zn))

    here = vec.at[:, span(at.grp * WIDE, WIDE)]
    packs = [
        pltpu.make_async_copy(pack_ref, here, s_misc.at[4]),
        remote(pack_ref, here, s_misc.at[5], r_misc.at[5], at.sib),
        remote(pack_ref, here, s_misc.at[6], r_misc.at[6], at.xn),
        remote(pack_ref, here, s_misc.at[7], r_misc.at[7], at.xd),
    ]
    for copy in packs:
        copy.start()

    def quarter_rows(kind):
        return full[kind].shape[2] // PIECES[kind] // 4

    def part_of(kind, p, first, count=4, of=1):
        q = quarter_rows(kind) // of
        return span(4 * of * p * q + first * q, q) if count == 1 else pl.ds(4 * p * q, count * q)

    def wider_parts(kind, p, y, zlow):
        return part_of(kind, p, y, 1), part_of(kind, p, 2 + zlow, 1)

    def launch(l, kind, p):
        w, i = index[l, kind], piece_index[l, kind, p]
        src, dst = ins[kind].at[l], full[kind].at[l]
        part = part_of(kind, p, quarter, 1)
        if kind in runs:
            width, count = runs[kind]
            mine = 2 * x + c
            for j in range(count):
                to = pl.ds(j * width, width)
                keep = span((2 * j + c) * width, width)
                give = span((2 * j + 1 - c) * width, width)
                remote(src.at[part, keep], dst.at[mine, part, to], s_send.at[w], s_rx.at[i], at.xn).start()
                remote(src.at[part, give], dst.at[mine, part, to], s_send.at[w], s_rx.at[i], at.xd).start()
                if p == 0:
                    remote(src.at[:, give], dst.at[mine, :, to], s_send.at[w], s_rs.at[w], at.sib).start()
                    pltpu.make_async_copy(src.at[:, keep], dst.at[mine, :, to], s_loc.at[w]).start()
        else:
            for part in wider_parts(kind, p, at.y, at.zlow) if (l, kind, p) in WIDER else (part,):
                remote(src.at[part], dst.at[x, part], s_send.at[w], s_rx.at[i], at.xn).start()
            if p == 0:
                pltpu.make_async_copy(src, dst.at[x], s_loc.at[w]).start()

    def theirs(l, kind, part):
        dst = full[kind].at[l]
        if kind in runs:
            return dst.at[span(2 * (1 - x), 2), part]
        return dst.at[pl.ds(1 - x, 1), part]

    link = dict(x=4.0, y=0.0, z=0.0)

    def travel(name, us):
        link[name] = max(plan.now, link[name]) + us
        return link[name] + 2.5

    def hop(kind):
        shape = full[kind].shape
        return 2 * shape[1] * shape[2] * shape[3] / 2**20 / PIECES[kind] / 4 / 0.094 * 1.05

    def relay1(l, kind, p):
        key = (l, kind, p)
        w, i = index[l, kind], piece_index[key]
        if key in WIDER:
            settle(theirs(l, kind, part_of(kind, p, 0, 2)), s_rx.at[i])
            to_y, to_z = (theirs(l, kind, part) for part in wider_parts(kind, p, at.y, at.zlow))
        else:
            to_y = to_z = theirs(l, kind, part_of(kind, p, quarter, 1))
            settle(to_y, s_rx.at[i])
        remote(to_y, to_y, s_send.at[w], s_ry.at[i], at.yn).start()
        remote(to_z, to_z, s_send.at[w], s_rz.at[i], at.zn).start()
        t = max(travel("y", hop(kind)), travel("z", hop(kind)))
        if key in WIDER:
            plan.add(t, ("ok", *key), functools.partial(arrived, *key))
        else:
            plan.add(t, ("r2", *key), functools.partial(relay2, *key))
        plan.order()

    def relay2(l, kind, p):
        key = (l, kind, p)
        w, i = index[l, kind], piece_index[key]
        from_y, from_z = 2 * (1 - at.y) + at.zlow, 2 * at.y + 1 - at.zlow
        settle(theirs(l, kind, part_of(kind, p, from_y, 1)), s_ry.at[i])
        piece = theirs(l, kind, part_of(kind, p, 2 * from_y, 1, 2))
        remote(piece, piece, s_send.at[w], s_ra.at[i], at.zn).start()
        settle(theirs(l, kind, part_of(kind, p, from_z, 1)), s_rz.at[i])
        piece = theirs(l, kind, part_of(kind, p, 2 * from_z + 1, 1, 2))
        remote(piece, piece, s_send.at[w], s_rb.at[i], at.yn).start()
        t = max(travel("y", hop(kind) / 2), travel("z", hop(kind) / 2))
        plan.add(t, ("ok", *key), functools.partial(arrived, *key))
        plan.order()

    def arrived(l, kind, p):
        key = (l, kind, p)
        i = piece_index[key]
        if key in WIDER:
            by_y, by_z = (theirs(l, kind, part) for part in wider_parts(kind, p, 1 - at.y, 1 - at.zlow))
            settle(by_y, s_ry.at[i])
            settle(by_z, s_rz.at[i])
        else:
            far = 2 * (1 - at.y) + 1 - at.zlow
            settle(theirs(l, kind, part_of(kind, p, 2 * far, 1, 2)), s_ra.at[i])
            settle(theirs(l, kind, part_of(kind, p, 2 * far + 1, 1, 2)), s_rb.at[i])

    def have(l, kind):
        for p in range(PIECES[kind]):
            plan.need(("ok", l, kind, p))
        w = index[l, kind]
        if kind in runs:
            settle(full[kind].at[l, 0], s_rs.at[w])
        settle(full[kind].at[l, 0], s_loc.at[w])
        pltpu.make_async_copy(full[kind].at[l], saves[kind].at[l], s_loc.at[w]).start()

    tokens = [
        remote(tok_ref.at[1 - x], tok.at[1], s_misc.at[0], r_misc.at[0], at.xn),
        pltpu.make_async_copy(tok_ref.at[x], tok.at[0], s_misc.at[3]),
    ]
    for key in piece_index:
        if key[:2] == (0, "up") and key[2] == 0:
            for copy in tokens:
                copy.start()
            token_time = travel("x", 7.3)
        launch(*key)
        t = travel("x", hop(key[1]) * (2 if key in WIDER else 1))
        plan.add(t, ("r1", *key), functools.partial(relay1, *key))
    x_time = travel("x", 7.3)
    late = [
        remote(cot_ref.at[1 - x], cot.at[1], s_misc.at[1], r_misc.at[1], at.xn),
        pltpu.make_async_copy(cot_ref.at[x], cot.at[0], s_misc.at[8]),
    ]
    for copy in late:
        copy.start()
    mask = chip_flags(at, tv_ref, rows, seq)
    saved = []

    def seed():
        for copy in late:
            copy.wait()
        valid = jnp.where(x == 0, iv_ref[0:1, 0:1], iv_ref[0:1, 1:2]).astype(F32)
        weight = mask[:rows].astype(F32) * valid
        for i in range(2):
            for j in range(block // STEP):
                r = i * block + j * STEP
                dm[pl.ds(r, STEP), :] = (
                    cot[i, pl.ds(j * STEP, STEP), :].astype(F32) * weight[r:r + STEP, :]
                ).astype(BF16)
        copy = remote(dm.at[own], dm.at[other], s_misc.at[2], r_misc.at[2], at.sib)
        copy.start()
        saved.append(copy)

    def seeded():
        saved[0].wait()
        copy = pltpu.make_async_copy(dm, dm_out, s_misc.at[10])
        copy.start()
        saved.append(copy)

    plan.add(x_time, "seed", seed)
    plan.add(x_time + 5, "seeded", seeded)
    plan.order()

    for copy in packs:
        copy.wait()
    vec_save = pltpu.make_async_copy(vec, vec_out, s_misc.at[9])
    vec_save.start()
    for l in range(layers):
        for j in range(f // WIDE):
            half, sub = divmod(j, f // WIDE // 2)
            bup[l:l + 1, pl.ds(j * WIDE, WIDE)] = vec[
                l * SMALL + BUP + sub:l * SMALL + BUP + sub + 1, span((2 * half + c) * WIDE, WIDE)
            ]
    plan.now = token_time
    plan.poll()
    for copy in tokens:
        copy.wait()
    for i in range(2):
        for j in range(block // STEP):
            x_ref[pl.ds(i * block + j * STEP, STEP), :] = tok[i, pl.ds(j * STEP, STEP), :].astype(F32)
    plan.spend(1)

    def save(src, dst, slot):
        copy = pltpu.make_async_copy(src, dst, s_save.at[slot])
        copy.start()
        return copy

    pending = {}
    for l in range(layers):
        def row(name, l=l):
            return vec[l * SMALL + name:l * SMALL + name + 1, :]

        def norm_out(src_ref, dst_ref, gain, shift, l=l):
            for i in range(rows // STEP):
                r = pl.ds(i * STEP, STEP)
                hat, _ = norm_rows(src_ref[r, :])
                dst_ref[r, :] = (hat * row(gain) + row(shift)).astype(BF16)

        def weight(kind, cs, l=l):
            w = full[kind][l, :, :, cs]
            return w.reshape(w.shape[0] * w.shape[1], w.shape[2])

        norm_out(x_ref, h1, G1, B1)
        cp = remote(h1.at[own], h1.at[other], s_core.at[0], r_core.at[0], at.sib)
        cp.start()
        x_saved = save(x_ref, xs.at[l], 0)
        plan.spend(2)
        have(l, "qkv")
        if l:
            pending["qkv"].wait()
        bq = jnp.where(c == 0, row(BQV), vec[l * SMALL + BQV + 1:l * SMALL + BQV + 2, :])
        scale = HEAD ** -0.5
        parts = (
            (0, bq[:, :hc] * scale, scale), (hc, jnp.zeros((1, hc), F32), 1.0), (2 * hc, bq[:, hc:], 1.0)
        )

        def qkv_rows(r, l=l, parts=parts):
            for base, bias, factor in parts:
                for j in range(hc // WIDE):
                    cs = pl.ds(base + j * WIDE, WIDE)
                    out = nn(h1[r, :], weight("qkv", cs))
                    qkv[r, cs] = (out * factor + bias[:, j * WIDE:(j + 1) * WIDE]).astype(BF16)
                    plan.spend(0.35)

        qkv_rows(own)
        cp.wait()
        qkv_rows(other)
        h1_saved = save(h1, h1s.at[l], 1)
        pending["qkv"] = save(qkv, qkvs.at[l], 2)
        if l:
            pending["att"].wait()
        for p in range(hc // 128):
            q2 = qkv[:, p * 128:(p + 1) * 128]
            k2 = qkv[:, hc + p * 128:hc + (p + 1) * 128]
            v2 = qkv[:, 2 * hc + p * 128:2 * hc + (p + 1) * 128]
            vt = v2.T
            outs = []
            for a in range(2):
                pt = scores_t(k2, half_lanes(q2, a), mask)
                outs.append(nn(vt[a * HEAD:(a + 1) * HEAD, :], pt.astype(BF16)))
                plan.spend(1.4)
            att[:, p * 128:(p + 1) * 128] = jnp.concatenate(outs, axis=0).T.astype(BF16)
        pending["att"] = save(att, as_.at[l], 3)

        def exchange(left, kind, base, bias, out, slot):
            def far(j):
                put[:, cols(j)] = nn(left[other, :], weight(kind, cols(j))).astype(BF16)

            loop(d // WIDE, far)
            cp = remote(put, got.at[slot], s_core.at[1], r_core.at[1], at.sib)
            cp.start()
            plan.spend(1)

            def near(j):
                out[:, cols(j)] = nn(left[own, :], weight(kind, cols(j))) + base[:, cols(j)] + vec[
                    l * SMALL + bias:l * SMALL + bias + 1, cols(j)
                ]

            loop(d // WIDE, near)
            plan.spend(1)
            cp.wait()
            out[...] += got[slot].astype(F32)
            plan.spend(1)

        have(l, "out")
        if l:
            pending["x2"].wait()
        exchange(att, "out", x_ref, BOUT, x2_ref, 0)
        pending["x2"] = save(x2_ref, x2s.at[l], 4)
        norm_out(x2_ref, h2, G2, B2)
        cp = remote(h2.at[own], h2.at[other], s_core.at[2], r_core.at[2], at.sib)
        cp.start()
        plan.spend(2)
        have(l, "up")
        if l:
            pending["z"].wait()
            pending["gp"].wait()

        def up_rows(r):
            def body(j):
                u = nn(h2[r, :], weight("up", cols(j))) + bup[l:l + 1, cols(j)]
                phi = 0.5 + 0.5 * lax.erf(u * 0.7071067811865476)
                z[r, cols(j)] = (u * phi).astype(BF16)
                gp[r, cols(j)] = (phi + u * jnp.exp(u * u * -0.5) * 0.3989422804014327).astype(BF16)

            for part in range(2):
                loop(f // WIDE // 2, lambda j: body(j + part * (f // WIDE // 2)))
                plan.spend(1.9)

        up_rows(own)
        cp.wait()
        up_rows(other)
        h2_saved = save(h2, h2s.at[l], 5)
        pending["z"] = save(z, zs.at[l], 6)
        pending["gp"] = save(gp, gps.at[l], 7)
        have(l, "down")
        for copy in (x_saved, h1_saved, h2_saved):
            copy.wait()
        exchange(z, "down", x2_ref, BDOWN, x_ref, 1)

    for i in range(2):
        for j in range(block // STEP):
            tok[i, pl.ds(j * STEP, STEP), :] = x_ref[pl.ds(i * block + j * STEP, STEP), :].astype(BF16)
    act = pltpu.make_async_copy(tok, act_out, s_misc.at[11])
    act.start()
    while plan.events:
        plan.fire()
    for copy in (act, vec_save, saved[1]):
        copy.wait()
    for name in ("qkv", "att", "x2", "z", "gp"):
        pending[name].wait()
    for (l, kind), i in index.items():
        settle(full[kind].at[l, pl.ds(0, 3 if kind in runs else 1)], s_send.at[i])
        settle(full[kind].at[l], s_loc.at[i])


ANY = pl.BlockSpec(memory_space=pl.ANY)
VM = pl.BlockSpec(memory_space=pltpu.VMEM)


def dma(*shape):
    return pltpu.SemaphoreType.DMA(shape)


def run_fwd(tok, cot, smalls, tv, iv, w_qkv, w_out, w_up, w_down, seq):
    layers, n, d3 = w_qkv.shape
    d = d3 // 3
    hc, f = d // 2, 2 * w_down.shape[1]
    block = -(-seq // 32) * 32
    rows, both = 2 * block, 4 * block
    weights = [(4, n, 3 * hc), (2, n, d), (4, n, f), (2, w_down.shape[1], d)]
    acts = [
        ((rows, d), F32), ((rows, d), F32), ((both, d), BF16), ((both, 3 * hc), BF16),
        ((both, hc), BF16), ((both, d), BF16), ((both, f), BF16), ((both, f), BF16),
    ]
    shapes = [((layers, *s), BF16) for s in weights] + [((layers, *s), t) for s, t in acts]
    shapes += [((both, d), BF16), ((2, block, d), BF16), ((layers * SMALL, d), F32)]
    count, pieces = layers * len(KINDS), layers * sum(PIECES.values())
    return pl.pallas_call(
        functools.partial(fwd_kernel, seq),
        out_shape=[jax.ShapeDtypeStruct(s, t) for s, t in shapes],
        in_specs=[VM] * 12 + [ANY] * 4,
        out_specs=[ANY] * len(shapes),
        scratch_shapes=[pltpu.VMEM((layers, *s), BF16) for s in weights]
        + [pltpu.VMEM(s, t) for s, t in acts]
        + [
            pltpu.VMEM((rows, d), BF16), pltpu.VMEM((2, rows, d), BF16),
            pltpu.VMEM((2, block, d), BF16), pltpu.VMEM((layers * SMALL, d), F32), pltpu.VMEM((8, f), F32),
            pltpu.VMEM((2, block, d), BF16), pltpu.VMEM((both, d), BF16), pltpu.VMEM((layers * SMALL, WIDE), F32),
            pltpu.VMEM((2, block, d), BF16), pltpu.VMEM((2, block, d), BF16),
        ]
        + [dma(pieces)] * 5
        + [dma(count)] * 3
        + [dma(3), dma(3), dma(8), dma(12), dma(8)],
        compiler_params=pltpu.CompilerParams(
            collective_id=1, has_side_effects=True, vmem_limit_bytes=VMEM_LIMIT
        ),
        cost_estimate=pl.CostEstimate(flops=17 * 10**9, bytes_accessed=80 * 10**6, transcendentals=0),
        name="forward",
    )(tok, cot, *smalls, tv, iv, w_qkv, w_out, w_up, w_down)


LINK, HOP, STAGE = 11.5, 2.5, 0.6
NS, NY, NZ, NT = 6, 3, 3, 6
CHUNK = 256
CROSS = (("down", 1), ("down", 3), ("up", 1))


def chunks_of(layers):
    chunks = []
    for l in reversed(range(layers)):
        chunks += [("down", l, i) for i in range(4)] + [("up", l, i) for i in range(4)]
        chunks += [("out", l, 0)] + [("qkv", l, i) for i in range(3)]
    return chunks + [("small", 0, 0)]


def crossed(chunk):
    return (chunk[0], chunk[2]) in CROSS


def units_of(chunks):
    units, first, last = [], {}, {}
    for k, (kind, l, i) in enumerate(chunks):
        if crossed(chunks[k]):
            continue
        pieces = {("qkv", 0, 1): (128, 128), ("qkv", 0, 2): (128, 64, 64), ("small", 0, 0): (64,)}
        start = 0
        first[k] = len(units)
        for n in pieces.get((kind, l, i), (CHUNK,)):
            units.append((k, start, n))
            start += n
        last[k] = len(units) - 1
    return units, first, last


class Ring:
    def __init__(self, at, plan, chunks, outs, bufs, sems):
        self.at, self.plan, self.chunks, self.outs = at, plan, chunks, outs
        self.g, self.xr, self.yr, self.zr, self.wr, self.t, self.zd, self.xd, self.yd, self.cd, self.td = bufs
        (self.x_send, self.x_recv, self.y_send, self.y_recv, self.z_send, self.z_recv, self.w_send, self.w_recv,
         self.f_send, self.f_recv) = sems[:10]
        self.d_send, self.d_recv, self.d_out, self.cx, self.cy, self.cz, self.cw, self.cb = sems[10:]
        self.units, self.first, self.last = units_of(chunks)
        self.turn = {k: a for a, k in enumerate(self.first)}
        self.cross = [k for k, chunk in enumerate(chunks) if crossed(chunk)]
        self.count = len(self.units)
        self.link = dict(x=0.0, y=0.0, out=0.0, mid=0.0, back=0.0)
        self.copies, self.done, self.ready = {}, set(), {}

    def size(self, u):
        return self.units[u][2]

    def send(self, links, rows):
        t = max(self.plan.now, *(self.link[name] for name in links)) + LINK * rows / CHUNK
        for name in links:
            self.link[name] = t
        return t + HOP

    def pick(self, limit):
        best = None
        for (stage, u), t in self.ready.items():
            if t > limit or (best and best[0] <= t):
                continue
            ahead = [(stage, u - 1)]
            ahead += {1: [(2, u - NY)], 2: [(3, u - NZ), (6, u - NT)], 3: [(4, u - NZ)], 4: [(5, u - NZ)]}.get(stage, [])
            if all(v < 0 or (other, v) in self.done for other, v in ahead):
                best = (t, stage, u)
        return best

    def step(self, best):
        t, stage, u = best
        del self.ready[stage, u]
        self.plan.now = max(self.plan.now, t) + STAGE
        if stage > 10:
            (self.d2, self.d3, self.d4, self.d5, self.d6, self.d7)[stage - 12](u)
            links, rows = {
                12: (("x",), 128), 13: (("y",), 64), 14: (("mid", "out", "back"), 96), 15: (("y",), 64),
                16: (("out", "back"), 128),
            }.get(stage, (None, 0))
        else:
            (self.s1, self.s2, self.s3, self.s4, self.s5, self.s6)[stage - 1](u)
            links = {1: ("y",), 2: ("out",), 3: ("mid",), 4: ("back",), 5: ("y",)}.get(stage)
            rows = self.size(u) // 2
        self.done.add((stage, u))
        if links:
            self.ready[stage + 1, u] = self.send(links, rows)

    def poll(self):
        while best := self.pick(self.plan.now):
            self.step(best)

    def catch_up(self, stage, u):
        while (stage, u) not in self.done:
            self.step(self.pick(float("inf")))

    def reserve(self, k):
        if k >= NS:
            old = k - NS
            if old in self.turn:
                self.catch_up(2, self.last[old])
            else:
                self.catch_up(14, self.cross.index(old))
        if self.turn.get(k, 0) >= NS:
            self.catch_up(1, self.last[list(self.turn)[self.turn[k] - NS]])

    def launch(self, k):
        if k not in self.turn:
            d = self.cross.index(k)
            self.move(d, 0, self.g.at[k % NS, :, self.rows_of(1 - self.at.inn)], self.zd.at[d], self.at.zn)
            self.ready[12, d] = self.send(("out", "back"), CHUNK)
            return
        a = self.turn[k]
        if a >= NS:
            pl.semaphore_wait(self.cx, 1)
        for u in range(self.first[k], self.last[k] + 1):
            _, start, n = self.units[u]
            copy = remote(
                self.g.at[k % NS, 0, pl.ds(start, n)], self.xr.at[a % NS, pl.ds(start, n)],
                self.x_send.at[u], self.x_recv.at[u], self.at.xn,
            )
            copy.start()
            self.copies["x", u] = copy
            self.ready[1, u] = self.send(("x",), n)

    def rows_of(self, part):
        return span(part * (CHUNK // 2), CHUNK // 2)

    def move(self, d, hop, src, dst, peer):
        copy = remote(src, dst, self.d_send.at[hop, d], self.d_recv.at[hop, d], peer)
        copy.start()
        self.copies[hop, d] = copy

    def d2(self, d):
        slot, mine = self.cross[d] % NS, self.rows_of(self.at.inn)
        self.copies[0, d].wait()
        for hh in range(2):
            self.add(self.g.at[slot, hh, mine], self.zd.at[d, hh], CHUNK // 2)
        self.move(d, 1, self.g.at[slot, 0, mine], self.xd.at[d], self.at.xn)

    def d3(self, d):
        slot, mine, quarter = self.cross[d] % NS, self.rows_of(self.at.inn), CHUNK // 4
        self.copies[1, d].wait()
        self.add(self.g.at[slot, 1, mine], self.xd.at[d], CHUNK // 2)
        give = span((2 * self.at.inn + 1 - self.at.y) * quarter, quarter)
        self.move(d, 2, self.g.at[slot, 1, give], self.yd.at[d], self.at.yn)

    def d4(self, d):
        slot, quarter = self.cross[d] % NS, CHUNK // 4
        t = self.td.at[d, span(self.at.y * quarter, quarter)]
        self.copies[2, d].wait()
        self.add(t, self.yd.at[d], quarter, self.g.at[slot, 1], (2 * self.at.inn + self.at.y) * quarter)
        self.move(d, 3, t, self.cd.at[d], self.at.mid)

    def d5(self, d):
        quarter = CHUNK // 4
        t = self.td.at[d, span(self.at.y * quarter, quarter)]
        self.copies[3, d].wait()
        self.add(t, self.cd.at[d], quarter)
        self.move(d, 4, t, t, self.at.yn)

    def d6(self, d):
        at = self.at
        kind, l, i = self.chunks[self.cross[d]]
        out = self.outs[kind]
        self.copies[4, d].wait()
        if kind == "down":
            dst = out.at[l, span((2 * i + at.inn) * (CHUNK // 2), CHUNK // 2)]
        else:
            width = self.td.shape[2]
            dst = out.at[l, self.rows_of(at.inn), span((2 * (i % 2) + at.c) * width, width)]
        sent = self.d_out.at[d]
        pltpu.make_async_copy(self.td.at[d], dst, sent).start()
        remote(self.td.at[d], dst, sent, self.f_recv.at[KINDS.index(kind)], at.zn).start()

    def d7(self, d):
        settle(self.zd.at[d], self.d_out.at[d])

    def credit(self, sem, u, slots, peer):
        if u + slots < self.count:
            pl.semaphore_signal(sem, inc=1, device_id=peer, device_id_type=MESH)

    def claim(self, sem, u, slots):
        if u >= slots:
            pl.semaphore_wait(sem, 1)

    def add(self, dst, src, count, base=None, base_at=None):
        def body(j):
            r = cols(j, 32)
            b = dst[r, :] if base is None else base[pl.ds(pl.multiple_of(base_at + j * 32, 32), 32), :]
            dst[r, :] = (b.astype(F32) + src[r, :].astype(F32)).astype(BF16)

        loop(count // 32, body)

    def s1(self, u):
        at = self.at
        k, start, n = self.units[u]
        slot, a = k % NS, self.turn[k]
        self.copies["x", u].wait()
        self.add(self.g.at[slot, 1, pl.ds(start, n)], self.xr.at[a % NS, pl.ds(start, n)], n)
        if u == self.last[k] and a + NS < len(self.turn):
            pl.semaphore_signal(self.cx, inc=1, device_id=at.xn, device_id_type=MESH)
        self.claim(self.cy, u, NY)
        copy = remote(
            self.g.at[slot, 1, span(start + (1 - at.y) * (n // 2), n // 2)], self.yr.at[u % NY, pl.ds(0, n // 2)],
            self.y_send.at[u], self.y_recv.at[u % NY], at.yn,
        )
        copy.start()
        self.copies["y", u] = copy

    def part(self, ref, u, slots):
        return ref.at[u % slots, pl.ds(0, self.size(u) // 2)]

    def s2(self, u):
        at = self.at
        k, start, n = self.units[u]
        t = self.part(self.t, u, NT)
        self.copies["y", u].wait()
        self.add(t, self.part(self.yr, u, NY), n // 2, self.g.at[k % NS, 1], start + at.y * (n // 2))
        self.credit(self.cy, u, NY, at.yn)

        @pl.when(at.outer)
        def _():
            self.claim(self.cz, u, NZ)
            remote(t, self.part(self.zr, u, NZ), self.z_send.at[u % NT], self.z_recv.at[u % NZ], at.zn).start()

    def s3(self, u):
        n, at = self.size(u), self.at
        t = self.part(self.t, u, NT)

        @pl.when(at.outer)
        def _():
            settle(t, self.z_send.at[u % NT])

        @pl.when(at.inner)
        def _():
            got = self.part(self.zr, u, NZ)
            settle(got, self.z_recv.at[u % NZ])
            self.add(t, got, n // 2)
            self.credit(self.cz, u, NZ, at.zn)
            self.claim(self.cw, u, NZ)
            remote(t, self.part(self.wr, u, NZ), self.z_send.at[u % NT], self.w_recv.at[u % NZ], at.mid).start()

    def s4(self, u):
        n, at = self.size(u), self.at

        @pl.when(at.inner)
        def _():
            t = self.part(self.t, u, NT)
            got = self.part(self.wr, u, NZ)
            settle(got, self.w_recv.at[u % NZ])
            settle(t, self.z_send.at[u % NT])
            self.add(t, got, n // 2)
            self.credit(self.cw, u, NZ, at.mid)
            self.claim(self.cb, u, NZ)
            remote(t, self.part(self.zr, u, NZ), self.w_send.at[u % NT], self.z_recv.at[u % NZ], at.zn).start()

    def s5(self, u):
        n, at = self.size(u), self.at
        t = self.part(self.t, u, NT)

        @pl.when(at.outer)
        def _():
            got = self.part(self.zr, u, NZ)
            settle(got, self.z_recv.at[u % NZ])

            def body(j):
                t[cols(j, 32), :] = got[cols(j, 32), :]

            loop(n // 64, body)
            self.credit(self.cb, u, NZ, at.zn)

        k, start, n = self.units[u]
        kind, l, i = self.chunks[k]
        out = self.outs[kind]
        sent = self.f_send.at[u % NT]
        if kind == "small":
            pltpu.make_async_copy(t, out, sent).start()
            return
        half = n // 2
        width = t.shape[1]

        def deliver(src, dst, mine, kind_index):
            if mine:
                pltpu.make_async_copy(src, dst, sent).start()
                remote(src, dst, sent, self.f_recv.at[kind_index], at.yn).start()
            else:
                remote(src, dst, sent, self.f_recv.at[kind_index], at.sib).start()
                remote(src, dst, sent, self.f_recv.at[kind_index], at.yd).start()

        if kind in ("down", "out"):
            deliver(t, out.at[l, span(i * CHUNK + start + at.y * half, half)], True, KINDS.index(kind))
        elif kind == "up":
            side, run = divmod(i, 2)
            deliver(t, out.at[l, span(start + at.y * half, half), span((2 * run + at.c) * width, width)], side == 0, 2)
        else:
            for side in range(2):
                for run in range(2):
                    src = t.at[:, pl.ds((2 * side + run) * WIDE, WIDE)]
                    dst = out.at[l, span(start + at.y * half, half), span(i * width + (2 * run + at.c) * WIDE, WIDE)]
                    deliver(src, dst, side == 0, 0)

    def s6(self, u):
        at = self.at
        t = self.part(self.t, u, NT)
        k, _, n = self.units[u]
        settle(t if self.chunks[k][0] == "small" else self.g.at[0, 0, pl.ds(0, n)], self.f_send.at[u % NT])

        @pl.when(at.inner)
        def _():
            settle(t, self.w_send.at[u % NT])

    def finish(self):
        while best := self.pick(float("inf")):
            self.step(best)
        for i, kind in enumerate(KINDS):
            out = self.outs[kind]
            rows = out.shape[1]
            settle(out.at[:, pl.ds(0, rows // 2 if kind in ("out", "down") else rows * 3 // 4)], self.f_recv.at[i])


def bwd_kernel(
    seq, dm_ref, act_ref, vec_ref, tv_ref, vqkv, vout, vup, vdown, xs, x2s, h1s, qkvs, as_, h2s, zs, gps,
    oqkv, oout, oup, odown, osmall, otok, oact,
    wqkv, wout, wup, wdown, x_ref, x2_ref, h1, qkv, att, h2, z, gp,
    g_ref, dm, da, dj, dx2, dh, put, got, small, small_put, small_got, s_load, s_core, r_core, s_misc, r_misc, *rest,
):
    at = Place()
    layers = vqkv.shape[0]
    rows, d = x_ref.shape
    block = rows // 2
    hc, f = att.shape[1], z.shape[1]
    own, other = pl.ds(0, rows), pl.ds(rows, rows)
    x, c = at.x, at.c
    plan = Plan()
    chunks = chunks_of(layers)
    rings, ring_sems = rest[:11], rest[11:]
    ring_g = rings[0]
    ring = Ring(
        at, plan, chunks, dict(qkv=oqkv, out=oout, up=oup, down=odown, small=osmall),
        rings, ring_sems,
    )
    plan.poll = ring.poll
    number = {chunk: u for u, chunk in enumerate(chunks)}

    stores = dict(
        z=(zs, z), wdown=(vdown, wdown), gp=(gps, gp), h2=(h2s, h2), wup=(vup, wup), x2=(x2s, x2_ref),
        wout=(vout, wout), att=(as_, att), qkv=(qkvs, qkv), wqkv=(vqkv, wqkv), h1=(h1s, h1), x=(xs, x_ref),
    )
    slots = {name: i for i, name in enumerate(stores)}
    loads = {}

    def load(name, l):
        if l < 0:
            return
        src, dst = stores[name]
        loads[name, l] = pltpu.make_async_copy(src.at[l], dst, s_load.at[slots[name]])
        loads[name, l].start()

    dm_load = pltpu.make_async_copy(dm_ref, dm.at[0], s_misc.at[0])
    dm_load.start()
    for name in stores:
        load(name, layers - 1)
    greet((at.sib, at.xn, at.yn, at.yd, at.zn, at.mid))

    def by_half(hh):
        return hh * x + (1 - hh) * (1 - x)

    mask = chip_flags(at, tv_ref, rows, seq)
    small[...] = jnp.zeros_like(small)
    act = [
        remote(act_ref.at[1], oact.at[x], s_misc.at[4], r_misc.at[4], at.xn),
        pltpu.make_async_copy(act_ref.at[0], oact.at[x], s_misc.at[5]),
    ]
    for l in reversed(range(layers)):
        def row(name, l=l):
            return vec_ref[l * SMALL + name:l * SMALL + name + 1, :]

        def set_small(name, value, l=l):
            small[l * SMALL + name:l * SMALL + name + 1, :] = value

        def round_rows(src_ref, name, slot):
            total = jnp.zeros((8, d), F32)
            for i in range(rows // STEP):
                r = pl.ds(i * STEP, STEP)
                if src_ref is None:
                    low = dm[slot, r, :].astype(F32)
                    g_ref[r, :] = low
                else:
                    low = src_ref[r, :].astype(BF16)
                    dm[slot, r, :] = low
                    low = low.astype(F32)
                total = total + low[0:8, :] + low[8:16, :]
            set_small(name, jnp.sum(total, axis=0, keepdims=True))

        def send_round(src_ref, name, slot):
            round_rows(src_ref, name, slot)
            copy = remote(dm.at[slot, own], dm.at[slot, other], s_core.at[slot], r_core.at[slot], at.sib)
            copy.start()
            return copy

        def exchange(left, w):
            per = w.shape[1]

            def piece(j):
                b = j // (per // WIDE)
                return w[b, span((j % (per // WIDE)) * WIDE, WIDE), :]

            def far(j):
                put[:, cols(j)] = nt(left[other, :], piece(j)).astype(BF16)

            loop(d // WIDE, far)
            plan.spend(1.5)
            copy = remote(put, got, s_core.at[2], r_core.at[2], at.sib)
            copy.start()

            def near(j):
                dh[:, cols(j)] = nt(left[own, :], piece(j))

            loop(d // WIDE, near)
            plan.spend(1.5)
            copy.wait()
            plan.spend(0.5)

        def norm_back(value_ref, base_ref, out_ref, gain, shift):
            total_g = jnp.zeros((8, d), F32)
            total_b = jnp.zeros((8, d), F32)
            for i in range(rows // STEP):
                r = pl.ds(i * STEP, STEP)
                hat, rstd = norm_rows(value_ref[r, :])
                grad = dh[r, :] + got[r, :].astype(F32)
                prod = grad * hat
                total_g = total_g + prod[0:8, :] + prod[8:16, :]
                total_b = total_b + grad[0:8, :] + grad[8:16, :]
                dhat = grad * row(gain)
                m1 = jnp.mean(dhat, axis=-1, keepdims=True)
                m2 = jnp.mean(dhat * hat, axis=-1, keepdims=True)
                out_ref[r, :] = base_ref[r, :] + rstd * (dhat - m1 - hat * m2)
            set_small(gain, jnp.sum(total_g, axis=0, keepdims=True))
            set_small(shift, jnp.sum(total_b, axis=0, keepdims=True))

        def produce(chunk, maker, us):
            u = number[chunk]
            ring.reserve(u)
            loop(2, lambda hh: maker(ring_g.at[u % NS, hh], by_half(hh)))
            ring.launch(u)
            plan.spend(us)

        if l == layers - 1:
            dm_load.wait()
            loads["z", l].wait()
        else:
            copy = send_round(g_ref, BDOWN, 0)
            loads["z", l].wait()
            plan.spend(2)
            copy.wait()
        for i in range(4):
            def make(dst, h, i=i):
                dst[...] = tn(z[:, span(h * (f // 2) + i * CHUNK, CHUNK)], dm[0]).astype(BF16)

            produce(("down", l, i), make, 1.3)
        if l == layers - 1:
            round_rows(None, BDOWN, 0)
            for copy in act:
                copy.start()
        load("z", l - 1)
        loads["wdown", l].wait()
        loads["gp", l].wait()

        def dz_body(j):
            b = j // (f // 2 // WIDE)
            w = wdown[b, span((j % (f // 2 // WIDE)) * WIDE, WIDE), :]
            for r in (own, other):
                low = (nt(dm[0, r, :], w) * gp[r, cols(j)].astype(F32)).astype(BF16)
                gp[r, cols(j)] = low

        for part in range(2):
            loop(f // WIDE // 2, lambda j: dz_body(j + part * (f // WIDE // 2)))
            plan.spend(2)
        load("wdown", l - 1)
        for j in range(f // WIDE):
            half, sub = divmod(j, f // WIDE // 2)
            small[l * SMALL + BUP + sub:l * SMALL + BUP + sub + 1, span((2 * half + c) * WIDE, WIDE)] = jnp.sum(
                gp[:, j * WIDE:(j + 1) * WIDE].astype(F32), axis=0, keepdims=True
            )
        loads["h2", l].wait()
        loads["wup", l].wait()
        for i in range(4):
            side, run = divmod(i, 2)

            def make(dst, h, side=side, run=run):
                rh = c if side == 0 else 1 - c
                left = h2[:, span(h * (d // 2) + rh * CHUNK, CHUNK)]
                dst[...] = tn(left, gp[:, run * (f // 2):(run + 1) * (f // 2)]).astype(BF16)

            if i == 2:
                exchange(gp, wup)
                load("wup", l - 1)
                loads["x2", l].wait()
                norm_back(x2_ref, g_ref, dx2, G2, B2)
                load("x2", l - 1)
                plan.spend(3)
                copy = send_round(dx2, BOUT, 1)
            produce(("up", l, i), make, 1.3)
        load("gp", l - 1)
        load("h2", l - 1)

        loads["wout", l].wait()
        loads["att", l].wait()
        copy.wait()
        for j in range(hc // WIDE):
            for r in (own, other):
                da[r, pl.ds(j * WIDE, WIDE)] = nt(dm[1, r, :], wout[j]).astype(BF16)
        load("wout", l - 1)

        def make(dst, h):
            dst[...] = tn(att[:, span(h * CHUNK, CHUNK)], dm[1]).astype(BF16)

        produce(("out", l, 0), make, 2)
        load("att", l - 1)
        loads["qkv", l].wait()
        sums = {}
        for p in range(hc // 128):
            cq, ck, cv = (pl.ds(k * hc + p * 128, 128) for k in range(3))
            q2, k2, v2, da2 = qkv[:, cq], qkv[:, ck], qkv[:, cv], da[:, cq]
            kt = k2.T
            dk = dv = None
            parts = []
            for a in range(2):
                qa, daa = half_lanes(q2, a), half_lanes(da2, a)
                pt = scores_t(k2, qa, mask)
                dpt = nt(v2, daa)
                delta = jnp.sum(dpt * pt, axis=0, keepdims=True)
                dst = (pt * (dpt - delta)).astype(BF16)
                dva = nn(pt.astype(BF16), daa)
                dka = nn(dst, qa)
                parts.append(nn(kt[a * HEAD:(a + 1) * HEAD, :], dst))
                dk = dka if dk is None else dk + dka
                dv = dva if dv is None else dv + dva
                plan.spend(2.7)
            dq = (jnp.concatenate(parts, axis=0).T * HEAD ** -0.5).astype(BF16)
            dv = dv.astype(BF16)
            dj[:, cq] = dq
            dj[:, ck] = dk.astype(BF16)
            dj[:, cv] = dv
            for k, value in ((0, dq), (1, dv)):
                total = jnp.sum(value.astype(F32), axis=0, keepdims=True)
                for core in range(2):
                    r = l * SMALL + BQV + core
                    small[r:r + 1, k * hc + p * 128:k * hc + (p + 1) * 128] = jnp.where(
                        c == core, total, jnp.zeros_like(total)
                    )
        load("qkv", l - 1)
        loads["wqkv", l].wait()
        loads["h1", l].wait()
        for i in range(3):
            def make(dst, h, i=i):
                for side in range(2):
                    rh = c if side == 0 else 1 - c
                    left = h1[:, span(h * (d // 2) + rh * CHUNK, CHUNK)]
                    dst[:, side * hc:(side + 1) * hc] = tn(left, dj[:, i * hc:(i + 1) * hc]).astype(BF16)

            if i == 1:
                exchange(dj, wqkv)
                load("wqkv", l - 1)
                loads["x", l].wait()
                norm_back(x_ref, dx2, g_ref, G1, B1)
                load("x", l - 1)
                plan.spend(3)
            produce(("qkv", l, i), make, 1.3)
        load("h1", l - 1)

    for j in range(rows // STEP):
        put[pl.ds(j * STEP, STEP), :] = g_ref[pl.ds(j * STEP, STEP), :].astype(BF16)
    back = [
        remote(put.at[pl.ds(block, block)], otok.at[x], s_misc.at[1], r_misc.at[1], at.xn),
        pltpu.make_async_copy(put.at[pl.ds(0, block)], otok.at[x], s_misc.at[2]),
    ]
    small_put[...] = small[...].astype(BF16)
    copy = remote(small_put, small_got, s_misc.at[3], r_misc.at[3], at.sib)
    copy.start()
    copy.wait()
    total = (small_put[...].astype(F32) + small_got[...].astype(F32)).astype(BF16)
    u = number["small", 0, 0]
    ring.reserve(u)
    n = total.shape[0]
    for hh in range(2):
        for k in range(2):
            ring_g[u % NS, hh, k * n:(k + 1) * n, :] = total
    ring.launch(u)
    for copy in back:
        copy.start()
    ring.finish()
    for copy in (*back, *act):
        copy.wait()


def run_bwd(dm, act, vec, tv, weights, acts, seq):
    layers, _, n, hc3 = weights[0].shape
    d = acts[0].shape[2]
    rows = acts[0].shape[1]
    block, both = rows // 2, 2 * rows
    hc, f = hc3 // 3, weights[2].shape[3]
    chunks = chunks_of(layers)
    units = len(units_of(chunks)[0])
    crosses = sum(crossed(chunk) for chunk in chunks)
    outs = [(layers, n, 3 * d), (layers, n, d), (layers, n, 2 * f), (layers, f // 2, d), (layers * SMALL, d)]
    outs += [(2, block, d)] * 2
    args = (dm, act, vec, tv, *weights, *acts)
    return pl.pallas_call(
        functools.partial(bwd_kernel, seq),
        out_shape=[jax.ShapeDtypeStruct(s, BF16) for s in outs],
        in_specs=[ANY, ANY, VM, VM] + [ANY] * 12,
        out_specs=[ANY] * len(outs),
        scratch_shapes=[pltpu.VMEM(w.shape[1:], w.dtype) for w in (*weights, *acts)]
        + [
            pltpu.VMEM((rows, d), F32), pltpu.VMEM((2, both, d), BF16),
            pltpu.VMEM((both, hc), BF16), pltpu.VMEM((both, 3 * hc), BF16), pltpu.VMEM((rows, d), F32),
            pltpu.VMEM((rows, d), F32), pltpu.VMEM((rows, d), BF16), pltpu.VMEM((rows, d), BF16),
            pltpu.VMEM((layers * SMALL, d), F32), pltpu.VMEM((layers * SMALL, d), BF16),
            pltpu.VMEM((layers * SMALL, d), BF16),
            dma(12), dma(3), dma(3), dma(6), dma(6),
            pltpu.VMEM((NS, 2, CHUNK, d), BF16), pltpu.VMEM((NS, CHUNK, d), BF16),
            pltpu.VMEM((NY, CHUNK // 2, d), BF16), pltpu.VMEM((NZ, CHUNK // 2, d), BF16),
            pltpu.VMEM((NZ, CHUNK // 2, d), BF16), pltpu.VMEM((NT, CHUNK // 2, d), BF16),
            pltpu.VMEM((crosses, 2, CHUNK // 2, d), BF16), pltpu.VMEM((crosses, CHUNK // 2, d), BF16),
            pltpu.VMEM((crosses, CHUNK // 4, d), BF16), pltpu.VMEM((crosses, CHUNK // 4, d), BF16),
            pltpu.VMEM((crosses, CHUNK // 2, d), BF16),
            dma(units), dma(units), dma(units), dma(NY), dma(NT), dma(NZ), dma(NT), dma(NZ), dma(NT), dma(4),
            dma(5, crosses), dma(5, crosses), dma(crosses),
        ]
        + [pltpu.SemaphoreType.REGULAR] * 5,
        compiler_params=pltpu.CompilerParams(
            collective_id=2, has_side_effects=True, vmem_limit_bytes=VMEM_LIMIT
        ),
        cost_estimate=pl.CostEstimate(flops=34 * 10**9, bytes_accessed=120 * 10**6, transcendentals=0),
        name="backward",
    )(*args)


def finish_kernel(gqkv, gout, gup, gdown, small, act, gtok, oact, ogtok, oqkv, oout, oup, odown, *vectors):
    seq = oact.shape[0]

    @pl.when(jnp.logical_and(pl.program_id(0) == 0, pl.program_id(1) == 0))
    def _():
        for src, dst in ((act, oact), (gtok, ogtok)):
            dst[...] = jnp.stack([src[0, :seq, :], src[1, :seq, :]], axis=1)

    for src, dst in ((gqkv, oqkv), (gout, oout), (gup, oup), (gdown, odown)):
        dst[...] = src[...].astype(F32)
    mine = span(lax.axis_index("grp") * WIDE, WIDE)
    layers = vectors[0].shape[0]
    rows = [small[l * SMALL:(l + 1) * SMALL, mine].astype(F32) for l in range(layers)]
    at = 0
    for out in vectors:
        for j in range(out.shape[1] // WIDE):
            for l in range(layers):
                out[l:l + 1, j * WIDE:(j + 1) * WIDE] = rows[l][at:at + 1, :]
            at += 1


def run_finish(gqkv, gout, gup, gdown, small, act, gtok, seq, widths):
    bigs = (gqkv, gout, gup, gdown)
    layers = gqkv.shape[0]
    steps = 2

    def big(g):
        return pl.BlockSpec((1, g.shape[1] // steps, g.shape[2]), lambda l, s: (l, s, 0))

    def flat(shape):
        return pl.BlockSpec(shape, lambda l, s: (0,) * len(shape))

    rows = [(seq, act.shape[0], act.shape[2])] * 2
    vectors = [(layers, w) for w in widths]
    return pl.pallas_call(
        finish_kernel,
        grid=(layers, steps),
        out_shape=[jax.ShapeDtypeStruct(r, BF16) for r in rows]
        + [jax.ShapeDtypeStruct(g.shape, F32) for g in bigs]
        + [jax.ShapeDtypeStruct(v, F32) for v in vectors],
        in_specs=[big(g) for g in bigs] + [flat(small.shape), flat(act.shape), flat(gtok.shape)],
        out_specs=[flat(r) for r in rows] + [big(g) for g in bigs] + [flat(v) for v in vectors],
        compiler_params=pltpu.CompilerParams(vmem_limit_bytes=VMEM_LIMIT),
        name="finish",
    )(*bigs, small, act, gtok)


def local(
    tokens, cotangent, image_valid, token_valid,
    norm1_gain, norm1_bias, w_qkv, b_qv, w_out, b_out, norm2_gain, norm2_bias, w_up, b_up, w_down, b_down,
):
    seq = tokens.shape[1]
    smalls = (norm1_gain, norm1_bias, b_out, norm2_gain, norm2_bias, b_down, b_qv, b_up)
    res = run_fwd(
        tokens.transpose(1, 0, 2), cotangent.transpose(1, 0, 2), smalls, token_valid, image_valid[None, :], w_qkv, w_out, w_up, w_down, seq
    )
    weights, acts, (dm, act, vec) = res[:4], res[4:12], res[12:]
    gqkv, gout, gup, gdown, gsmall, gtok, act = run_bwd(dm, act, vec, token_valid, weights, acts, seq)
    blocks = lax.axis_size("rep") // 8
    if blocks > 1:
        groups = [[i + 8 * b for b in range(blocks)] for i in range(8)]
        gqkv, gout, gup, gdown, gsmall = (
            lax.psum(g, "rep", axis_index_groups=groups) for g in (gqkv, gout, gup, gdown, gsmall)
        )
    act, gtok, gqkv, gout, gup, gdown, *vectors = run_finish(
        gqkv, gout, gup, gdown, gsmall, act, gtok, seq, [w.shape[1] for w in smalls]
    )
    act, gtok = act.transpose(1, 0, 2), gtok.transpose(1, 0, 2)
    gg1, gb1, gbout, gg2, gb2, gbdown, gbqv, gbup = vectors
    return (
        act, gtok, gg1, gb1, gqkv, gbqv, gout, gbout, gg2, gb2, gup, gbup, gdown, gbdown,
    )


def solution(mesh):
    rows3, mat, vec = P("rep", "grp", None), P(None, "grp", None), P(None, "grp")
    weights = (vec, vec, mat, vec, mat, vec, vec, vec, mat, vec, mat, vec)
    return jax.shard_map(
        local,
        mesh=mesh,
        in_specs=(rows3, rows3, P("rep"), P("rep", None)) + weights,
        out_specs=(rows3, rows3) + weights,
        check_vma=False,
    )
```

```python
import functools

import jax
import jax.numpy as jnp
from jax import lax
from jax.experimental import pallas as pl
from jax.experimental.pallas import tpu as pltpu
from jax.sharding import PartitionSpec as P

HEAD = 64
MESH = pl.DeviceIdType.MESH
F32 = jnp.float32
BF16 = jnp.bfloat16
VMEM_LIMIT = 62 * 2**20
WIDE = 256
STEP = 16
G1, B1, BOUT, G2, B2, BDOWN, BQV, BUP = 0, 1, 2, 3, 4, 5, 6, 8
SMALL = 16
PIECES = dict(qkv=2, out=1, up=2, down=2)
WIDER = ((0, "down", 0), (0, "down", 1), (1, "down", 0))


def nn(a, b):
    return lax.dot_general(a, b, (((1,), (0,)), ((), ())), preferred_element_type=F32)


def nt(a, b):
    return lax.dot_general(a, b, (((1,), (1,)), ((), ())), preferred_element_type=F32)


def tn(a, b):
    return lax.dot_general(a, b, (((0,), (0,)), ((), ())), preferred_element_type=F32)


def span(start, size):
    return pl.ds(pl.multiple_of(start, size), size)


def cols(j, width=WIDE):
    return span(j * width, width)


def loop(count, body):
    def step(j, carry):
        body(j)
        return carry

    lax.fori_loop(0, count, step, 0)


class Place:
    def __init__(self):
        self.rep, self.grp = lax.axis_index("rep"), lax.axis_index("grp")
        rep, grp = self.rep, self.grp
        self.x, self.c = grp // 2, grp % 2
        self.y, self.z = rep % 2, (rep // 2) % 4
        self.zlow = self.z % 2
        core, chip = 1 - 2 * self.c, 2 - 4 * self.x
        self.sib = (rep, grp + core)
        self.xn = (rep, grp + chip)
        self.xd = (rep, grp + chip + core)
        yrep = rep + 1 - 2 * self.y
        self.yn = (yrep, grp)
        self.yd = (yrep, grp + core)
        self.zn = (rep + 2 - 4 * self.zlow, grp)
        self.inn = ((self.z + 1) // 2) % 2
        self.inner = self.inn == 1
        self.outer = self.inn == 0
        self.mid = (rep + 6 - 4 * self.z, grp)


def greet(peers):
    barrier = pltpu.get_barrier_semaphore()
    for peer in peers:
        pl.semaphore_signal(barrier, inc=1, device_id=peer, device_id_type=MESH)
    pl.semaphore_wait(barrier, len(peers))


def remote(src, dst, send, recv, peer):
    return pltpu.make_async_remote_copy(
        src_ref=src, dst_ref=dst, send_sem=send, recv_sem=recv, device_id=peer, device_id_type=MESH
    )


def settle(ref, sem):
    pltpu.make_async_copy(ref, ref, sem).wait()


def norm_rows(v):
    mean = jnp.mean(v, axis=-1, keepdims=True)
    off = v - mean
    rstd = lax.rsqrt(jnp.mean(off * off, axis=-1, keepdims=True) + 1e-6)
    return off * rstd, rstd


def scores_t(k2, qa, mask):
    st = jnp.where(mask, nt(k2, qa), -1e9)
    top = jnp.max(st, axis=0, keepdims=True)
    e = jnp.exp(st - top)
    return e * (1.0 / jnp.sum(e, axis=0, keepdims=True))


def half_lanes(v, a):
    lane = lax.broadcasted_iota(jnp.int32, v.shape, 1)
    return jnp.where((lane >= HEAD) == (a == 1), v, jnp.zeros_like(v))


def chip_flags(at, tv_ref, rows, seq):
    lengths = jnp.sum(tv_ref[...], axis=1, keepdims=True)
    length = jnp.where(at.x == 0, lengths[0:1, :], lengths[1:2, :])
    row = lax.broadcasted_iota(jnp.int32, (2 * rows, 1), 0)
    core = jnp.where(row < rows, at.c, 1 - at.c)
    row = jnp.where(row < rows, row, row - rows)
    block = rows // 2
    chip = jnp.where(row < block, at.x, 1 - at.x)
    row = jnp.where(row < block, row, row - block)
    slot = (2 * chip + core) * seq + row
    return jnp.logical_and(row < seq, slot < length)


class Plan:
    def __init__(self):
        self.now, self.events, self.done = 0.0, [], set()

    def add(self, when, name, action):
        self.events.append((when, name, action))

    def order(self):
        self.events.sort(key=lambda e: e[0])

    def poll(self):
        while self.events and self.events[0][0] <= self.now:
            self.fire()

    def fire(self):
        when, name, action = self.events.pop(0)
        self.now = max(self.now, when)
        action()
        self.done.add(name)

    def need(self, name):
        while name not in self.done:
            self.fire()

    def spend(self, us):
        self.now += us
        self.poll()


KINDS = ("qkv", "out", "up", "down")


def fwd_kernel(
    seq, tok_in, cot_in, g1_in, b1_in, bo_in, g2_in, b2_in, bd_in, bqv_in, bup_in, tv_ref, iv_ref, wqkv_in, wout_in, wup_in, wdown_in,
    vqkv, vout, vup, vdown, xs, x2s, h1s, qkvs, as_, h2s, zs, gps, dm_out, act_out, vec_out,
    wqkv, wout, wup, wdown, x_ref, x2_ref, h1, qkv, att, h2, z, gp, put, got, tok, vec, bup, cot, dm, pack_ref, tok_ref, cot_ref,
    s_rx, s_ry, s_rz, s_ra, s_rb, s_rs, s_loc, s_send, s_core, r_core, s_save, s_misc, r_misc,
):
    at = Place()
    layers = vqkv.shape[0]
    rows, d = x_ref.shape
    block = rows // 2
    hc, f = att.shape[1], z.shape[1]
    own, other = pl.ds(0, rows), pl.ds(rows, rows)
    x, c = at.x, at.c
    quarter = at.y * 2 + at.zlow
    ins = dict(qkv=wqkv_in, out=wout_in, up=wup_in, down=wdown_in)
    full = dict(qkv=wqkv, out=wout, up=wup, down=wdown)
    saves = dict(qkv=vqkv, out=vout, up=vup, down=vdown)
    runs = dict(qkv=(d // 4, 6), up=(f // 2, 2))
    plan = Plan()
    index = {}
    piece_index = {}
    for l in range(layers):
        for kind in KINDS:
            index[l, kind] = len(index)
            for p in range(PIECES[kind]):
                piece_index[l, kind, p] = len(piece_index)

    def stage(src, dst):
        for i in range(2):
            dst[i, seq // STEP * STEP:, :] = jnp.zeros((block - seq // STEP * STEP, d), BF16)
            dst[i, 0:seq, :] = src[:, i, :]

    at_row = 0
    for ref in (g1_in, b1_in, bo_in, g2_in, b2_in, bd_in, bqv_in, bup_in):
        values = ref[...].astype(F32)
        for j in range(ref.shape[1] // WIDE):
            for l in range(layers):
                pack_ref[l * SMALL + at_row:l * SMALL + at_row + 1, :] = values[l:l + 1, j * WIDE:(j + 1) * WIDE]
            at_row += 1
    for l in range(layers):
        pack_ref[l * SMALL + at_row:(l + 1) * SMALL, :] = jnp.zeros((SMALL - at_row, WIDE), F32)
    greet((at.sib, at.xn, at.xd, at.yn, at.zn))

    here = vec.at[:, span(at.grp * WIDE, WIDE)]
    packs = [
        pltpu.make_async_copy(pack_ref, here, s_misc.at[4]),
        remote(pack_ref, here, s_misc.at[5], r_misc.at[5], at.sib),
        remote(pack_ref, here, s_misc.at[6], r_misc.at[6], at.xn),
        remote(pack_ref, here, s_misc.at[7], r_misc.at[7], at.xd),
    ]
    for copy in packs:
        copy.start()

    def quarter_rows(kind):
        return full[kind].shape[2] // PIECES[kind] // 4

    def part_of(kind, p, first, count=4, of=1):
        q = quarter_rows(kind) // of
        return span(4 * of * p * q + first * q, q) if count == 1 else pl.ds(4 * p * q, count * q)

    def wider_parts(kind, p, y, zlow):
        return part_of(kind, p, y, 1), part_of(kind, p, 2 + zlow, 1)

    def launch(l, kind, p):
        w, i = index[l, kind], piece_index[l, kind, p]
        src, dst = ins[kind].at[l], full[kind].at[l]
        part = part_of(kind, p, quarter, 1)
        if kind in runs:
            width, count = runs[kind]
            mine = 2 * x + c
            for j in range(count):
                to = pl.ds(j * width, width)
                keep = span((2 * j + c) * width, width)
                give = span((2 * j + 1 - c) * width, width)
                remote(src.at[part, keep], dst.at[mine, part, to], s_send.at[w], s_rx.at[i], at.xn).start()
                remote(src.at[part, give], dst.at[mine, part, to], s_send.at[w], s_rx.at[i], at.xd).start()
                if p == 0:
                    remote(src.at[:, give], dst.at[mine, :, to], s_send.at[w], s_rs.at[w], at.sib).start()
                    pltpu.make_async_copy(src.at[:, keep], dst.at[mine, :, to], s_loc.at[w]).start()
        else:
            for part in wider_parts(kind, p, at.y, at.zlow) if (l, kind, p) in WIDER else (part,):
                remote(src.at[part], dst.at[x, part], s_send.at[w], s_rx.at[i], at.xn).start()
            if p == 0:
                pltpu.make_async_copy(src, dst.at[x], s_loc.at[w]).start()

    def theirs(l, kind, part):
        dst = full[kind].at[l]
        if kind in runs:
            return dst.at[span(2 * (1 - x), 2), part]
        return dst.at[pl.ds(1 - x, 1), part]

    link = dict(x=4.0, y=0.0, z=0.0)

    def travel(name, us):
        link[name] = max(plan.now, link[name]) + us
        return link[name] + 2.5

    def hop(kind):
        shape = full[kind].shape
        return 2 * shape[1] * shape[2] * shape[3] / 2**20 / PIECES[kind] / 4 / 0.094 * 1.05

    def relay1(l, kind, p):
        key = (l, kind, p)
        w, i = index[l, kind], piece_index[key]
        if key in WIDER:
            settle(theirs(l, kind, part_of(kind, p, 0, 2)), s_rx.at[i])
            to_y, to_z = (theirs(l, kind, part) for part in wider_parts(kind, p, at.y, at.zlow))
        else:
            to_y = to_z = theirs(l, kind, part_of(kind, p, quarter, 1))
            settle(to_y, s_rx.at[i])
        remote(to_y, to_y, s_send.at[w], s_ry.at[i], at.yn).start()
        remote(to_z, to_z, s_send.at[w], s_rz.at[i], at.zn).start()
        t = max(travel("y", hop(kind)), travel("z", hop(kind)))
        if key in WIDER:
            plan.add(t, ("ok", *key), functools.partial(arrived, *key))
        else:
            plan.add(t, ("r2", *key), functools.partial(relay2, *key))
        plan.order()

    def relay2(l, kind, p):
        key = (l, kind, p)
        w, i = index[l, kind], piece_index[key]
        from_y, from_z = 2 * (1 - at.y) + at.zlow, 2 * at.y + 1 - at.zlow
        settle(theirs(l, kind, part_of(kind, p, from_y, 1)), s_ry.at[i])
        piece = theirs(l, kind, part_of(kind, p, 2 * from_y, 1, 2))
        remote(piece, piece, s_send.at[w], s_ra.at[i], at.zn).start()
        settle(theirs(l, kind, part_of(kind, p, from_z, 1)), s_rz.at[i])
        piece = theirs(l, kind, part_of(kind, p, 2 * from_z + 1, 1, 2))
        remote(piece, piece, s_send.at[w], s_rb.at[i], at.yn).start()
        t = max(travel("y", hop(kind) / 2), travel("z", hop(kind) / 2))
        plan.add(t, ("ok", *key), functools.partial(arrived, *key))
        plan.order()

    def arrived(l, kind, p):
        key = (l, kind, p)
        i = piece_index[key]
        if key in WIDER:
            by_y, by_z = (theirs(l, kind, part) for part in wider_parts(kind, p, 1 - at.y, 1 - at.zlow))
            settle(by_y, s_ry.at[i])
            settle(by_z, s_rz.at[i])
        else:
            far = 2 * (1 - at.y) + 1 - at.zlow
            settle(theirs(l, kind, part_of(kind, p, 2 * far, 1, 2)), s_ra.at[i])
            settle(theirs(l, kind, part_of(kind, p, 2 * far + 1, 1, 2)), s_rb.at[i])

    def have(l, kind):
        for p in range(PIECES[kind]):
            plan.need(("ok", l, kind, p))
        w = index[l, kind]
        if kind in runs:
            settle(full[kind].at[l, 0], s_rs.at[w])
        settle(full[kind].at[l, 0], s_loc.at[w])
        pltpu.make_async_copy(full[kind].at[l], saves[kind].at[l], s_loc.at[w]).start()

    tokens = [
        remote(tok_ref.at[1 - x], tok.at[1], s_misc.at[0], r_misc.at[0], at.xn),
        pltpu.make_async_copy(tok_ref.at[x], tok.at[0], s_misc.at[3]),
    ]
    for key in piece_index:
        if key[:2] == (0, "up") and key[2] == 0:
            stage(tok_in, tok_ref)
            for copy in tokens:
                copy.start()
            token_time = travel("x", 7.3)
        launch(*key)
        t = travel("x", hop(key[1]) * (2 if key in WIDER else 1))
        plan.add(t, ("r1", *key), functools.partial(relay1, *key))
    x_time = travel("x", 7.3)
    late = [
        remote(cot_ref.at[1 - x], cot.at[1], s_misc.at[1], r_misc.at[1], at.xn),
        pltpu.make_async_copy(cot_ref.at[x], cot.at[0], s_misc.at[8]),
    ]
    stage(cot_in, cot_ref)
    for copy in late:
        copy.start()
    mask = chip_flags(at, tv_ref, rows, seq)
    saved = []

    def seed():
        for copy in late:
            copy.wait()
        valid = jnp.where(x == 0, iv_ref[0:1, 0:1], iv_ref[0:1, 1:2]).astype(F32)
        weight = mask[:rows].astype(F32) * valid
        for i in range(2):
            for j in range(block // STEP):
                r = i * block + j * STEP
                dm[pl.ds(r, STEP), :] = (
                    cot[i, pl.ds(j * STEP, STEP), :].astype(F32) * weight[r:r + STEP, :]
                ).astype(BF16)
        copy = remote(dm.at[own], dm.at[other], s_misc.at[2], r_misc.at[2], at.sib)
        copy.start()
        saved.append(copy)

    def seeded():
        saved[0].wait()
        copy = pltpu.make_async_copy(dm, dm_out, s_misc.at[10])
        copy.start()
        saved.append(copy)

    plan.add(x_time, "seed", seed)
    plan.add(x_time + 5, "seeded", seeded)
    plan.order()

    for copy in packs:
        copy.wait()
    vec_save = pltpu.make_async_copy(vec, vec_out, s_misc.at[9])
    vec_save.start()
    for l in range(layers):
        for j in range(f // WIDE):
            half, sub = divmod(j, f // WIDE // 2)
            bup[l:l + 1, pl.ds(j * WIDE, WIDE)] = vec[
                l * SMALL + BUP + sub:l * SMALL + BUP + sub + 1, span((2 * half + c) * WIDE, WIDE)
            ]
    plan.now = token_time
    plan.poll()
    for copy in tokens:
        copy.wait()
    for i in range(2):
        for j in range(block // STEP):
            x_ref[pl.ds(i * block + j * STEP, STEP), :] = tok[i, pl.ds(j * STEP, STEP), :].astype(F32)
    plan.spend(1)

    def save(src, dst, slot):
        copy = pltpu.make_async_copy(src, dst, s_save.at[slot])
        copy.start()
        return copy

    pending = {}
    for l in range(layers):
        def row(name, l=l):
            return vec[l * SMALL + name:l * SMALL + name + 1, :]

        def norm_out(src_ref, dst_ref, gain, shift, l=l):
            for i in range(rows // STEP):
                r = pl.ds(i * STEP, STEP)
                hat, _ = norm_rows(src_ref[r, :])
                dst_ref[r, :] = (hat * row(gain) + row(shift)).astype(BF16)

        def weight(kind, cs, l=l):
            w = full[kind][l, :, :, cs]
            return w.reshape(w.shape[0] * w.shape[1], w.shape[2])

        norm_out(x_ref, h1, G1, B1)
        cp = remote(h1.at[own], h1.at[other], s_core.at[0], r_core.at[0], at.sib)
        cp.start()
        x_saved = save(x_ref, xs.at[l], 0)
        plan.spend(2)
        have(l, "qkv")
        if l:
            pending["qkv"].wait()
        bq = jnp.where(c == 0, row(BQV), vec[l * SMALL + BQV + 1:l * SMALL + BQV + 2, :])
        scale = HEAD ** -0.5
        parts = (
            (0, bq[:, :hc] * scale, scale), (hc, jnp.zeros((1, hc), F32), 1.0), (2 * hc, bq[:, hc:], 1.0)
        )

        def qkv_rows(r, l=l, parts=parts):
            for base, bias, factor in parts:
                for j in range(hc // WIDE):
                    cs = pl.ds(base + j * WIDE, WIDE)
                    out = nn(h1[r, :], weight("qkv", cs))
                    qkv[r, cs] = (out * factor + bias[:, j * WIDE:(j + 1) * WIDE]).astype(BF16)
                    plan.spend(0.35)

        qkv_rows(own)
        cp.wait()
        qkv_rows(other)
        h1_saved = save(h1, h1s.at[l], 1)
        pending["qkv"] = save(qkv, qkvs.at[l], 2)
        if l:
            pending["att"].wait()
        for p in range(hc // 128):
            q2 = qkv[:, p * 128:(p + 1) * 128]
            k2 = qkv[:, hc + p * 128:hc + (p + 1) * 128]
            v2 = qkv[:, 2 * hc + p * 128:2 * hc + (p + 1) * 128]
            vt = v2.T
            outs = []
            for a in range(2):
                pt = scores_t(k2, half_lanes(q2, a), mask)
                outs.append(nn(vt[a * HEAD:(a + 1) * HEAD, :], pt.astype(BF16)))
                plan.spend(1.4)
            att[:, p * 128:(p + 1) * 128] = jnp.concatenate(outs, axis=0).T.astype(BF16)
        pending["att"] = save(att, as_.at[l], 3)

        def exchange(left, kind, base, bias, out, slot):
            def far(j):
                put[:, cols(j)] = nn(left[other, :], weight(kind, cols(j))).astype(BF16)

            loop(d // WIDE, far)
            cp = remote(put, got.at[slot], s_core.at[1], r_core.at[1], at.sib)
            cp.start()
            plan.spend(1)

            def near(j):
                out[:, cols(j)] = nn(left[own, :], weight(kind, cols(j))) + base[:, cols(j)] + vec[
                    l * SMALL + bias:l * SMALL + bias + 1, cols(j)
                ]

            loop(d // WIDE, near)
            plan.spend(1)
            cp.wait()
            out[...] += got[slot].astype(F32)
            plan.spend(1)

        have(l, "out")
        if l:
            pending["x2"].wait()
        exchange(att, "out", x_ref, BOUT, x2_ref, 0)
        pending["x2"] = save(x2_ref, x2s.at[l], 4)
        norm_out(x2_ref, h2, G2, B2)
        cp = remote(h2.at[own], h2.at[other], s_core.at[2], r_core.at[2], at.sib)
        cp.start()
        plan.spend(2)
        have(l, "up")
        if l:
            pending["z"].wait()
            pending["gp"].wait()

        def up_rows(r):
            def body(j):
                u = nn(h2[r, :], weight("up", cols(j))) + bup[l:l + 1, cols(j)]
                phi = 0.5 + 0.5 * lax.erf(u * 0.7071067811865476)
                z[r, cols(j)] = (u * phi).astype(BF16)
                gp[r, cols(j)] = (phi + u * jnp.exp(u * u * -0.5) * 0.3989422804014327).astype(BF16)

            for part in range(2):
                loop(f // WIDE // 2, lambda j: body(j + part * (f // WIDE // 2)))
                plan.spend(1.9)

        up_rows(own)
        cp.wait()
        up_rows(other)
        h2_saved = save(h2, h2s.at[l], 5)
        pending["z"] = save(z, zs.at[l], 6)
        pending["gp"] = save(gp, gps.at[l], 7)
        have(l, "down")
        for copy in (x_saved, h1_saved, h2_saved):
            copy.wait()
        exchange(z, "down", x2_ref, BDOWN, x_ref, 1)

    for i in range(2):
        for j in range(block // STEP):
            tok[i, pl.ds(j * STEP, STEP), :] = x_ref[pl.ds(i * block + j * STEP, STEP), :].astype(BF16)
    act = pltpu.make_async_copy(tok, act_out, s_misc.at[11])
    act.start()
    while plan.events:
        plan.fire()
    for copy in (act, vec_save, saved[1]):
        copy.wait()
    for name in ("qkv", "att", "x2", "z", "gp"):
        pending[name].wait()
    for (l, kind), i in index.items():
        settle(full[kind].at[l, pl.ds(0, 3 if kind in runs else 1)], s_send.at[i])
        settle(full[kind].at[l], s_loc.at[i])


ANY = pl.BlockSpec(memory_space=pl.ANY)
VM = pl.BlockSpec(memory_space=pltpu.VMEM)


def dma(*shape):
    return pltpu.SemaphoreType.DMA(shape)


def run_fwd(tok, cot, smalls, tv, iv, w_qkv, w_out, w_up, w_down, seq):
    layers, n, d3 = w_qkv.shape
    d = d3 // 3
    hc, f = d // 2, 2 * w_down.shape[1]
    block = -(-seq // 32) * 32
    rows, both = 2 * block, 4 * block
    weights = [(4, n, 3 * hc), (2, n, d), (4, n, f), (2, w_down.shape[1], d)]
    acts = [
        ((rows, d), F32), ((rows, d), F32), ((both, d), BF16), ((both, 3 * hc), BF16),
        ((both, hc), BF16), ((both, d), BF16), ((both, f), BF16), ((both, f), BF16),
    ]
    shapes = [((layers, *s), BF16) for s in weights] + [((layers, *s), t) for s, t in acts]
    shapes += [((both, d), BF16), ((2, block, d), BF16), ((layers * SMALL, d), F32)]
    count, pieces = layers * len(KINDS), layers * sum(PIECES.values())
    return pl.pallas_call(
        functools.partial(fwd_kernel, seq),
        out_shape=[jax.ShapeDtypeStruct(s, t) for s, t in shapes],
        in_specs=[VM] * 12 + [ANY] * 4,
        out_specs=[ANY] * len(shapes),
        scratch_shapes=[pltpu.VMEM((layers, *s), BF16) for s in weights]
        + [pltpu.VMEM(s, t) for s, t in acts]
        + [
            pltpu.VMEM((rows, d), BF16), pltpu.VMEM((2, rows, d), BF16),
            pltpu.VMEM((2, block, d), BF16), pltpu.VMEM((layers * SMALL, d), F32), pltpu.VMEM((8, f), F32),
            pltpu.VMEM((2, block, d), BF16), pltpu.VMEM((both, d), BF16), pltpu.VMEM((layers * SMALL, WIDE), F32),
            pltpu.VMEM((2, block, d), BF16), pltpu.VMEM((2, block, d), BF16),
        ]
        + [dma(pieces)] * 5
        + [dma(count)] * 3
        + [dma(3), dma(3), dma(8), dma(12), dma(8)],
        compiler_params=pltpu.CompilerParams(
            collective_id=1, has_side_effects=True, vmem_limit_bytes=VMEM_LIMIT
        ),
        cost_estimate=pl.CostEstimate(flops=17 * 10**9, bytes_accessed=80 * 10**6, transcendentals=0),
        name="forward",
    )(tok, cot, *smalls, tv, iv, w_qkv, w_out, w_up, w_down)


LINK, HOP, STAGE = 11.5, 2.5, 0.6
NS, NY, NZ, NT = 6, 3, 3, 6
CHUNK = 256
CROSS = (("down", 1), ("down", 3), ("up", 1))


def chunks_of(layers):
    chunks = []
    for l in reversed(range(layers)):
        chunks += [("down", l, i) for i in range(4)] + [("up", l, i) for i in range(4)]
        chunks += [("out", l, 0)] + [("qkv", l, i) for i in range(3)]
    return chunks + [("small", 0, 0)]


def crossed(chunk):
    return (chunk[0], chunk[2]) in CROSS


def units_of(chunks):
    units, first, last = [], {}, {}
    for k, (kind, l, i) in enumerate(chunks):
        if crossed(chunks[k]):
            continue
        pieces = {("qkv", 0, 1): (128, 128), ("qkv", 0, 2): (128, 64, 64), ("small", 0, 0): (64,)}
        start = 0
        first[k] = len(units)
        for n in pieces.get((kind, l, i), (CHUNK,)):
            units.append((k, start, n))
            start += n
        last[k] = len(units) - 1
    return units, first, last


class Ring:
    def __init__(self, at, plan, chunks, outs, bufs, sems):
        self.at, self.plan, self.chunks, self.outs = at, plan, chunks, outs
        self.g, self.xr, self.yr, self.zr, self.wr, self.t, self.zd, self.xd, self.yd, self.cd, self.td = bufs
        (self.x_send, self.x_recv, self.y_send, self.y_recv, self.z_send, self.z_recv, self.w_send, self.w_recv,
         self.f_send, self.f_recv) = sems[:10]
        self.d_send, self.d_recv, self.d_out, self.cx, self.cy, self.cz, self.cw, self.cb = sems[10:]
        self.units, self.first, self.last = units_of(chunks)
        self.turn = {k: a for a, k in enumerate(self.first)}
        self.cross = [k for k, chunk in enumerate(chunks) if crossed(chunk)]
        self.count = len(self.units)
        self.link = dict(x=0.0, y=0.0, out=0.0, mid=0.0, back=0.0)
        self.copies, self.done, self.ready = {}, set(), {}

    def size(self, u):
        return self.units[u][2]

    def send(self, links, rows):
        t = max(self.plan.now, *(self.link[name] for name in links)) + LINK * rows / CHUNK
        for name in links:
            self.link[name] = t
        return t + HOP

    def pick(self, limit):
        best = None
        for (stage, u), t in self.ready.items():
            if t > limit or (best and best[0] <= t):
                continue
            ahead = [(stage, u - 1)]
            ahead += {1: [(2, u - NY)], 2: [(3, u - NZ), (6, u - NT)], 3: [(4, u - NZ)], 4: [(5, u - NZ)]}.get(stage, [])
            if all(v < 0 or (other, v) in self.done for other, v in ahead):
                best = (t, stage, u)
        return best

    def step(self, best):
        t, stage, u = best
        del self.ready[stage, u]
        self.plan.now = max(self.plan.now, t) + STAGE
        if stage > 10:
            (self.d2, self.d3, self.d4, self.d5, self.d6, self.d7)[stage - 12](u)
            links, rows = {
                12: (("x",), 128), 13: (("y",), 64), 14: (("mid", "out", "back"), 96), 15: (("y",), 64),
                16: (("out", "back"), 128),
            }.get(stage, (None, 0))
        else:
            (self.s1, self.s2, self.s3, self.s4, self.s5, self.s6)[stage - 1](u)
            links = {1: ("y",), 2: ("out",), 3: ("mid",), 4: ("back",), 5: ("y",)}.get(stage)
            rows = self.size(u) // 2
        self.done.add((stage, u))
        if links:
            self.ready[stage + 1, u] = self.send(links, rows)

    def poll(self):
        while best := self.pick(self.plan.now):
            self.step(best)

    def catch_up(self, stage, u):
        while (stage, u) not in self.done:
            self.step(self.pick(float("inf")))

    def reserve(self, k):
        if k >= NS:
            old = k - NS
            if old in self.turn:
                self.catch_up(2, self.last[old])
            else:
                self.catch_up(14, self.cross.index(old))
        if self.turn.get(k, 0) >= NS:
            self.catch_up(1, self.last[list(self.turn)[self.turn[k] - NS]])

    def launch(self, k):
        if k not in self.turn:
            d = self.cross.index(k)
            self.move(d, 0, self.g.at[k % NS, :, self.rows_of(1 - self.at.inn)], self.zd.at[d], self.at.zn)
            self.ready[12, d] = self.send(("out", "back"), CHUNK)
            return
        a = self.turn[k]
        if a >= NS:
            pl.semaphore_wait(self.cx, 1)
        for u in range(self.first[k], self.last[k] + 1):
            _, start, n = self.units[u]
            copy = remote(
                self.g.at[k % NS, 0, pl.ds(start, n)], self.xr.at[a % NS, pl.ds(start, n)],
                self.x_send.at[u], self.x_recv.at[u], self.at.xn,
            )
            copy.start()
            self.copies["x", u] = copy
            self.ready[1, u] = self.send(("x",), n)

    def rows_of(self, part):
        return span(part * (CHUNK // 2), CHUNK // 2)

    def move(self, d, hop, src, dst, peer):
        copy = remote(src, dst, self.d_send.at[hop, d], self.d_recv.at[hop, d], peer)
        copy.start()
        self.copies[hop, d] = copy

    def d2(self, d):
        slot, mine = self.cross[d] % NS, self.rows_of(self.at.inn)
        self.copies[0, d].wait()
        for hh in range(2):
            self.add(self.g.at[slot, hh, mine], self.zd.at[d, hh], CHUNK // 2)
        self.move(d, 1, self.g.at[slot, 0, mine], self.xd.at[d], self.at.xn)

    def d3(self, d):
        slot, mine, quarter = self.cross[d] % NS, self.rows_of(self.at.inn), CHUNK // 4
        self.copies[1, d].wait()
        self.add(self.g.at[slot, 1, mine], self.xd.at[d], CHUNK // 2)
        give = span((2 * self.at.inn + 1 - self.at.y) * quarter, quarter)
        self.move(d, 2, self.g.at[slot, 1, give], self.yd.at[d], self.at.yn)

    def d4(self, d):
        slot, quarter = self.cross[d] % NS, CHUNK // 4
        t = self.td.at[d, span(self.at.y * quarter, quarter)]
        self.copies[2, d].wait()
        self.add(t, self.yd.at[d], quarter, self.g.at[slot, 1], (2 * self.at.inn + self.at.y) * quarter)
        self.move(d, 3, t, self.cd.at[d], self.at.mid)

    def d5(self, d):
        quarter = CHUNK // 4
        t = self.td.at[d, span(self.at.y * quarter, quarter)]
        self.copies[3, d].wait()
        self.add(t, self.cd.at[d], quarter)
        self.move(d, 4, t, t, self.at.yn)

    def d6(self, d):
        at = self.at
        kind, l, i = self.chunks[self.cross[d]]
        out = self.outs[kind]
        self.copies[4, d].wait()
        if kind == "down":
            dst = out.at[l, span((2 * i + at.inn) * (CHUNK // 2), CHUNK // 2)]
        else:
            width = self.td.shape[2]
            dst = out.at[l, self.rows_of(at.inn), span((2 * (i % 2) + at.c) * width, width)]
        sent = self.d_out.at[d]
        pltpu.make_async_copy(self.td.at[d], dst, sent).start()
        remote(self.td.at[d], dst, sent, self.f_recv.at[KINDS.index(kind)], at.zn).start()

    def d7(self, d):
        settle(self.zd.at[d], self.d_out.at[d])

    def credit(self, sem, u, slots, peer):
        if u + slots < self.count:
            pl.semaphore_signal(sem, inc=1, device_id=peer, device_id_type=MESH)

    def claim(self, sem, u, slots):
        if u >= slots:
            pl.semaphore_wait(sem, 1)

    def add(self, dst, src, count, base=None, base_at=None):
        def body(j):
            r = cols(j, 32)
            b = dst[r, :] if base is None else base[pl.ds(pl.multiple_of(base_at + j * 32, 32), 32), :]
            dst[r, :] = (b.astype(F32) + src[r, :].astype(F32)).astype(BF16)

        loop(count // 32, body)

    def s1(self, u):
        at = self.at
        k, start, n = self.units[u]
        slot, a = k % NS, self.turn[k]
        self.copies["x", u].wait()
        self.add(self.g.at[slot, 1, pl.ds(start, n)], self.xr.at[a % NS, pl.ds(start, n)], n)
        if u == self.last[k] and a + NS < len(self.turn):
            pl.semaphore_signal(self.cx, inc=1, device_id=at.xn, device_id_type=MESH)
        self.claim(self.cy, u, NY)
        copy = remote(
            self.g.at[slot, 1, span(start + (1 - at.y) * (n // 2), n // 2)], self.yr.at[u % NY, pl.ds(0, n // 2)],
            self.y_send.at[u], self.y_recv.at[u % NY], at.yn,
        )
        copy.start()
        self.copies["y", u] = copy

    def part(self, ref, u, slots):
        return ref.at[u % slots, pl.ds(0, self.size(u) // 2)]

    def s2(self, u):
        at = self.at
        k, start, n = self.units[u]
        t = self.part(self.t, u, NT)
        self.copies["y", u].wait()
        self.add(t, self.part(self.yr, u, NY), n // 2, self.g.at[k % NS, 1], start + at.y * (n // 2))
        self.credit(self.cy, u, NY, at.yn)

        @pl.when(at.outer)
        def _():
            self.claim(self.cz, u, NZ)
            remote(t, self.part(self.zr, u, NZ), self.z_send.at[u % NT], self.z_recv.at[u % NZ], at.zn).start()

    def s3(self, u):
        n, at = self.size(u), self.at
        t = self.part(self.t, u, NT)

        @pl.when(at.outer)
        def _():
            settle(t, self.z_send.at[u % NT])

        @pl.when(at.inner)
        def _():
            got = self.part(self.zr, u, NZ)
            settle(got, self.z_recv.at[u % NZ])
            self.add(t, got, n // 2)
            self.credit(self.cz, u, NZ, at.zn)
            self.claim(self.cw, u, NZ)
            remote(t, self.part(self.wr, u, NZ), self.z_send.at[u % NT], self.w_recv.at[u % NZ], at.mid).start()

    def s4(self, u):
        n, at = self.size(u), self.at

        @pl.when(at.inner)
        def _():
            t = self.part(self.t, u, NT)
            got = self.part(self.wr, u, NZ)
            settle(got, self.w_recv.at[u % NZ])
            settle(t, self.z_send.at[u % NT])
            self.add(t, got, n // 2)
            self.credit(self.cw, u, NZ, at.mid)
            self.claim(self.cb, u, NZ)
            remote(t, self.part(self.zr, u, NZ), self.w_send.at[u % NT], self.z_recv.at[u % NZ], at.zn).start()

    def s5(self, u):
        n, at = self.size(u), self.at
        t = self.part(self.t, u, NT)

        @pl.when(at.outer)
        def _():
            got = self.part(self.zr, u, NZ)
            settle(got, self.z_recv.at[u % NZ])

            def body(j):
                t[cols(j, 32), :] = got[cols(j, 32), :]

            loop(n // 64, body)
            self.credit(self.cb, u, NZ, at.zn)

        k, start, n = self.units[u]
        kind, l, i = self.chunks[k]
        out = self.outs[kind]
        sent = self.f_send.at[u % NT]
        if kind == "small":
            pltpu.make_async_copy(t, out, sent).start()
            return
        half = n // 2
        width = t.shape[1]

        def deliver(src, dst, mine, kind_index):
            if mine:
                pltpu.make_async_copy(src, dst, sent).start()
                remote(src, dst, sent, self.f_recv.at[kind_index], at.yn).start()
            else:
                remote(src, dst, sent, self.f_recv.at[kind_index], at.sib).start()
                remote(src, dst, sent, self.f_recv.at[kind_index], at.yd).start()

        if kind in ("down", "out"):
            deliver(t, out.at[l, span(i * CHUNK + start + at.y * half, half)], True, KINDS.index(kind))
        elif kind == "up":
            side, run = divmod(i, 2)
            deliver(t, out.at[l, span(start + at.y * half, half), span((2 * run + at.c) * width, width)], side == 0, 2)
        else:
            for side in range(2):
                for run in range(2):
                    src = t.at[:, pl.ds((2 * side + run) * WIDE, WIDE)]
                    dst = out.at[l, span(start + at.y * half, half), span(i * width + (2 * run + at.c) * WIDE, WIDE)]
                    deliver(src, dst, side == 0, 0)

    def s6(self, u):
        at = self.at
        t = self.part(self.t, u, NT)
        k, _, n = self.units[u]
        settle(t if self.chunks[k][0] == "small" else self.g.at[0, 0, pl.ds(0, n)], self.f_send.at[u % NT])

        @pl.when(at.inner)
        def _():
            settle(t, self.w_send.at[u % NT])

    def finish(self):
        while best := self.pick(float("inf")):
            self.step(best)
        for i, kind in enumerate(KINDS):
            out = self.outs[kind]
            rows = out.shape[1]
            settle(out.at[:, pl.ds(0, rows // 2 if kind in ("out", "down") else rows * 3 // 4)], self.f_recv.at[i])


def bwd_kernel(
    seq, dm_ref, act_ref, vec_ref, tv_ref, vqkv, vout, vup, vdown, xs, x2s, h1s, qkvs, as_, h2s, zs, gps,
    oqkv, oout, oup, odown, osmall, otok, oact,
    wqkv, wout, wup, wdown, x_ref, x2_ref, h1, qkv, att, h2, z, gp,
    g_ref, dm, da, dj, dx2, dh, put, got, small, small_put, small_got, s_load, s_core, r_core, s_misc, r_misc, *rest,
):
    at = Place()
    layers = vqkv.shape[0]
    rows, d = x_ref.shape
    block = rows // 2
    hc, f = att.shape[1], z.shape[1]
    own, other = pl.ds(0, rows), pl.ds(rows, rows)
    x, c = at.x, at.c
    plan = Plan()
    chunks = chunks_of(layers)
    rings, ring_sems = rest[:11], rest[11:]
    ring_g = rings[0]
    ring = Ring(
        at, plan, chunks, dict(qkv=oqkv, out=oout, up=oup, down=odown, small=osmall),
        rings, ring_sems,
    )
    plan.poll = ring.poll
    number = {chunk: u for u, chunk in enumerate(chunks)}

    stores = dict(
        z=(zs, z), wdown=(vdown, wdown), gp=(gps, gp), h2=(h2s, h2), wup=(vup, wup), x2=(x2s, x2_ref),
        wout=(vout, wout), att=(as_, att), qkv=(qkvs, qkv), wqkv=(vqkv, wqkv), h1=(h1s, h1), x=(xs, x_ref),
    )
    slots = {name: i for i, name in enumerate(stores)}
    loads = {}

    def load(name, l):
        if l < 0:
            return
        src, dst = stores[name]
        loads[name, l] = pltpu.make_async_copy(src.at[l], dst, s_load.at[slots[name]])
        loads[name, l].start()

    dm_load = pltpu.make_async_copy(dm_ref, dm.at[0], s_misc.at[0])
    dm_load.start()
    for name in stores:
        load(name, layers - 1)
    greet((at.sib, at.xn, at.yn, at.yd, at.zn, at.mid))

    def by_half(hh):
        return hh * x + (1 - hh) * (1 - x)

    mask = chip_flags(at, tv_ref, rows, seq)
    small[...] = jnp.zeros_like(small)
    act = [
        remote(act_ref.at[1], oact.at[x], s_misc.at[4], r_misc.at[4], at.xn),
        pltpu.make_async_copy(act_ref.at[0], oact.at[x], s_misc.at[5]),
    ]
    for l in reversed(range(layers)):
        def row(name, l=l):
            return vec_ref[l * SMALL + name:l * SMALL + name + 1, :]

        def set_small(name, value, l=l):
            small[l * SMALL + name:l * SMALL + name + 1, :] = value

        def round_rows(src_ref, name, slot):
            total = jnp.zeros((8, d), F32)
            for i in range(rows // STEP):
                r = pl.ds(i * STEP, STEP)
                if src_ref is None:
                    low = dm[slot, r, :].astype(F32)
                    g_ref[r, :] = low
                else:
                    low = src_ref[r, :].astype(BF16)
                    dm[slot, r, :] = low
                    low = low.astype(F32)
                total = total + low[0:8, :] + low[8:16, :]
            set_small(name, jnp.sum(total, axis=0, keepdims=True))

        def send_round(src_ref, name, slot):
            round_rows(src_ref, name, slot)
            copy = remote(dm.at[slot, own], dm.at[slot, other], s_core.at[slot], r_core.at[slot], at.sib)
            copy.start()
            return copy

        def exchange(left, w):
            per = w.shape[1]

            def piece(j):
                b = j // (per // WIDE)
                return w[b, span((j % (per // WIDE)) * WIDE, WIDE), :]

            def far(j):
                put[:, cols(j)] = nt(left[other, :], piece(j)).astype(BF16)

            loop(d // WIDE, far)
            plan.spend(1.5)
            copy = remote(put, got, s_core.at[2], r_core.at[2], at.sib)
            copy.start()

            def near(j):
                dh[:, cols(j)] = nt(left[own, :], piece(j))

            loop(d // WIDE, near)
            plan.spend(1.5)
            copy.wait()
            plan.spend(0.5)

        def norm_back(value_ref, base_ref, out_ref, gain, shift):
            total_g = jnp.zeros((8, d), F32)
            total_b = jnp.zeros((8, d), F32)
            for i in range(rows // STEP):
                r = pl.ds(i * STEP, STEP)
                hat, rstd = norm_rows(value_ref[r, :])
                grad = dh[r, :] + got[r, :].astype(F32)
                prod = grad * hat
                total_g = total_g + prod[0:8, :] + prod[8:16, :]
                total_b = total_b + grad[0:8, :] + grad[8:16, :]
                dhat = grad * row(gain)
                m1 = jnp.mean(dhat, axis=-1, keepdims=True)
                m2 = jnp.mean(dhat * hat, axis=-1, keepdims=True)
                out_ref[r, :] = base_ref[r, :] + rstd * (dhat - m1 - hat * m2)
            set_small(gain, jnp.sum(total_g, axis=0, keepdims=True))
            set_small(shift, jnp.sum(total_b, axis=0, keepdims=True))

        def produce(chunk, maker, us):
            u = number[chunk]
            ring.reserve(u)
            loop(2, lambda hh: maker(ring_g.at[u % NS, hh], by_half(hh)))
            ring.launch(u)
            plan.spend(us)

        if l == layers - 1:
            dm_load.wait()
            loads["z", l].wait()
        else:
            copy = send_round(g_ref, BDOWN, 0)
            loads["z", l].wait()
            plan.spend(2)
            copy.wait()
        for i in range(4):
            def make(dst, h, i=i):
                dst[...] = tn(z[:, span(h * (f // 2) + i * CHUNK, CHUNK)], dm[0]).astype(BF16)

            produce(("down", l, i), make, 1.3)
        if l == layers - 1:
            round_rows(None, BDOWN, 0)
            for copy in act:
                copy.start()
        load("z", l - 1)
        loads["wdown", l].wait()
        loads["gp", l].wait()

        def dz_body(j):
            b = j // (f // 2 // WIDE)
            w = wdown[b, span((j % (f // 2 // WIDE)) * WIDE, WIDE), :]
            for r in (own, other):
                low = (nt(dm[0, r, :], w) * gp[r, cols(j)].astype(F32)).astype(BF16)
                gp[r, cols(j)] = low

        for part in range(2):
            loop(f // WIDE // 2, lambda j: dz_body(j + part * (f // WIDE // 2)))
            plan.spend(2)
        load("wdown", l - 1)
        for j in range(f // WIDE):
            half, sub = divmod(j, f // WIDE // 2)
            small[l * SMALL + BUP + sub:l * SMALL + BUP + sub + 1, span((2 * half + c) * WIDE, WIDE)] = jnp.sum(
                gp[:, j * WIDE:(j + 1) * WIDE].astype(F32), axis=0, keepdims=True
            )
        loads["h2", l].wait()
        loads["wup", l].wait()
        for i in range(4):
            side, run = divmod(i, 2)

            def make(dst, h, side=side, run=run):
                rh = c if side == 0 else 1 - c
                left = h2[:, span(h * (d // 2) + rh * CHUNK, CHUNK)]
                dst[...] = tn(left, gp[:, run * (f // 2):(run + 1) * (f // 2)]).astype(BF16)

            if i == 2:
                exchange(gp, wup)
                load("wup", l - 1)
                loads["x2", l].wait()
                norm_back(x2_ref, g_ref, dx2, G2, B2)
                load("x2", l - 1)
                plan.spend(3)
                copy = send_round(dx2, BOUT, 1)
            produce(("up", l, i), make, 1.3)
        load("gp", l - 1)
        load("h2", l - 1)

        loads["wout", l].wait()
        loads["att", l].wait()
        copy.wait()
        for j in range(hc // WIDE):
            for r in (own, other):
                da[r, pl.ds(j * WIDE, WIDE)] = nt(dm[1, r, :], wout[j]).astype(BF16)
        load("wout", l - 1)

        def make(dst, h):
            dst[...] = tn(att[:, span(h * CHUNK, CHUNK)], dm[1]).astype(BF16)

        produce(("out", l, 0), make, 2)
        load("att", l - 1)
        loads["qkv", l].wait()
        sums = {}
        for p in range(hc // 128):
            cq, ck, cv = (pl.ds(k * hc + p * 128, 128) for k in range(3))
            q2, k2, v2, da2 = qkv[:, cq], qkv[:, ck], qkv[:, cv], da[:, cq]
            kt = k2.T
            dk = dv = None
            parts = []
            for a in range(2):
                qa, daa = half_lanes(q2, a), half_lanes(da2, a)
                pt = scores_t(k2, qa, mask)
                dpt = nt(v2, daa)
                delta = jnp.sum(dpt * pt, axis=0, keepdims=True)
                dst = (pt * (dpt - delta)).astype(BF16)
                dva = nn(pt.astype(BF16), daa)
                dka = nn(dst, qa)
                parts.append(nn(kt[a * HEAD:(a + 1) * HEAD, :], dst))
                dk = dka if dk is None else dk + dka
                dv = dva if dv is None else dv + dva
                plan.spend(2.7)
            dq = (jnp.concatenate(parts, axis=0).T * HEAD ** -0.5).astype(BF16)
            dv = dv.astype(BF16)
            dj[:, cq] = dq
            dj[:, ck] = dk.astype(BF16)
            dj[:, cv] = dv
            for k, value in ((0, dq), (1, dv)):
                total = jnp.sum(value.astype(F32), axis=0, keepdims=True)
                for core in range(2):
                    r = l * SMALL + BQV + core
                    small[r:r + 1, k * hc + p * 128:k * hc + (p + 1) * 128] = jnp.where(
                        c == core, total, jnp.zeros_like(total)
                    )
        load("qkv", l - 1)
        loads["wqkv", l].wait()
        loads["h1", l].wait()
        for i in range(3):
            def make(dst, h, i=i):
                for side in range(2):
                    rh = c if side == 0 else 1 - c
                    left = h1[:, span(h * (d // 2) + rh * CHUNK, CHUNK)]
                    dst[:, side * hc:(side + 1) * hc] = tn(left, dj[:, i * hc:(i + 1) * hc]).astype(BF16)

            if i == 1:
                exchange(dj, wqkv)
                load("wqkv", l - 1)
                loads["x", l].wait()
                norm_back(x_ref, dx2, g_ref, G1, B1)
                load("x", l - 1)
                plan.spend(3)
            produce(("qkv", l, i), make, 1.3)
        load("h1", l - 1)

    for j in range(rows // STEP):
        put[pl.ds(j * STEP, STEP), :] = g_ref[pl.ds(j * STEP, STEP), :].astype(BF16)
    back = [
        remote(put.at[pl.ds(block, block)], otok.at[x], s_misc.at[1], r_misc.at[1], at.xn),
        pltpu.make_async_copy(put.at[pl.ds(0, block)], otok.at[x], s_misc.at[2]),
    ]
    small_put[...] = small[...].astype(BF16)
    copy = remote(small_put, small_got, s_misc.at[3], r_misc.at[3], at.sib)
    copy.start()
    copy.wait()
    total = (small_put[...].astype(F32) + small_got[...].astype(F32)).astype(BF16)
    u = number["small", 0, 0]
    ring.reserve(u)
    n = total.shape[0]
    for hh in range(2):
        for k in range(2):
            ring_g[u % NS, hh, k * n:(k + 1) * n, :] = total
    ring.launch(u)
    for copy in back:
        copy.start()
    ring.finish()
    for copy in (*back, *act):
        copy.wait()


def run_bwd(dm, act, vec, tv, weights, acts, seq):
    layers, _, n, hc3 = weights[0].shape
    d = acts[0].shape[2]
    rows = acts[0].shape[1]
    block, both = rows // 2, 2 * rows
    hc, f = hc3 // 3, weights[2].shape[3]
    chunks = chunks_of(layers)
    units = len(units_of(chunks)[0])
    crosses = sum(crossed(chunk) for chunk in chunks)
    outs = [(layers, n, 3 * d), (layers, n, d), (layers, n, 2 * f), (layers, f // 2, d), (layers * SMALL, d)]
    outs += [(2, block, d)] * 2
    args = (dm, act, vec, tv, *weights, *acts)
    return pl.pallas_call(
        functools.partial(bwd_kernel, seq),
        out_shape=[jax.ShapeDtypeStruct(s, BF16) for s in outs],
        in_specs=[ANY, ANY, VM, VM] + [ANY] * 12,
        out_specs=[ANY] * len(outs),
        scratch_shapes=[pltpu.VMEM(w.shape[1:], w.dtype) for w in (*weights, *acts)]
        + [
            pltpu.VMEM((rows, d), F32), pltpu.VMEM((2, both, d), BF16),
            pltpu.VMEM((both, hc), BF16), pltpu.VMEM((both, 3 * hc), BF16), pltpu.VMEM((rows, d), F32),
            pltpu.VMEM((rows, d), F32), pltpu.VMEM((rows, d), BF16), pltpu.VMEM((rows, d), BF16),
            pltpu.VMEM((layers * SMALL, d), F32), pltpu.VMEM((layers * SMALL, d), BF16),
            pltpu.VMEM((layers * SMALL, d), BF16),
            dma(12), dma(3), dma(3), dma(6), dma(6),
            pltpu.VMEM((NS, 2, CHUNK, d), BF16), pltpu.VMEM((NS, CHUNK, d), BF16),
            pltpu.VMEM((NY, CHUNK // 2, d), BF16), pltpu.VMEM((NZ, CHUNK // 2, d), BF16),
            pltpu.VMEM((NZ, CHUNK // 2, d), BF16), pltpu.VMEM((NT, CHUNK // 2, d), BF16),
            pltpu.VMEM((crosses, 2, CHUNK // 2, d), BF16), pltpu.VMEM((crosses, CHUNK // 2, d), BF16),
            pltpu.VMEM((crosses, CHUNK // 4, d), BF16), pltpu.VMEM((crosses, CHUNK // 4, d), BF16),
            pltpu.VMEM((crosses, CHUNK // 2, d), BF16),
            dma(units), dma(units), dma(units), dma(NY), dma(NT), dma(NZ), dma(NT), dma(NZ), dma(NT), dma(4),
            dma(5, crosses), dma(5, crosses), dma(crosses),
        ]
        + [pltpu.SemaphoreType.REGULAR] * 5,
        compiler_params=pltpu.CompilerParams(
            collective_id=2, has_side_effects=True, vmem_limit_bytes=VMEM_LIMIT
        ),
        cost_estimate=pl.CostEstimate(flops=34 * 10**9, bytes_accessed=120 * 10**6, transcendentals=0),
        name="backward",
    )(*args)


def finish_kernel(gqkv, gout, gup, gdown, small, act, gtok, oact, ogtok, oqkv, oout, oup, odown, *vectors):
    seq = oact.shape[0]

    @pl.when(jnp.logical_and(pl.program_id(0) == 0, pl.program_id(1) == 0))
    def _():
        for src, dst in ((act, oact), (gtok, ogtok)):
            dst[...] = jnp.stack([src[0, :seq, :], src[1, :seq, :]], axis=1)

    for src, dst in ((gqkv, oqkv), (gout, oout), (gup, oup), (gdown, odown)):
        dst[...] = src[...].astype(F32)
    mine = span(lax.axis_index("grp") * WIDE, WIDE)
    layers = vectors[0].shape[0]
    rows = [small[l * SMALL:(l + 1) * SMALL, mine].astype(F32) for l in range(layers)]
    at = 0
    for out in vectors:
        for j in range(out.shape[1] // WIDE):
            for l in range(layers):
                out[l:l + 1, j * WIDE:(j + 1) * WIDE] = rows[l][at:at + 1, :]
            at += 1


def run_finish(gqkv, gout, gup, gdown, small, act, gtok, seq, widths):
    bigs = (gqkv, gout, gup, gdown)
    layers = gqkv.shape[0]
    steps = 2

    def big(g):
        return pl.BlockSpec((1, g.shape[1] // steps, g.shape[2]), lambda l, s: (l, s, 0))

    def flat(shape):
        return pl.BlockSpec(shape, lambda l, s: (0,) * len(shape))

    rows = [(seq, act.shape[0], act.shape[2])] * 2
    vectors = [(layers, w) for w in widths]
    return pl.pallas_call(
        finish_kernel,
        grid=(layers, steps),
        out_shape=[jax.ShapeDtypeStruct(r, BF16) for r in rows]
        + [jax.ShapeDtypeStruct(g.shape, F32) for g in bigs]
        + [jax.ShapeDtypeStruct(v, F32) for v in vectors],
        in_specs=[big(g) for g in bigs] + [flat(small.shape), flat(act.shape), flat(gtok.shape)],
        out_specs=[flat(r) for r in rows] + [big(g) for g in bigs] + [flat(v) for v in vectors],
        compiler_params=pltpu.CompilerParams(vmem_limit_bytes=VMEM_LIMIT),
        name="finish",
    )(*bigs, small, act, gtok)


def local(
    tokens, cotangent, image_valid, token_valid,
    norm1_gain, norm1_bias, w_qkv, b_qv, w_out, b_out, norm2_gain, norm2_bias, w_up, b_up, w_down, b_down,
):
    seq = tokens.shape[1]
    smalls = (norm1_gain, norm1_bias, b_out, norm2_gain, norm2_bias, b_down, b_qv, b_up)
    res = run_fwd(
        tokens.transpose(1, 0, 2), cotangent.transpose(1, 0, 2), smalls, token_valid, image_valid[None, :], w_qkv, w_out, w_up, w_down, seq
    )
    weights, acts, (dm, act, vec) = res[:4], res[4:12], res[12:]
    gqkv, gout, gup, gdown, gsmall, gtok, act = run_bwd(dm, act, vec, token_valid, weights, acts, seq)
    blocks = lax.axis_size("rep") // 8
    if blocks > 1:
        groups = [[i + 8 * b for b in range(blocks)] for i in range(8)]
        gqkv, gout, gup, gdown, gsmall = (
            lax.psum(g, "rep", axis_index_groups=groups) for g in (gqkv, gout, gup, gdown, gsmall)
        )
    act, gtok, gqkv, gout, gup, gdown, *vectors = run_finish(
        gqkv, gout, gup, gdown, gsmall, act, gtok, seq, [w.shape[1] for w in smalls]
    )
    act, gtok = act.transpose(1, 0, 2), gtok.transpose(1, 0, 2)
    gg1, gb1, gbout, gg2, gb2, gbdown, gbqv, gbup = vectors
    return (
        act, gtok, gg1, gb1, gqkv, gbqv, gout, gbout, gg2, gb2, gup, gbup, gdown, gbdown,
    )


def solution(mesh):
    rows3, mat, vec = P("rep", "grp", None), P(None, "grp", None), P(None, "grp")
    weights = (vec, vec, mat, vec, mat, vec, vec, vec, mat, vec, mat, vec)
    return jax.shard_map(
        local,
        mesh=mesh,
        in_specs=(rows3, rows3, P("rep"), P("rep", None)) + weights,
        out_specs=(rows3, rows3) + weights,
        check_vma=False,
    )
```
